128 devices in a mesh: shard: 4 (over z), context: 8 (over x, core), tensor: 4 (over y).
Axes of the slice: x: 4, y: 4, z: 4, core: 2. Of those that a mesh axis runs over, the one named last changes fastest.
Arguments:
- tokens_in: bfloat16 [8192, 2048], P(('shard', 'context')), may hold values from -6 to 6
- cotangent: bfloat16 [8192, 2048], P(('shard', 'context')), may hold values from -6 to 6
- segments: int32 [4, 2048], P('shard'), may hold values from 0 to 4, as said below
- positions: int32 [8192], P(('shard', 'context')), may hold values from 0 to 2047, as said below
- norm1_gain: bfloat16 [2048], P(('shard', 'context')), may hold values from 0.099609375 to 1.8984375
- q_weight: bfloat16 [2048, 2048], P(('shard', 'context'), 'tensor'), may hold values from -0.125 to 0.125
- k_weight: bfloat16 [2048, 2048], P(('shard', 'context'), 'tensor'), may hold values from -0.125 to 0.125
- v_weight: bfloat16 [2048, 2048], P(('shard', 'context'), 'tensor'), may hold values from -0.125 to 0.125
- o_weight: bfloat16 [2048, 2048], P('tensor', ('shard', 'context')), may hold values from -4 to 4
- norm2_gain: bfloat16 [2048], P(('shard', 'context')), may hold values from 0.099609375 to 1.8984375
- gate_weight: bfloat16 [2048, 8192], P(('shard', 'context'), 'tensor'), may hold values from -0.125 to 0.125
- up_weight: bfloat16 [2048, 8192], P(('shard', 'context'), 'tensor'), may hold values from -0.125 to 0.125
- down_weight: bfloat16 [8192, 2048], P('tensor', ('shard', 'context')), may hold values from -0.0625 to 0.0625
Outputs:
- layer_out: bfloat16 [8192, 2048], P(('shard', 'context'))
- input_grad: bfloat16 [8192, 2048], P(('shard', 'context'))
- grad_norm1: float32 [2048], P(('shard', 'context'))
- grad_q: float32 [2048, 2048], P(('shard', 'context'), 'tensor')
- grad_k: float32 [2048, 2048], P(('shard', 'context'), 'tensor')
- grad_v: float32 [2048, 2048], P(('shard', 'context'), 'tensor')
- grad_o: float32 [2048, 2048], P('tensor', ('shard', 'context'))
- grad_norm2: float32 [2048], P(('shard', 'context'))
- grad_gate: float32 [2048, 8192], P(('shard', 'context'), 'tensor')
- grad_up: float32 [2048, 8192], P(('shard', 'context'), 'tensor')
- grad_down: float32 [8192, 2048], P('tensor', ('shard', 'context'))
The draws below stay inside these ranges and needn't reach their ends.
Inputs may be any that keep to these rules, and one draw needn't show every extreme that they name: `segments`: within a sequence the document numbers never fall and rise by one at each boundary; every sequence holds documents 0 to 4. Within one document the positions rise by one from token to token.
All inputs are finite; a program needn't handle non-finite values.
Results may differ from the reference program's by a relative error of at most 0.03.
Values may be sent and summed in bfloat16 or wider, within the bound.
A program may use at most 192 MiB of HBM per device.

```python
import math
import jax
import jax.numpy as jnp
from jax import lax

D = 2048
HEADS = 32
HEAD_DIM = 64
FF = 8192
SEQ = 2048
ROWS = 256
SEQS = 4
TOKENS = 8192
QW = 2048


def document_layout(key):
    first_key, second_key, third_key, fourth_key = jax.random.split(key, 4)
    least_doc = ROWS * 25 // 32
    long_start = jax.random.randint(first_key, (SEQS, 1), least_doc + 1, ROWS)
    front_cut = jax.random.randint(second_key, (SEQS, 1), 1, ROWS) % (long_start - least_doc) + 1
    long_end = jax.random.randint(third_key, (SEQS, 1), SEQ - ROWS + 1, SEQ - least_doc)
    back_cut = long_end + least_doc + jax.random.randint(fourth_key, (SEQS, 1), 0, ROWS) % (SEQ - long_end - least_doc)
    token_index = jnp.arange(SEQ, dtype=jnp.int32)[None, :]
    segment = (token_index >= front_cut).astype(jnp.int32) + (token_index >= long_start).astype(jnp.int32) + (token_index >= long_end).astype(jnp.int32) + (token_index >= back_cut).astype(jnp.int32)
    doc_start = jnp.where(segment == 1, front_cut, jnp.where(segment == 2, long_start, jnp.where(segment == 3, long_end, back_cut)))
    place = jnp.where(segment == 0, token_index + SEQ - front_cut, token_index - doc_start)
    return (segment.astype(jnp.int32), place.astype(jnp.int32))


def draw_segments(key, part):
    segment, place = document_layout(key)
    return segment


def draw_positions(key, part):
    segment, place = document_layout(key)
    return place.reshape(SEQS * SEQ)


def shard_levels(stream_key, extent, cuts, smallest, top_value):
    def one(dim, blocks):
        draws = jax.random.uniform(jax.random.fold_in(jax.random.fold_in(stream_key, 6), dim), (blocks,), jnp.float32, smallest / len(cuts), top_value / len(cuts))
        return jnp.repeat(jnp.exp(draws), extent[dim] // blocks).reshape((-1,) + (1,) * (len(extent) - dim - 1))

    loudness = one(*cuts[0])
    for cut in cuts[1:]:
        loudness = loudness * one(*cut)
    return loudness


def bell_draw(key, shape, spread, bound, cuts=(), kind=jnp.bfloat16):
    drawn = jax.random.normal(key, shape, jnp.float32) * spread
    if len(cuts) > 0:
        drawn = shard_levels(key, shape, cuts, -0.22, 0.18) * drawn
    return jnp.clip(drawn, min=-bound, max=bound).astype(kind)


def setup_inputs(seed: int = 0) -> dict:
    splits = jax.random.split(jax.random.key(seed), 14)
    tokens_in = bell_draw(splits[0], (TOKENS, D), 1.0, 6.0, ((0, 32),))
    cotangent = bell_draw(splits[1], (TOKENS, D), 1.0, 6.0, ((0, 32),))
    segments = draw_segments(jax.random.fold_in(splits[13], 71), 0)
    positions = draw_positions(jax.random.fold_in(splits[13], 71), 0)
    norm1_gain = jnp.clip(1.0 + 0.18 * jax.random.normal(splits[4], (D,), jnp.float32), 0.099609375, 1.8984375).astype(jnp.bfloat16)
    q_weight = bell_draw(splits[5], (D, QW), D ** -0.5, 0.125, ((0, 32), (1, 4)))
    k_weight = bell_draw(splits[6], (D, QW), D ** -0.5, 0.125, ((0, 32), (1, 4)))
    v_weight = bell_draw(splits[7], (D, QW), D ** -0.5, 0.125, ((0, 32), (1, 4)))
    o_weight = bell_draw(splits[8], (QW, D), (max(1, 2 * QW // SEQ)) ** -0.5, 4.0, ((0, 4), (1, 32)))
    norm2_gain = jnp.clip(1.0 + 0.18 * jax.random.normal(splits[9], (D,), jnp.float32), 0.099609375, 1.8984375).astype(jnp.bfloat16)
    gate_weight = bell_draw(splits[10], (D, FF), D ** -0.5, 0.125, ((0, 32), (1, 4)))
    up_weight = bell_draw(splits[11], (D, FF), D ** -0.5, 0.125, ((0, 32), (1, 4)))
    down_weight = bell_draw(splits[12], (FF, D), FF ** -0.5, 0.0625, ((0, 4), (1, 32)))
    return dict(tokens_in=tokens_in, cotangent=cotangent, segments=segments, positions=positions, norm1_gain=norm1_gain, q_weight=q_weight, k_weight=k_weight, v_weight=v_weight, o_weight=o_weight, norm2_gain=norm2_gain, gate_weight=gate_weight, up_weight=up_weight, down_weight=down_weight)


@jax.custom_vjp
def low(v):
    return lax.optimization_barrier(v.astype(jnp.bfloat16)).astype(jnp.float32)

@jax.custom_vjp
def low_back(v):
    return v

def low_keep(v):
    return (low(v), None)

def low_pass(kept, grad):
    return (grad,)

def back_keep(v):
    return (v, None)

def back_low(kept, grad):
    return (low(grad),)
low.defvjp(low_keep, low_pass)
low_back.defvjp(back_keep, back_low)
highest = lax.Precision.HIGHEST
epsilon = 1e-05
rope_base = 130000.0
masked_low = -1000000000.0

def matmul(left, right):
    return jnp.dot(left, right, precision=highest, preferred_element_type=jnp.float32)

def angle_tables(positions):
    half = HEAD_DIM // 2
    frequency = rope_base ** (-(jnp.arange(half, dtype=jnp.float32) * 2.0) / HEAD_DIM)
    angle = positions.astype(jnp.float32)[:, None] * frequency[None, :]
    return (jnp.cos(angle)[:, None, :], jnp.sin(angle)[:, None, :])

def rotate(vectors, cosine, sine):
    half = HEAD_DIM // 2
    first = vectors[..., :half]
    second = vectors[..., half:]
    return jnp.concatenate([first * cosine - second * sine, second * cosine + first * sine], axis=-1)

def attention(queries, keys, values, seq_segs):
    length = queries.shape[0]
    block = math.gcd(length, 512)
    count = length // block
    token_index = jnp.arange(length, dtype=jnp.int32)

    def block_attend(pieces):
        q_block, q_seg, q_index = pieces
        allowed = ((q_seg[:, None] == seq_segs[None, :]) & (token_index[None, :] <= q_index[:, None]))[None]
        raw_scores = low_back(jnp.einsum('qhd,khd->hqk', q_block, keys, precision=highest))
        scores = jnp.where(allowed, raw_scores * HEAD_DIM ** (-0.5), masked_low)
        peak = lax.optimization_barrier(jnp.max(scores, axis=-1, keepdims=True))
        weights = jnp.where(allowed, jnp.exp(scores - peak), 0.0)
        total = lax.optimization_barrier(jnp.sum(weights, axis=-1))
        summed = low_back(jnp.einsum('hqk,khd->qhd', low(weights), values, precision=highest))
        return summed / jnp.transpose(total)[:, :, None]
    pieces = (queries.reshape(count, block, HEADS, HEAD_DIM), seq_segs.reshape(count, block), token_index.reshape(count, block))
    result = lax.map(jax.checkpoint(block_attend), pieces)
    return result.reshape(length, HEADS, HEAD_DIM)

def layer(inputs, gain_one, q_full, k_full, v_full, o_full, gain_two, gate_full, up_full, down_full, seq_segs, seq_pos):
    length = inputs.shape[0]
    scale_one = lax.rsqrt(lax.optimization_barrier(jnp.mean(inputs * inputs, axis=-1, keepdims=True)) + epsilon)
    normed_one = low(inputs * scale_one * gain_one)
    q_lin = low_back(matmul(normed_one, q_full)).reshape(length, HEADS, HEAD_DIM)
    k_lin = low_back(matmul(normed_one, k_full)).reshape(length, HEADS, HEAD_DIM)
    v_lin = low_back(matmul(normed_one, v_full)).reshape(length, HEADS, HEAD_DIM)
    cosine, sine = angle_tables(seq_pos)
    queries = low(rotate(q_lin, cosine, sine))
    keys = low(rotate(k_lin, cosine, sine))
    values = low(v_lin)
    attended = attention(queries, keys, values, seq_segs)
    branch = low_back(matmul(low(attended.reshape(length, QW)), o_full))
    middle = inputs + branch
    scale_two = lax.rsqrt(lax.optimization_barrier(jnp.mean(middle * middle, axis=-1, keepdims=True)) + epsilon)
    normed_two = low(middle * scale_two * gain_two)
    gate = low_back(matmul(normed_two, gate_full))
    upper = low_back(matmul(normed_two, up_full))
    hidden = low(jax.nn.silu(gate) * upper)
    mixed = low_back(matmul(hidden, down_full))
    return middle + mixed

def reference(tokens_in, cotangent, segments, positions, norm1_gain, q_weight, k_weight, v_weight, o_weight, norm2_gain, gate_weight, up_weight, down_weight):
    params = tuple((w.astype(jnp.float32) for w in (norm1_gain, q_weight, k_weight, v_weight, o_weight, norm2_gain, gate_weight, up_weight, down_weight)))
    inputs_all = tokens_in.astype(jnp.float32).reshape(SEQS, SEQ, D)
    cotangent_all = cotangent.astype(jnp.float32).reshape(SEQS, SEQ, D)
    positions_all = positions.reshape(SEQS, SEQ)

    def sequence_step(carried, element):
        inputs, seq_cot, seq_segs, seq_pos = element

        def forward(inputs, *weights):
            return layer(inputs, *weights, seq_segs, seq_pos)
        result, puller = jax.vjp(forward, inputs, *params)
        grads = puller(seq_cot)
        carried = tuple((c + g for c, g in zip(carried, grads[1:])))
        return (carried, (result, grads[0]))
    zeros = tuple((jnp.zeros_like(w) for w in params))
    totals, (results, input_grads) = lax.scan(sequence_step, zeros, (inputs_all, cotangent_all, segments, positions_all))
    return (results.reshape(TOKENS, D).astype(jnp.bfloat16), input_grads.reshape(TOKENS, D).astype(jnp.bfloat16), totals[0], totals[1], totals[2], totals[3], totals[4], totals[5], totals[6], totals[7], totals[8])
```

```python
import jax
import jax.numpy as jnp
from jax import lax
from jax.experimental import pallas as pl
from jax.experimental.pallas import tpu as pltpu
from jax.sharding import Mesh
from jax.sharding import PartitionSpec as P

HEAD_DIM = 64
BLOCK = 512

epsilon = 1e-05
rope_base = 130000.0
masked_low = -1000000000.0

f32 = jnp.float32
bf16 = jnp.bfloat16
MESH = pl.DeviceIdType.MESH
VMEM = pl.BlockSpec(memory_space=pltpu.VMEM)
HBM = pl.BlockSpec(memory_space=pl.ANY)


def dot_nn(a, b):
    return lax.dot_general(a, b, (((1,), (0,)), ((), ())), preferred_element_type=f32)


def dot_nt(a, b):
    return lax.dot_general(a, b, (((1,), (1,)), ((), ())), preferred_element_type=f32)


def dot_tn(a, b):
    return lax.dot_general(a, b, (((0,), (0,)), ((), ())), preferred_element_type=f32)


def place():
    return tuple(lax.axis_index(a) for a in ("shard", "x", "core", "tensor"))


def turned(index, step):
    return lax.rem(index + step, 4)


def on_axis(axis, index):
    return {axis: index}


def meet(axes):
    barrier = pltpu.get_barrier_semaphore()
    count = 0
    for axis in axes:
        me = lax.axis_index(axis)
        peers = [1 - me] if axis == "core" else [turned(me, d) for d in (1, 2, 3)]
        for peer in peers:
            pl.semaphore_signal(barrier, inc=1, device_id={axis: peer}, device_id_type=MESH)
            count += 1
    pl.semaphore_wait(barrier, count)


def remote(src, dst, send, recv, axis, index):
    return pltpu.make_async_remote_copy(
        src_ref=src, dst_ref=dst, send_sem=send, recv_sem=recv, device_id={axis: index}, device_id_type=MESH
    )


def gather_kernel(
    wq, wk, wv, wo, gains, tokens, cot, table,
    full, gain_all, chip_tokens, chip_cot, chip_table, normed, gain_rows,
    local, core_send, core_recv, send, recv, gain_send, gain_recv,
):
    z, x, core, y = place()
    half = wq.shape[1] // 2
    rows = wq.shape[0]
    meet(("core", "x", "shard"))
    at = pl.ds(pl.multiple_of(core * rows, rows), rows)
    keep = pl.ds(pl.multiple_of(core * half, half), half)
    give = pl.ds(pl.multiple_of((1 - core) * half, half), half)
    inside, across = [], []
    pairs = [(gains, gains, gain_all.at[z, x, core])]
    for k, w in enumerate((wq, wk, wv, wo)):
        pairs.append((w.at[:, keep], w.at[:, give], full.at[z, x, at, pl.ds(k * half, half)]))
    pairs += [(a, a, b.at[core]) for a, b in ((tokens, chip_tokens), (table, chip_table), (cot, chip_cot))]
    for k, (mine, theirs, there) in enumerate(pairs):
        inside.append(pltpu.make_async_copy(mine, there, local.at[k]))
        across.append(remote(theirs, there, core_send.at[k], core_recv.at[k], "core", 1 - core))
        across[-1].start()
        inside[-1].start()

    def arrived(ks):
        for k in ks:
            inside[k].wait()
            across[k].wait_recv()

    first, second = pl.ds(0, 2 * half), pl.ds(2 * half, 2 * half)
    started = []

    def spread(src, dst, s, r, axis, me, k):
        for d in (1, 2, 3):
            copy = remote(src, dst, s.at[k, d - 1], r.at[k, d - 1], axis, turned(me, d))
            copy.start()
            started.append(copy)

    arrived((0,))
    spread(gain_all.at[z, x], gain_all.at[z, x], gain_send, gain_recv, "x", x, 0)
    arrived((1, 2))
    spread(full.at[z, x, :, first], full.at[z, x, :, first], send, recv, "x", x, 0)
    arrived((3, 4))
    spread(full.at[z, x, :, second], full.at[z, x, :, second], send, recv, "shard", z, 1)
    for copy in started[0:3]:
        copy.wait_recv()
    spread(gain_all.at[z], gain_all.at[z], gain_send, gain_recv, "shard", z, 1)
    for copy in started[3:6]:
        copy.wait_recv()
    spread(full.at[z, :, :, first], full.at[z, :, :, first], send, recv, "shard", z, 2)
    for copy in started[6:9]:
        copy.wait_recv()
    spread(full.at[:, x, :, second], full.at[:, x, :, second], send, recv, "x", x, 3)
    for copy in started[9:12]:
        copy.wait_recv()
    for i in range(16):
        two = (gain_all[i // 4, i % 4, 0] + gain_all[i // 4, i % 4, 1]).astype(f32)
        gain_rows[:, pl.ds(i * 128, 128)] = two[0:8, :]
    arrived((5, 6, 7))

    def norm(i, unused):
        values = chip_tokens[i // 4, pl.ds(pl.multiple_of(lax.rem(i, 4) * 64, 64), 64), :].astype(f32)
        scale = lax.rsqrt(jnp.mean(values * values, axis=-1, keepdims=True) + epsilon)
        normed[pl.ds(pl.multiple_of(i * 64, 64), 64), :] = ((values * scale) * gain_rows[0:1, :]).astype(bf16)
        return unused

    lax.fori_loop(0, 8, norm, 0)
    for copy in started[12:]:
        copy.wait_recv()
    for copy in across + started:
        copy.wait_send()


def gather_attention(wq, wk, wv, wo, gains, tokens, cot, table):
    rows, width = tokens.shape
    sds = jax.ShapeDtypeStruct
    dma = pltpu.SemaphoreType.DMA
    return pl.pallas_call(
        gather_kernel,
        out_shape=(
            sds((4, 4, 128, 2 * wq.shape[1]), bf16),
            sds((4, 4, 2, 16, 128), bf16),
            sds((2, rows, width), bf16),
            sds((2, rows, width), bf16),
            sds((2, rows, 128), f32),
            sds((2 * rows, width), bf16),
            sds((8, width), f32),
        ),
        in_specs=[HBM] * 4 + [VMEM] + [HBM] * 3,
        out_specs=(HBM, VMEM, VMEM, HBM, HBM, VMEM, VMEM),
        scratch_shapes=[dma((8,)), dma((8,)), dma((8,)), dma((4, 3)), dma((4, 3)), dma((2, 3)), dma((2, 3))],
        compiler_params=pltpu.CompilerParams(
            collective_id=0, has_side_effects=True, vmem_limit_bytes=40 << 20
        ),
    )(wq, wk, wv, wo, gains, tokens, cot, table)


def rope(vectors, table_cos, table_sin):
    n = vectors.shape[1]
    lane = lax.broadcasted_iota(jnp.int32, vectors.shape, 1)
    other = jnp.where(
        lax.rem(lane, HEAD_DIM) < HEAD_DIM // 2,
        pltpu.roll(vectors, n - HEAD_DIM // 2, 1),
        pltpu.roll(vectors, HEAD_DIM // 2, 1),
    )
    return vectors * table_cos + other * table_sin


def masked(raw, begin, j, i):
    key = lax.broadcasted_iota(jnp.int32, raw.shape, 0) + j * BLOCK
    query = lax.broadcasted_iota(jnp.int32, raw.shape, 1) + i * BLOCK
    return jnp.where((key >= begin) & (key <= query), raw * HEAD_DIM ** (-0.5), masked_low)


def sum_and_share(c, y, own, other, pair, near, out, mid_of, csem, ysem, asem, fsem):
    started = []
    for d in (2, 1, 3, 0):
        k = turned(y, d)
        copy = remote(other.at[k], pair.at[k], csem.at[0, d], csem.at[1, d], "core", 1 - c)
        copy.start()
        started.append(copy)
    arrive = dict(zip((2, 1, 3, 0), started))
    ysent = {}
    for d in (2, 1, 3):
        k = turned(y, d)
        arrive[d].wait_recv()
        arrive[d].wait_send()
        other[k] = (own[k] + pair[k].astype(f32)).astype(bf16)
        ysent[d] = remote(other.at[k], near.at[d - 1], ysem.at[0, d - 1], ysem.at[1, d - 1], "tensor", k)
        ysent[d].start()
    arrive[0].wait_recv()
    arrive[0].wait_send()
    total = own[y] + pair[y].astype(f32)
    for d in (1, 3, 2):
        ysent[d].wait_recv()
        total = total + near[d - 1].astype(f32)
    mid_of(total)
    share = {}
    for d in (2, 1, 3):
        share[d] = remote(out.at[c, y], out.at[c, y], asem.at[0, d - 1], asem.at[1, d - 1], "tensor", turned(y, d))
        share[d].start()
    forward = [remote(out.at[c, y], out.at[c, y], fsem.at[0, 0], fsem.at[1, 0], "core", 1 - c)]
    forward[0].start()
    for d in (1, 3, 2):
        share[d].wait_recv()
        k = turned(y, 4 - d)
        forward.append(remote(out.at[c, k], out.at[c, k], fsem.at[0, d], fsem.at[1, d], "core", 1 - c))
        forward[-1].start()
    for copy in forward:
        copy.wait_recv()
    for copy in [*ysent.values(), *share.values(), *forward]:
        copy.wait_send()


def forward_kernel(
    normed, weights, table, start, tokens, gain_rows,
    qkv_out, low, attended_out, lse, middle, normed_two,
    packed, arrived, value_t, head_out, low_in, own, other, pair, near,
    xsem, lsem, csem, ysem, asem, fsem,
):
    z, x, c, y = place()
    meet(("core", "x", "tensor"))
    chip = normed.shape[0]
    wide = 4 * HEAD_DIM
    cosine = jnp.concatenate([table[:, 0:64]] * 4, axis=1)
    sine = jnp.concatenate([table[:, 64:128]] * 4, axis=1)
    queries = rope(dot_nn(normed[...], weights[:, 0:wide]), cosine, sine).astype(bf16)
    keys = rope(dot_nn(normed[...], weights[:, wide : 2 * wide]), cosine, sine).astype(bf16)
    for h in range(4):
        lanes = slice(h * HEAD_DIM, (h + 1) * HEAD_DIM)
        packed[h, 0:chip, :] = jnp.concatenate([queries[:, lanes], keys[:, lanes]], axis=1)
    values = dot_nn(normed[...], weights[:, 2 * wide : 3 * wide]).astype(bf16)
    for h in range(4):
        lanes = slice(h * HEAD_DIM, (h + 1) * HEAD_DIM)
        packed[h, chip:, :] = jnp.concatenate(
            [values[0 : chip // 2, lanes], values[chip // 2 :, lanes]], axis=1
        )
    sent = []
    for d in (2, 1, 3):
        k = turned(x, d)
        sent.append(remote(packed.at[k], arrived.at[x], xsem.at[0, d - 1], xsem.at[1, d - 1], "x", k))
        sent[-1].start()
    arrived[x] = packed[x]
    for copy in sent:
        copy.wait_recv()
    for k in range(4):
        rows = slice(k * chip, (k + 1) * chip)
        qkv_out[0, rows, :] = arrived[k, 0:chip, 0:64]
        qkv_out[1, rows, :] = arrived[k, 0:chip, 64:128]
        block = jnp.concatenate([arrived[k, chip:, 0:64], arrived[k, chip:, 64:128]], axis=0)
        qkv_out[2, rows, :] = block
        value_t[:, rows] = jnp.transpose(block)
    low_sent = []
    for i in range(4):
        at = slice(i * BLOCK, (i + 1) * BLOCK)
        begin = start[:, at]
        mine = qkv_out[0, at, :]

        def step(j, state):
            peak, total, summed = state
            key_at = pl.ds(pl.multiple_of(j * BLOCK, BLOCK), BLOCK)
            scores = masked(dot_nt(qkv_out[1, key_at, :], mine), begin, j, i)
            new = jnp.maximum(peak, jnp.max(scores, axis=0, keepdims=True))
            weight = jnp.exp(scores - new)
            factor = jnp.exp(peak - new)
            total = total * factor + jnp.sum(weight, axis=0, keepdims=True)
            summed = summed * factor + dot_nn(value_t[:, key_at], weight.astype(bf16))
            return (new, total, summed)

        state = (
            jnp.full((1, BLOCK), masked_low, f32),
            jnp.zeros((1, BLOCK), f32),
            jnp.zeros((HEAD_DIM, BLOCK), f32),
        )
        state = step(i, state)
        peak, total, summed = lax.fori_loop(0, i, step, state) if i else state
        attended = jnp.transpose(summed / total)
        attended_out[at, :] = attended
        lse[:, at] = peak + jnp.log(total)
        head_out[i] = attended.astype(bf16)

        @pl.when(x != i)
        def send(i=i):
            remote(head_out.at[i], low_in.at[x], lsem.at[0, i], lsem.at[1, x], "x", i).start()

    low_in[x] = head_out[x]
    for d in (1, 2, 3):
        k = turned(x, d)
        copy = remote(head_out.at[k], low_in.at[k], lsem.at[0, k], lsem.at[1, k], "x", k)
        copy.wait_recv()
        copy.wait_send()
    low[...] = jnp.concatenate([low_in[h] for h in range(4)], axis=1)
    half = chip // 2
    quarter = half // 4
    out_weights = weights[:, 3 * wide : 4 * wide]
    theirs = low[pl.ds(pl.multiple_of((1 - c) * half, half), half), :]
    other[...] = dot_nt(theirs, out_weights).astype(bf16).reshape(other.shape)
    mine = low[pl.ds(pl.multiple_of(c * half, half), half), :]
    own[...] = dot_nt(mine, out_weights).reshape(own.shape)

    def finish(total):
        row = tokens[c, pl.ds(pl.multiple_of(y * quarter, quarter), quarter), :].astype(f32)
        mid = row + total
        middle[...] = mid
        scale = lax.rsqrt(jnp.mean(mid * mid, axis=-1, keepdims=True) + epsilon)
        normed_two[c, y] = ((mid * scale) * gain_rows[1:2, :]).astype(bf16)

    sum_and_share(c, y, own, other, pair, near, normed_two, finish, csem, ysem, asem, fsem)
    for copy in sent:
        copy.wait_send()


def attention_forward(normed, weights, table, start, tokens, gain_rows):
    chip, width = normed.shape
    seq = start.shape[1]
    sds = jax.ShapeDtypeStruct
    dma = pltpu.SemaphoreType.DMA
    quarter = chip // 8
    return pl.pallas_call(
        forward_kernel,
        out_shape=(
            sds((3, seq, HEAD_DIM), bf16),
            sds((chip, 4 * HEAD_DIM), bf16),
            sds((seq, HEAD_DIM), f32),
            sds((1, seq), f32),
            sds((quarter, width), f32),
            sds((2, 4, quarter, width), bf16),
        ),
        in_specs=[VMEM] * 6,
        out_specs=(VMEM,) * 6,
        scratch_shapes=[
            pltpu.VMEM((4, chip * 3 // 2, 128), bf16),
            pltpu.VMEM((4, chip * 3 // 2, 128), bf16),
            pltpu.VMEM((HEAD_DIM, seq), bf16),
            pltpu.VMEM((4, chip, HEAD_DIM), bf16),
            pltpu.VMEM((4, chip, HEAD_DIM), bf16),
            pltpu.VMEM((4, quarter, width), f32),
            pltpu.VMEM((4, quarter, width), bf16),
            pltpu.VMEM((4, quarter, width), bf16),
            pltpu.VMEM((3, quarter, width), bf16),
            dma((2, 3)), dma((2, 4)), dma((2, 4)), dma((2, 3)), dma((2, 3)), dma((2, 4)),
        ],
        compiler_params=pltpu.CompilerParams(
            collective_id=1, has_side_effects=True, vmem_limit_bytes=56 << 20
        ),
    )(normed, weights, table, start, tokens, gain_rows)


def mlp_kernel(
    normed, cot, gate_w, up_w, down_w, mixed, d_normed, grads, normed_t, cot_t, mixed_sum, d_sum
):
    step = pl.program_id(0)

    @pl.when(step == 0)
    def first():
        normed_t[...] = jnp.transpose(normed[...])
        cot_t[...] = jnp.transpose(cot[...])
        mixed_sum[...] = jnp.zeros_like(mixed_sum)
        d_sum[...] = jnp.zeros_like(d_sum)

    gate = dot_nn(normed[...], gate_w[...])
    upper = dot_nn(normed[...], up_w[...])
    d_hidden = dot_nn(cot[...], down_w[...])
    sigmoid = 1.0 / (1.0 + jnp.exp(-gate))
    silu = gate * sigmoid
    hidden = (silu * upper).astype(bf16)
    d_gate = (d_hidden * upper * (sigmoid * (1.0 + gate * (1.0 - sigmoid)))).astype(bf16)
    d_upper = (d_hidden * silu).astype(bf16)
    for k, (left, right) in enumerate(((normed_t, d_gate), (normed_t, d_upper), (cot_t, hidden))):
        grads[:, k] = dot_nn(left[...], right).astype(bf16).reshape(grads.shape[0], *grads.shape[2:])
    d_sum[...] += dot_nt(d_gate, gate_w[...]) + dot_nt(d_upper, up_w[...])
    mixed_sum[...] += dot_nt(hidden, down_w[...])

    @pl.when(step == pl.num_programs(0) - 1)
    def last():
        mixed[...] = mixed_sum[...].astype(bf16)
        d_normed[...] = d_sum[...].astype(bf16)


def mlp(normed, cot, full):
    chip, width = normed.shape
    ff = full.shape[1] // 3
    chunk = 256
    steps = ff // chunk
    sds = jax.ShapeDtypeStruct
    piece = [
        pl.BlockSpec((width, chunk), lambda f, k=k: (0, k * steps + f)) for k in range(3)
    ]
    return pl.pallas_call(
        mlp_kernel,
        grid=(steps,),
        out_shape=(
            sds((chip, width), bf16),
            sds((chip, width), bf16),
            sds((16, 3, width // 16, ff), bf16),
        ),
        in_specs=[VMEM, VMEM, *piece],
        out_specs=(VMEM, VMEM, pl.BlockSpec((16, 3, width // 16, chunk), lambda f: (0, 0, 0, f))),
        scratch_shapes=[
            pltpu.VMEM((width, chip), bf16),
            pltpu.VMEM((width, chip), bf16),
            pltpu.VMEM((chip, width), f32),
            pltpu.VMEM((chip, width), f32),
        ],
        compiler_params=pltpu.CompilerParams(vmem_limit_bytes=60 << 20),
        cost_estimate=pl.CostEstimate(flops=20 << 30, bytes_accessed=30 << 20, transcendentals=1 << 20),
    )(normed, cot, full, full, full)


def backward_kernel(
    d_part, mix_part, middle, own_tokens, own_cot, gain_rows, weights, low, normed, qkv, attended, lse, start, table,
    layer_out, input_grad, grads, gain_out,
    d_branch, d_mid, pair, half_sum, near, heads, head_in, key_t, d_key, d_value, packed, arrived, partial,
    turned_rows, terms, wide_in, wide_sum, thin_in, thin_sum, gain_part, gain_y, gain_c, gain_x, gain_z,
    csem, ysem, asem, fsem, hsem, psem, wsem, tsem, gsem, outsem,
):
    z, x, c, y = place()
    meet(("core", "x", "tensor", "shard"))
    chip, width = normed.shape
    half, quarter = chip // 2, chip // 8
    wide = 4 * HEAD_DIM
    waits = []

    def begin(copy):
        copy.start()
        waits.append(copy)
        return copy

    def cross(r, part):
        return {
            d: begin(remote(part.at[1 - c, turned(y, d)], pair.at[r, turned(y, d)], csem.at[r, 0, d], csem.at[r, 1, d], "core", 1 - c))
            for d in (2, 1, 3, 0)
        }

    def along(r, part, crossed):
        sent = {}
        for d in (2, 1, 3):
            k = turned(y, d)
            crossed[d].wait_recv()
            half_sum[r, k] = (part[c, k].astype(f32) + pair[r, k].astype(f32)).astype(bf16)
            sent[d] = begin(remote(half_sum.at[r, k], near.at[r, d - 1], ysem.at[r, 0, d - 1], ysem.at[r, 1, d - 1], "tensor", k))
        return sent

    def total_of(r, part, crossed, sent):
        crossed[0].wait_recv()
        total = part[c, y].astype(f32) + pair[r, y].astype(f32)
        for d in (1, 3, 2):
            sent[d].wait_recv()
            total = total + near[r, d - 1].astype(f32)
        return total

    def share(r, slot):
        return {
            d: begin(remote(slot, slot, asem.at[r, 0, d - 1], asem.at[r, 1, d - 1], "tensor", turned(y, d)))
            for d in (2, 1, 3)
        }

    d_crossed = cross(0, d_part)
    m_crossed = cross(1, mix_part)
    d_sent = along(0, d_part, d_crossed)
    mid = middle[...]
    scale = lax.rsqrt(jnp.mean(mid * mid, axis=-1, keepdims=True) + epsilon)
    unit = mid * scale
    d_two = total_of(0, d_part, d_crossed, d_sent)
    gain_two_part = jnp.sum(d_two * unit, axis=0, keepdims=True)
    scaled = d_two * gain_rows[1:2, :]
    d_middle = own_cot[...].astype(f32) + scale * (
        scaled - unit * jnp.mean(scaled * unit, axis=-1, keepdims=True)
    )
    d_mid[...] = d_middle
    d_branch[c, y] = d_middle.astype(bf16)
    shared = share(0, d_branch.at[c, y])
    forward = [begin(remote(d_branch.at[c, y], d_branch.at[c, y], fsem.at[0, 0], fsem.at[1, 0], "core", 1 - c))]
    m_sent = along(1, mix_part, m_crossed)
    for d in (1, 3, 2):
        shared[d].wait_recv()
        k = turned(y, 4 - d)
        forward.append(begin(remote(d_branch.at[c, k], d_branch.at[c, k], fsem.at[0, d], fsem.at[1, d], "core", 1 - c)))
    for copy in forward:
        copy.wait_recv()
    branch = d_branch[...].reshape(chip, width)
    d_heads = dot_nn(branch, weights[:, 3 * wide : 4 * wide]).astype(bf16)
    for h in range(4):
        heads[h] = d_heads[:, h * HEAD_DIM : (h + 1) * HEAD_DIM]
    head_sent = {}
    for d in (2, 1, 3):
        k = turned(x, d)
        head_sent[d] = begin(remote(heads.at[k], head_in.at[x], hsem.at[0, d - 1], hsem.at[1, d - 1], "x", k))
    head_in[x] = heads[x]
    layer_out[y] = (mid + total_of(1, mix_part, m_crossed, m_sent)).astype(bf16)
    out_shared = share(1, layer_out.at[y])
    turned_rows[...] = jnp.transpose(branch)
    terms[:, :, 3 * wide : 4 * wide] = (
        dot_nn(turned_rows[...], low[...]).astype(bf16).reshape(16, width // 16, wide)
    )
    for k in range(4):
        rows = slice(k * chip, (k + 1) * chip)
        key_t[:, rows] = jnp.transpose(qkv[1, rows, :])
    d_key[...] = jnp.zeros_like(d_key)
    d_value[...] = jnp.zeros_like(d_value)
    for d in (1, 3, 2):
        head_sent[d].wait_recv()

    for i in (3, 2, 1, 0):
        at = slice(i * BLOCK, (i + 1) * BLOCK)
        mine, d_out = qkv[0, at, :], head_in[i]
        product = d_out.astype(f32) * attended[at, :]
        center = jnp.sum(jnp.transpose(product), axis=0, keepdims=True)
        peak, first = lse[:, at], start[:, at]

        def step(j, d_query):
            key_at = pl.ds(pl.multiple_of(j * BLOCK, BLOCK), BLOCK)
            weight = jnp.exp(masked(dot_nt(qkv[1, key_at, :], mine), first, j, i) - peak)
            d_prob = dot_nt(qkv[2, key_at, :], d_out)
            d_raw = (weight * (d_prob - center) * HEAD_DIM ** (-0.5)).astype(bf16)
            d_key[key_at, :] += dot_nn(d_raw, mine)
            d_value[key_at, :] += dot_nn(weight.astype(bf16), d_out)
            return d_query + dot_nn(key_t[:, key_at], d_raw)

        d_query = lax.fori_loop(0, i + 1, step, jnp.zeros((HEAD_DIM, BLOCK), f32))
        packed[i, 0:chip, :] = jnp.concatenate(
            [jnp.transpose(d_query).astype(bf16), d_key[at, :].astype(bf16)], axis=1
        )
        d_rows = d_value[at, :].astype(bf16)
        packed[i, chip:, :] = jnp.concatenate([d_rows[0:half], d_rows[half:]], axis=1)

        @pl.when(x != i)
        def send(i=i):
            remote(packed.at[i], arrived.at[x], psem.at[0, i], psem.at[1, x], "x", i).start()

    arrived[x] = packed[x]
    turned_rows[...] = jnp.transpose(normed[...])
    for d in (1, 2, 3):
        k = turned(x, d)
        copy = remote(packed.at[k], arrived.at[k], psem.at[0, k], psem.at[1, k], "x", k)
        copy.wait_recv()
        waits.append(copy)
    cosine = jnp.concatenate([table[:, 0:64]] * 4, axis=1)
    sine = jnp.concatenate([table[:, 64:128]] * 4, axis=1)

    def side_by_side(lanes):
        return jnp.concatenate([arrived[h, 0:chip, lanes].astype(f32) for h in range(4)], axis=1)

    d_lin = jnp.concatenate(
        [
            rope(side_by_side(slice(0, 64)), cosine, -sine).astype(bf16),
            rope(side_by_side(slice(64, 128)), cosine, -sine).astype(bf16),
            jnp.concatenate(
                [
                    jnp.concatenate([arrived[h, chip:, lanes] for h in range(4)], axis=1)
                    for lanes in (slice(0, 64), slice(64, 128))
                ],
                axis=0,
            ),
        ],
        axis=1,
    )
    terms[:, :, 0 : 3 * wide] = dot_nn(turned_rows[...], d_lin).astype(bf16).reshape(16, width // 16, 3 * wide)

    first, second = pl.ds(0, 2 * wide), pl.ds(2 * wide, 2 * wide)
    wide_sent = {}
    for d in (2, 1, 3):
        kz, kx = turned(z, d), turned(x, d)
        wide_sent[0, d] = begin(remote(terms.at[pl.ds(pl.multiple_of(4 * kz, 4), 4), :, first], wide_in.at[0, d - 1], wsem.at[0, 0, d - 1], wsem.at[0, 1, d - 1], "shard", kz))
        for q in range(4):
            wide_sent[1, d, q] = begin(remote(terms.at[4 * q + kx, :, second], wide_in.at[1, d - 1, q], wsem.at[1 + q, 0, d - 1], wsem.at[1 + q, 1, d - 1], "x", kx))
    lin = [d_lin[0:half], d_lin[half:]]
    for k in range(2):
        partial[k] = dot_nt(lin[k], weights[:, 0 : 3 * wide]).astype(bf16).reshape(4, quarter, width)
    crossed = cross(2, partial)
    sent = along(2, partial, crossed)
    own = own_tokens[...].astype(f32)
    own_scale = lax.rsqrt(jnp.mean(own * own, axis=-1, keepdims=True) + epsilon)
    own_unit = own * own_scale
    d_one = total_of(2, partial, crossed, sent)
    scaled = d_one * gain_rows[0:1, :]
    input_grad[y] = (
        d_mid[...] + own_scale * (scaled - own_unit * jnp.mean(scaled * own_unit, axis=-1, keepdims=True))
    ).astype(bf16)
    in_shared = share(2, input_grad.at[y])
    both = jnp.concatenate(
        [jnp.sum(d_one * own_unit, axis=0, keepdims=True), gain_two_part, jnp.zeros((6, width), f32)], axis=0
    )
    for k in range(16):
        gain_part[k] = both[:, k * 128 : (k + 1) * 128]

    def pass_on(r, src_of, into, axis, me):
        return {
            d: begin(remote(src_of(turned(me, d)), into.at[d - 1], gsem.at[r, 0, d - 1], gsem.at[r, 1, d - 1], axis, turned(me, d)))
            for d in (2, 1, 3)
        }

    moved = pass_on(0, lambda k: gain_part.at[pl.ds(pl.multiple_of(4 * k, 4), 4)], gain_z, "shard", z)
    for d in (1, 3, 2):
        wide_sent[0, d].wait_recv()
    wide_sum[0] = (
        terms[pl.ds(pl.multiple_of(4 * z, 4), 4), :, 0 : 2 * wide].astype(f32)
        + wide_in[0, 0].astype(f32) + wide_in[0, 1].astype(f32) + wide_in[0, 2].astype(f32)
    ).astype(bf16)
    thin_sent = {}
    for d in (2, 1, 3):
        kx = turned(x, d)
        thin_sent[0, d] = begin(remote(wide_sum.at[0, kx], thin_in.at[0, d - 1], tsem.at[0, 0, d - 1], tsem.at[0, 1, d - 1], "x", kx))
    for d in (1, 3, 2):
        for q in range(4):
            wide_sent[1, d, q].wait_recv()
    for q in range(4):
        wide_sum[1, q] = (
            terms[4 * q + x, :, 2 * wide : 4 * wide].astype(f32)
            + wide_in[1, 0, q].astype(f32) + wide_in[1, 1, q].astype(f32) + wide_in[1, 2, q].astype(f32)
        ).astype(bf16)
    for d in (2, 1, 3):
        kz = turned(z, d)
        thin_sent[1, d] = begin(remote(wide_sum.at[1, kz], thin_in.at[1, d - 1], tsem.at[1, 0, d - 1], tsem.at[1, 1, d - 1], "shard", kz))
    for d in (1, 3, 2):
        moved[d].wait_recv()
    gain_part[pl.ds(pl.multiple_of(4 * z, 4), 4)] += gain_z[0] + gain_z[1] + gain_z[2]
    moved = pass_on(1, lambda k: gain_part.at[4 * z + k], gain_x, "x", x)
    for d in (1, 3, 2):
        moved[d].wait_recv()
    gain_y[3] = gain_part[4 * z + x] + gain_x[0] + gain_x[1] + gain_x[2]
    moved = pass_on(2, lambda k: gain_y.at[3], gain_y, "tensor", y)
    for d in (1, 3, 2):
        moved[d].wait_recv()
    gain_c[0] = (gain_y[0] + gain_y[1]) + (gain_y[2] + gain_y[3])
    across = begin(remote(gain_c.at[0], gain_c.at[1], gsem.at[3, 0, 0], gsem.at[3, 1, 0], "core", 1 - c))
    for s, me in ((0, x), (1, z)):
        for d in (1, 3, 2):
            thin_sent[s, d].wait_recv()
        thin_sum[:, s * 2 * wide : (s + 1) * 2 * wide] = (
            wide_sum[s, me].astype(f32)
            + thin_in[s, 0].astype(f32) + thin_in[s, 1].astype(f32) + thin_in[s, 2].astype(f32)
        ).astype(bf16)
    rows = width // 32
    mine = pl.ds(pl.multiple_of(c * rows, rows), rows)
    theirs = pl.ds(pl.multiple_of((1 - c) * rows, rows), rows)
    last = begin(remote(thin_sum.at[theirs], grads.at[c], outsem.at[0], outsem.at[1], "core", 1 - c))
    grads[c] = thin_sum[mine, :]
    across.wait_recv()
    gain_out[...] = gain_c[0] + gain_c[1]
    last.wait_recv()
    for shared in (out_shared, in_shared):
        for d in (1, 3, 2):
            shared[d].wait_recv()
    for copy in waits:
        copy.wait_send()


def attention_backward(
    d_part, mix_part, middle, own_tokens, own_cot, gain_rows, weights, low, normed, qkv, attended, lse, start, table
):
    chip, width = normed.shape
    seq = start.shape[1]
    quarter = chip // 8
    columns = weights.shape[1]
    sds = jax.ShapeDtypeStruct
    dma = pltpu.SemaphoreType.DMA
    vmem = pltpu.VMEM
    return pl.pallas_call(
        backward_kernel,
        out_shape=(
            sds((4, quarter, width), bf16),
            sds((4, quarter, width), bf16),
            sds((2, width // 32, columns), bf16),
            sds((8, 128), f32),
        ),
        in_specs=[VMEM] * 14,
        out_specs=(VMEM,) * 4,
        scratch_shapes=[
            vmem((2, 4, quarter, width), bf16),
            vmem((quarter, width), f32),
            vmem((3, 4, quarter, width), bf16),
            vmem((3, 4, quarter, width), bf16),
            vmem((3, 3, quarter, width), bf16),
            vmem((4, chip, HEAD_DIM), bf16),
            vmem((4, chip, HEAD_DIM), bf16),
            vmem((HEAD_DIM, seq), bf16),
            vmem((seq, HEAD_DIM), f32),
            vmem((seq, HEAD_DIM), f32),
            vmem((4, chip * 3 // 2, 128), bf16),
            vmem((4, chip * 3 // 2, 128), bf16),
            vmem((2, 4, quarter, width), bf16),
            vmem((width, chip), bf16),
            vmem((16, width // 16, columns), bf16),
            vmem((2, 3, 4, width // 16, columns // 2), bf16),
            vmem((2, 4, width // 16, columns // 2), bf16),
            vmem((2, 3, width // 16, columns // 2), bf16),
            vmem((width // 16, columns), bf16),
            vmem((16, 8, 128), f32),
            vmem((4, 8, 128), f32),
            vmem((2, 8, 128), f32),
            vmem((3, 8, 128), f32),
            vmem((3, 4, 8, 128), f32),
            dma((3, 2, 4)), dma((3, 2, 3)), dma((3, 2, 3)), dma((2, 4)), dma((2, 3)), dma((2, 4)),
            dma((5, 2, 3)), dma((2, 2, 3)), dma((4, 2, 3)), dma((2,)),
        ],
        compiler_params=pltpu.CompilerParams(
            collective_id=2, has_side_effects=True, vmem_limit_bytes=60 << 20
        ),
    )(d_part, mix_part, middle, own_tokens, own_cot, gain_rows, weights, low, normed, qkv, attended, lse, start, table)


def halves(arrays):
    return jnp.stack(
        [
            jnp.concatenate([a[:, c * (a.shape[1] // 2) : (c + 1) * (a.shape[1] // 2)] for a in arrays], axis=1)
            for c in range(2)
        ]
    )


def angle_table(positions):
    half = HEAD_DIM // 2
    frequency = rope_base ** (-(jnp.arange(half, dtype=f32) * 2.0) / HEAD_DIM)
    angle = positions.astype(f32)[:, None] * frequency[None, :]
    cosine, sine = jnp.cos(angle), jnp.sin(angle)
    return jnp.concatenate([cosine, cosine, -sine, sine], axis=1)


def body(
    tokens_in,
    cotangent,
    segments,
    positions,
    norm1_gain,
    q_weight,
    k_weight,
    v_weight,
    o_weight,
    norm2_gain,
    gate_weight,
    up_weight,
    down_weight,
):
    rows, width = tokens_in.shape
    tensor, core = lax.axis_index("tensor"), lax.axis_index("core")
    quarter = rows // 4
    mlp_block = lax.all_to_all(halves((gate_weight, up_weight, down_weight.T)), "core", 0, 0)
    mlp_block = mlp_block.reshape(2 * gate_weight.shape[0], -1)
    mlp_full = lax.all_gather(mlp_block, ("shard", "x"), axis=0, tiled=True)
    gains = jnp.stack([norm1_gain, norm2_gain])
    gains = lax.dynamic_update_slice(jnp.zeros((16, 128), bf16), gains, (0, core * gains.shape[1]))
    seq_segs = segments[0]
    start = jnp.sum((seq_segs[:, None] < seq_segs[None, :]).astype(jnp.int32), axis=0)[None, :]
    full, _, chip_tokens, chip_cot, chip_table, normed_one, gain_rows = gather_attention(
        q_weight, k_weight, v_weight, o_weight.T, gains, tokens_in, cotangent, angle_table(positions)
    )
    weights = full.reshape(width, -1)
    table = chip_table.reshape(2 * rows, -1)
    qkv, low, attended, lse, middle, normed_two = attention_forward(
        normed_one, weights, table, start, chip_tokens, gain_rows
    )
    mixed, d_normed, terms = mlp(normed_two.reshape(2 * rows, width), chip_cot.reshape(2 * rows, width), mlp_full)
    mlp_grads = lax.psum_scatter(terms, ("shard", "x"), scatter_dimension=0, tiled=True)
    own_tokens = lax.dynamic_slice_in_dim(tokens_in, tensor * quarter, quarter)
    own_cot = lax.dynamic_slice_in_dim(cotangent, tensor * quarter, quarter)
    split = (2, 4, quarter, width)
    layer_out, input_grad, attn_grads, gain_grads = attention_backward(
        d_normed.reshape(split), mixed.reshape(split), middle, own_tokens, own_cot, gain_rows, weights,
        low, normed_one, qkv, attended, lse, start, table,
    )
    gain_own = lax.dynamic_slice(gain_grads, (0, core * norm1_gain.shape[0]), (2, norm1_gain.shape[0]))
    narrow = attn_grads.shape[2] // 4
    mlp_grads = mlp_grads.reshape(3, 2, rows // 4, -1).transpose(1, 0, 2, 3)
    mlp_grads = lax.all_to_all(mlp_grads, "core", 0, 0)

    def attn_of(k):
        piece = attn_grads[:, :, k * narrow : (k + 1) * narrow].astype(f32)
        return jnp.concatenate([piece[0], piece[1]], axis=1)

    def mlp_of(k):
        return jnp.concatenate([mlp_grads[0, k], mlp_grads[1, k]], axis=1).astype(f32)

    return (
        layer_out.reshape(rows, width),
        input_grad.reshape(rows, width),
        gain_own[0],
        attn_of(0),
        attn_of(1),
        attn_of(2),
        attn_of(3).T,
        gain_own[1],
        mlp_of(0),
        mlp_of(1),
        mlp_of(2).T,
    )


def solution(mesh):
    apart = Mesh(mesh.devices.reshape(4, 4, 2, 4), ("shard", "x", "core", "tensor"))
    tokens = ("shard", "x", "core")
    placed = (
        P(tokens, None),
        P(tokens, None),
        P("shard", None),
        P(tokens),
        P(tokens),
        P(tokens, "tensor"),
        P(tokens, "tensor"),
        P(tokens, "tensor"),
        P("tensor", tokens),
        P(tokens),
        P(tokens, "tensor"),
        P(tokens, "tensor"),
        P("tensor", tokens),
    )
    return jax.shard_map(
        body,
        mesh=apart,
        in_specs=placed,
        out_specs=(
            P(tokens, None),
            P(tokens, None),
            P(tokens),
            P(tokens, "tensor"),
            P(tokens, "tensor"),
            P(tokens, "tensor"),
            P("tensor", tokens),
            P(tokens),
            P(tokens, "tensor"),
            P(tokens, "tensor"),
            P("tensor", tokens),
        ),
        check_vma=False,
    )
```

```python
import jax
import jax.numpy as jnp
from jax import lax
from jax.experimental import pallas as pl
from jax.experimental.pallas import tpu as pltpu
from jax.sharding import Mesh
from jax.sharding import PartitionSpec as P

HEAD_DIM = 64
BLOCK = 512

epsilon = 1e-05
rope_base = 130000.0
masked_low = -1000000000.0

f32 = jnp.float32
bf16 = jnp.bfloat16
MESH = pl.DeviceIdType.MESH
VMEM = pl.BlockSpec(memory_space=pltpu.VMEM)
HBM = pl.BlockSpec(memory_space=pl.ANY)


def dot_nn(a, b):
    return lax.dot_general(a, b, (((1,), (0,)), ((), ())), preferred_element_type=f32)


def dot_nt(a, b):
    return lax.dot_general(a, b, (((1,), (1,)), ((), ())), preferred_element_type=f32)


def place():
    return tuple(lax.axis_index(a) for a in ("shard", "x", "core", "tensor"))


def turned(index, step):
    return lax.rem(index + step, 4)


def some(index, size):
    return pl.ds(pl.multiple_of(index * size, size), size)


def meet(axes):
    barrier = pltpu.get_barrier_semaphore()
    count = 0
    for axis in axes:
        me = lax.axis_index(axis)
        peers = [1 - me] if axis == "core" else [turned(me, d) for d in (1, 2, 3)]
        for peer in peers:
            pl.semaphore_signal(barrier, inc=1, device_id={axis: peer}, device_id_type=MESH)
            count += 1
    pl.semaphore_wait(barrier, count)


def remote(src, dst, send, recv, axis, index):
    return pltpu.make_async_remote_copy(
        src_ref=src, dst_ref=dst, send_sem=send, recv_sem=recv, device_id={axis: index}, device_id_type=MESH
    )


class Gather:
    def __init__(self, axis, me, block, half, sems, waits):
        self.axis, self.me, self.block, self.half, self.sems, self.waits = axis, me, block, half, sems, waits

    def send(self, ref, slot, step):
        copy = remote(ref, ref, self.sems.at[0, slot], self.sems.at[1, slot], self.axis, turned(self.me, step))
        copy.start()
        self.waits.append(copy)
        return copy

    def start(self):
        mine = self.block(self.me)
        self.right, self.left = self.send(mine, 0, 1), self.send(mine, 1, 3)

    def forward(self):
        self.right.wait_recv()
        self.right_on = self.send(self.half(turned(self.me, 3), 0), 2, 1)
        self.left.wait_recv()
        self.left_on = self.send(self.half(turned(self.me, 1), 1), 3, 3)

    def finish(self):
        self.right_on.wait_recv()
        self.left_on.wait_recv()


class Reduce:
    def __init__(self, axis, me, half, early, late, carried, sems, waits):
        self.axis, self.me, self.half, self.sems, self.waits = axis, me, half, sems, waits
        self.early, self.late, self.carried = early, late, carried

    def send(self, src, dst, slot, step):
        copy = remote(src, dst, self.sems.at[0, slot], self.sems.at[1, slot], self.axis, turned(self.me, step))
        copy.start()
        self.waits.append(copy)
        return copy

    def start(self):
        far, right, left = turned(self.me, 2), turned(self.me, 1), turned(self.me, 3)
        self.far = [
            self.send(self.half(far, 0), self.early(0), 0, 1),
            self.send(self.half(far, 1), self.early(1), 1, 3),
        ]
        self.plain = [
            self.send(self.half(right, 1), self.late(0, 1), 2, 1),
            self.send(self.half(left, 0), self.late(1, 0), 3, 3),
        ]

    def join(self, add):
        for h in range(2):
            self.far[h].wait_recv()
            add(h)

    def pass_on(self):
        self.both = [self.send(self.carried(h), self.late(h, h), 4 + h, step) for h, step in ((0, 1), (1, 3))]

    def middle(self, add):
        self.join(add)
        self.pass_on()

    def finish(self):
        for copy in self.plain + self.both:
            copy.wait_recv()


def rope(vectors, table_cos, table_sin):
    n = vectors.shape[1]
    lane = lax.broadcasted_iota(jnp.int32, vectors.shape, 1)
    other = jnp.where(
        lax.rem(lane, HEAD_DIM) < HEAD_DIM // 2,
        pltpu.roll(vectors, n - HEAD_DIM // 2, 1),
        pltpu.roll(vectors, HEAD_DIM // 2, 1),
    )
    return vectors * table_cos + other * table_sin


def masked(raw, begin, j, i, diagonal):
    key = lax.broadcasted_iota(jnp.int32, raw.shape, 0)
    allowed = key >= begin - j * BLOCK
    if diagonal:
        allowed = allowed & (key <= lax.broadcasted_iota(jnp.int32, raw.shape, 1))
    return jnp.where(allowed, raw, masked_low)


def forward_kernel(
    wq, wk, wv, wo, wg, wu, wd, gain_one, gain_two, tokens, cot, rotary, seg_row,
    full_out, table_out, normed_out, packed_out, low_out, attended_out, middle_out, mixed_out, d_normed_out, terms_out,
    gain_rows, start, lse,
    full, normed, table, low, attended_t, middle, normed_two,
    gains, attn_give, mlp_give, gain_all, chip_tokens, packed, arrived, keys, value_t, scaled_q,
    head_out, low_in, own, other, pair, near,
    mlp_full, cot_held, cot_t, normed_t, both, made_hidden, made, d_held, mixed_held, d_hidden_held,
    local, core_sem, out_sem, made_sem, ring_sem, gain_sem, xsem, lsem, csem, ysem, asem, fsem,
):
    z, x, c, y = place()
    half = wq.shape[1] // 2
    shard = wq.shape[0]
    hidden = wg.shape[1] // 2
    groups = 2
    span = hidden // groups
    chip, width = normed.shape
    waits = []
    meet(("core", "x", "shard", "tensor"))

    at = some(c, shard)
    lane = lax.broadcasted_iota(jnp.int32, (8, 128), 1) // (2 * shard // 2)
    both_gains = jnp.concatenate(
        [gain_one[...].astype(f32), gain_two[...].astype(f32), jnp.zeros((6, shard), f32)], axis=0
    )
    both_gains = jnp.where(lane == c, jnp.concatenate([both_gains, both_gains], axis=1), 0.0)
    gains[...] = jnp.concatenate([both_gains, jnp.zeros((8, 128), f32)], axis=0).astype(bf16)
    for k, w in enumerate((wq, wk, wv, wo)):
        attn_give[:, k * half : (k + 1) * half] = w[:, some(1 - c, half)]
        full[z, x, at, k * half : (k + 1) * half] = w[:, some(c, half)]
    for k, w in enumerate((wg, wu, wd)):
        for g in range(groups):
            lanes = slice((3 * g + k) * span, (3 * g + k + 1) * span)
            mlp_give[:, lanes] = w[:, some((1 - c) * groups + g, span)]
            mlp_full[z, x, at, lanes] = w[:, some(c * groups + g, span)]
    pairs = [(gains, gains, gain_all.at[z, x, c]), (None, attn_give, full.at[z, x, at, :])]
    pairs += [(None, mlp_give, mlp_full.at[z, x, at, :])]
    pairs += [(a, a, b.at[c]) for a, b in ((tokens, chip_tokens), (rotary, table), (cot, cot_held))]
    inside, across = [], []
    for k, (mine, theirs, there) in enumerate(pairs):
        inside.append(pltpu.make_async_copy(mine, there, local.at[k]) if mine is not None else None)
        across.append(remote(theirs, there, core_sem.at[0, k], core_sem.at[1, k], "core", 1 - c))
        across[-1].start()
        if mine is not None:
            inside[-1].start()
    waits += across
    kept = []

    def keep(src, dst):
        kept.append(pltpu.make_async_copy(src, dst, out_sem.at[len(kept)]))
        kept[-1].start()

    def here(ks):
        for k in ks:
            if inside[k] is not None:
                inside[k].wait()
            across[k].wait_recv()

    def spread(src, r, axis, me):
        copies = []
        for d in (1, 2, 3):
            copies.append(remote(src, src, gain_sem.at[0, r, d - 1], gain_sem.at[1, r, d - 1], axis, turned(me, d)))
            copies[-1].start()
        waits.extend(copies)
        return copies

    all_rings = []

    def ring(axis, block, half_of):
        all_rings.append(Gather(axis, x if axis == "x" else z, block, half_of, ring_sem.at[len(all_rings)], waits))
        return all_rings[-1]

    def half_rows(h):
        return pl.ds(h * shard, shard)

    def both_of(p):
        return pl.ds(2 * p, 2)

    def first_along(axis, array, lanes):
        if axis == "x":
            return ring("x", lambda k: array.at[z, k, :, lanes], lambda k, h: array.at[z, k, half_rows(h), lanes])
        return ring("shard", lambda k: array.at[k, x, :, lanes], lambda k, h: array.at[k, x, half_rows(h), lanes])

    def then_along(axis, array, lanes):
        if axis == "x":
            return [
                ring("x", lambda k, p=p: array.at[both_of(p), k, :, lanes], lambda k, h, p=p: array.at[2 * p + h, k, :, lanes])
                for p in range(2)
            ]
        return [
            ring("shard", lambda k, p=p: array.at[k, both_of(p), :, lanes], lambda k, h, p=p: array.at[k, 2 * p + h, :, lanes])
            for p in range(2)
        ]

    qkv_a, qkv_b, out_a = pl.ds(0, 3 * half // 2), pl.ds(3 * half // 2, 3 * half // 2), pl.ds(3 * half, half)
    late_a = 3 * span * 7 // 12 // 128 * 128
    mlp_a1, mlp_b1 = pl.ds(0, 3 * span // 2), pl.ds(3 * span // 2, 3 * span // 2)
    mlp_a2, mlp_b2 = pl.ds(3 * span, late_a), pl.ds(3 * span + late_a, 3 * span - late_a)
    ax, az = first_along("x", full, qkv_a), then_along("shard", full, qkv_a)
    bz, bx = first_along("shard", full, qkv_b), then_along("x", full, qkv_b)
    ox, oz = first_along("x", full, out_a), then_along("shard", full, out_a)
    mx1, mz1 = first_along("x", mlp_full, mlp_a1), then_along("shard", mlp_full, mlp_a1)
    nz1, nx1 = first_along("shard", mlp_full, mlp_b1), then_along("x", mlp_full, mlp_b1)
    mx2, mz2 = first_along("x", mlp_full, mlp_a2), then_along("shard", mlp_full, mlp_a2)
    nz2, nx2 = first_along("shard", mlp_full, mlp_b2), then_along("x", mlp_full, mlp_b2)

    def start_all(rings):
        for one in rings:
            one.start()

    def forward_all(rings):
        for one in rings:
            one.forward()

    def finish_all(rings):
        for one in rings:
            one.finish()

    here((0,))
    gain_x = spread(gain_all.at[z, x], 0, "x", x)
    here((1,))
    start_all((ax, bz))
    here((2,))
    start_all((mx1, nz1))
    for copy in gain_x:
        copy.wait_recv()
    gain_z = spread(gain_all.at[z], 1, "shard", z)
    forward_all((ax, bz))
    ox.start()
    forward_all((mx1, nz1))
    ax.finish()
    start_all(az)
    bz.finish()
    start_all(bx)
    ox.forward()

    for copy in gain_z:
        copy.wait_recv()
    for i in range(16):
        two = (gain_all[i // 4, i % 4, 0] + gain_all[i // 4, i % 4, 1]).astype(f32)
        gain_rows[:, pl.ds(i * 128, 128)] = two[0:8, :]
    here((3, 4))

    def norm(i, unused):
        values = chip_tokens[i // 4, some(lax.rem(i, 4), 64), :].astype(f32)
        scale = lax.rsqrt(jnp.mean(values * values, axis=-1, keepdims=True) + epsilon)
        normed[some(i, 64), :] = ((values * scale) * gain_rows[0:1, :]).astype(bf16)
        return unused

    lax.fori_loop(0, chip // 64, norm, 0)
    keep(normed, normed_out)
    keep(table, table_out)
    row = seg_row[...].astype(f32)
    begins = [jnp.zeros((1, BLOCK), f32)] * 4
    for i in range(4):
        column = jnp.transpose(jnp.broadcast_to(row[:, i * BLOCK : (i + 1) * BLOCK], (128, BLOCK)))[:, 0:1]
        for j in range(i, 4):
            earlier = column < row[:, j * BLOCK : (j + 1) * BLOCK]
            begins[j] = begins[j] + jnp.sum(jnp.where(earlier, 1.0, 0.0), axis=0, keepdims=True)
    for i in range(4):
        start[:, i * BLOCK : (i + 1) * BLOCK] = begins[i].astype(jnp.int32)
    forward_all((az[0], bx[0], az[1], bx[1]))
    start_all((mx2, nz2))
    ox.finish()
    start_all(oz)
    mx1.finish()
    start_all(mz1)
    finish_all(az + bx)

    wide = 4 * HEAD_DIM

    def weights(k):
        return full[:, :, :, k * wide : (k + 1) * wide].reshape(width, wide)

    rotation = table[...].reshape(chip, 128)
    cosine = jnp.concatenate([rotation[:, 0:64]] * 4, axis=1)
    sine = jnp.concatenate([rotation[:, 64:128]] * 4, axis=1)
    queries = rope(dot_nn(normed[...], weights(0)), cosine, sine).astype(bf16)
    turned_keys = rope(dot_nn(normed[...], weights(1)), cosine, sine).astype(bf16)
    values = dot_nn(normed[...], weights(2)).astype(bf16)
    for h in range(4):
        lanes = slice(h * HEAD_DIM, (h + 1) * HEAD_DIM)
        packed[h, 0:chip, :] = jnp.concatenate([queries[:, lanes], turned_keys[:, lanes]], axis=1)
        packed[h, chip:, :] = jnp.concatenate(
            [values[0 : chip // 2, lanes], values[chip // 2 :, lanes]], axis=1
        )
    sent = []
    for d in (2, 1, 3):
        k = turned(x, d)
        sent.append(remote(packed.at[k], arrived.at[x], xsem.at[0, d - 1], xsem.at[1, d - 1], "x", k))
        sent[-1].start()
    waits += sent
    forward_all((mx2, nz2))
    forward_all(oz)
    nz1.finish()
    start_all(nx1)
    arrived[x] = packed[x]
    for copy in sent:
        copy.wait_recv()
    for k in range(4):
        rows = slice(k * chip, (k + 1) * chip)
        scaled_q[rows, :] = arrived[k, 0:chip, 0:64] * HEAD_DIM ** (-0.5)
        keys[rows, :] = arrived[k, 0:chip, 64:128]
        block = jnp.concatenate([arrived[k, chip:, 0:64], arrived[k, chip:, 64:128]], axis=0)
        value_t[:, rows] = jnp.transpose(block)
    keep(arrived, packed_out)

    for i in range(4):
        if i == 2:
            mz1[0].forward()
        if i == 3:
            mx2.finish()
            start_all(mz2)
        at = slice(i * BLOCK, (i + 1) * BLOCK)
        begin = start[:, at]
        mine = scaled_q[at, :]

        def step(j, state, diagonal=False):
            peak, total, summed = state
            scores = masked(dot_nt(keys[some(j, BLOCK), :], mine), begin, j, i, diagonal)
            new = jnp.maximum(peak, jnp.max(scores, axis=0, keepdims=True))
            weight = jnp.exp(scores - new)
            factor = jnp.exp(peak - new)
            total = total * factor + jnp.sum(weight, axis=0, keepdims=True)
            summed = summed * factor + dot_nn(value_t[:, some(j, BLOCK)], weight.astype(bf16))
            return (new, total, summed)

        state = (
            jnp.full((1, BLOCK), masked_low, f32),
            jnp.zeros((1, BLOCK), f32),
            jnp.zeros((HEAD_DIM, BLOCK), f32),
        )
        state = step(i, state, True)
        peak, total, summed = lax.fori_loop(0, i, step, state) if i else state
        attended = summed / total
        attended_t[:, at] = attended
        lse[:, at] = peak + jnp.log(total)
        head_out[i] = jnp.transpose(attended).astype(bf16)

        @pl.when(x != i)
        def send(i=i):
            remote(head_out.at[i], low_in.at[x], lsem.at[0, i], lsem.at[1, x], "x", i).start()

    nz2.finish()
    start_all(nx2)
    mz1[1].forward()
    nx1[0].forward()
    low_in[x] = head_out[x]
    for d in (1, 2, 3):
        k = turned(x, d)
        copy = remote(head_out.at[k], low_in.at[k], lsem.at[0, k], lsem.at[1, k], "x", k)
        copy.wait_recv()
        waits.append(copy)
    low[...] = jnp.concatenate([low_in[h] for h in range(4)], axis=1)
    finish_all(oz)
    keep(full, full_out)
    keep(low, low_out)
    keep(attended_t, attended_out)

    side, quarter = chip // 2, chip // 8
    out_weights = weights(3)
    other[...] = dot_nt(low[some(1 - c, side), :], out_weights).astype(bf16).reshape(other.shape)
    crossed = {}
    for d in (2, 1, 3, 0):
        k = turned(y, d)
        crossed[d] = remote(other.at[k], pair.at[k], csem.at[0, d], csem.at[1, d], "core", 1 - c)
        crossed[d].start()
    own[...] = dot_nt(low[some(c, side), :], out_weights).reshape(own.shape)
    along = {}
    for d in (2, 1, 3):
        k = turned(y, d)
        crossed[d].wait_recv()
        crossed[d].wait_send()
        other[k] = (own[k] + pair[k].astype(f32)).astype(bf16)
        along[d] = remote(other.at[k], near.at[d - 1], ysem.at[0, d - 1], ysem.at[1, d - 1], "tensor", k)
        along[d].start()
    crossed[0].wait_recv()
    crossed[0].wait_send()
    here((5,))
    nx1[1].forward()
    cot_t[...] = jnp.transpose(cot_held[...].reshape(chip, width))
    mz2[0].forward()
    total = own[y] + pair[y].astype(f32)
    for d in (1, 3, 2):
        along[d].wait_recv()
        total = total + near[d - 1].astype(f32)
    waits += [*along.values()]
    mid = chip_tokens[c, some(y, quarter), :].astype(f32) + total
    middle[...] = mid
    keep(middle, middle_out)
    scale = lax.rsqrt(jnp.mean(mid * mid, axis=-1, keepdims=True) + epsilon)
    normed_two[c, y] = ((mid * scale) * gain_rows[1:2, :]).astype(bf16)
    share = Gather(
        "tensor", y, lambda k: normed_two.at[c, k], lambda k, h: normed_two.at[c, k, pl.ds(h * quarter // 2, quarter // 2)],
        asem, waits,
    )
    forward = []

    def forward_on(k):
        slot = normed_two.at[c, k]
        d = len(forward)
        forward.append(remote(slot, slot, fsem.at[0, d], fsem.at[1, d], "core", 1 - c))
        forward[-1].start()

    share.start()
    forward_on(y)
    finish_all(nx1 + mz1)

    def group(g, k):
        return mlp_full[:, :, :, (3 * g + k) * span : (3 * g + k + 1) * span].reshape(width, span)

    chip_cot = cot_held[...].reshape(chip, width)
    share.forward()
    forward_on(turned(y, 3))
    forward_on(turned(y, 1))
    mz2[1].forward()
    nx2[0].forward()
    d_hidden_held[...] = dot_nn(chip_cot, group(0, 2))
    share.finish()
    forward_on(turned(y, 2))
    nx2[1].forward()
    for copy in forward:
        copy.wait_recv()
    waits += forward

    rows_two = normed_two[...].reshape(chip, width)
    normed_t[...] = jnp.transpose(rows_two)
    stores = {}
    for g in range(groups):
        if g == 1:
            finish_all(mz2 + nx2)
        gate = dot_nn(rows_two, group(g, 0))
        upper = dot_nn(rows_two, group(g, 1))
        d_hidden = dot_nn(chip_cot, group(g, 2)) if g else d_hidden_held[...]
        sigmoid = 1.0 / (1.0 + jnp.exp(-gate))
        silu = gate * sigmoid
        made_hidden[g] = (silu * upper).astype(bf16)
        both[g, :, 0:span] = (d_hidden * upper * (sigmoid * (1.0 + gate * (1.0 - sigmoid)))).astype(bf16)
        both[g, :, span : 2 * span] = (d_hidden * silu).astype(bf16)
        for k, (left, right) in enumerate(
            ((normed_t, both.at[g, :, 0:span]), (normed_t, both.at[g, :, span : 2 * span]), (cot_t, made_hidden.at[g]))
        ):
            if g:
                stores[g - 1, k].wait()
            for q in range(4):
                term = dot_nn(left[q * (width // 4) : (q + 1) * (width // 4), :], right[...])
                made[k, q] = term.astype(bf16).reshape(made.shape[2:])
            stores[g, k] = pltpu.make_async_copy(
                made.at[k], terms_out.at[:, :, :, pl.ds((3 * g + k) * span, span)], made_sem.at[g, k]
            )
            stores[g, k].start()
    for held, out, left, first, n in ((d_held, d_normed_out, both, 0, 2), (mixed_held, mixed_out, made_hidden, 2, 1)):
        for t in range(4):
            lanes = slice(t * (width // 4), (t + 1) * (width // 4))
            term = [
                dot_nt(
                    left[g],
                    mlp_full[t, :, :, (3 * g + first) * span : (3 * g + first + n) * span].reshape(width // 4, n * span),
                )
                for g in range(groups)
            ]
            held[:, lanes] = (term[0] + term[1]).astype(bf16)
        keep(held, out)
    for k in range(3):
        stores[groups - 1, k].wait()
    for copy in kept:
        copy.wait()
    for copy in waits:
        copy.wait_send()


def forward_pass(wq, wk, wv, wo, wg, wu, wd, gain_one, gain_two, tokens, cot, rotary, seg_row):
    rows, width = tokens.shape
    chip, quarter, seq = 2 * rows, rows // 4, seg_row.shape[1]
    columns, hidden = 2 * wq.shape[1], wg.shape[1] // 2
    sds = jax.ShapeDtypeStruct
    dma = pltpu.SemaphoreType.DMA
    vmem = pltpu.VMEM
    kept = (
        ((4, 4, width // 16, columns), bf16),
        ((chip, width), bf16),
        ((2, rows, 128), f32),
        ((chip, 4 * HEAD_DIM), bf16),
        ((HEAD_DIM, seq), f32),
        ((quarter, width), f32),
        ((2, 4, quarter, width), bf16),
    )
    full, normed, table, low, attended, middle, _ = (sds(*a) for a in kept)
    span = hidden // 2
    packed = (4, chip * 3 // 2, 128)
    return pl.pallas_call(
        forward_kernel,
        out_shape=(
            full,
            table,
            normed,
            sds(packed, bf16),
            low,
            attended,
            middle,
            sds((chip, width), bf16),
            sds((chip, width), bf16),
            sds((4, 4, width // 16, 3 * hidden), bf16),
            sds((8, width), f32),
            sds((1, seq), jnp.int32),
            sds((1, seq), f32),
        ),
        in_specs=[VMEM] * 9 + [HBM] * 3 + [VMEM],
        out_specs=(HBM,) * 10 + (VMEM,) * 3,
        scratch_shapes=[
            *(vmem(*a) for a in kept),
            vmem((16, 128), bf16),
            vmem((width // 32, columns), bf16),
            vmem((width // 32, 3 * hidden), bf16),
            vmem((4, 4, 2, 16, 128), bf16),
            vmem((2, rows, width), bf16),
            vmem(packed, bf16),
            vmem(packed, bf16),
            vmem((seq, HEAD_DIM), bf16),
            vmem((HEAD_DIM, seq), bf16),
            vmem((seq, HEAD_DIM), bf16),
            vmem((4, chip, HEAD_DIM), bf16),
            vmem((4, chip, HEAD_DIM), bf16),
            vmem((4, quarter, width), f32),
            vmem((4, quarter, width), bf16),
            vmem((4, quarter, width), bf16),
            vmem((3, quarter, width), bf16),
            vmem((4, 4, width // 16, 3 * hidden), bf16),
            vmem((2, rows, width), bf16),
            vmem((width, chip), bf16),
            vmem((width, chip), bf16),
            vmem((2, chip, 2 * span), bf16),
            vmem((2, chip, span), bf16),
            vmem((3, 4, 4, width // 16, span), bf16),
            vmem((chip, width), bf16),
            vmem((chip, width), bf16),
            vmem((chip, span), f32),
            dma((6,)), dma((2, 6)), dma((9,)), dma((2, 3)), dma((21, 2, 4)), dma((2, 2, 3)), dma((2, 3)), dma((2, 4)),
            dma((2, 4)), dma((2, 3)), dma((2, 4)), dma((2, 4)),
        ],
        compiler_params=pltpu.CompilerParams(
            collective_id=0, has_side_effects=True, vmem_limit_bytes=62 << 20
        ),
    )(wq, wk, wv, wo, wg, wu, wd, gain_one, gain_two, tokens, cot, rotary, seg_row)


def backward_kernel(
    d_part_in, mix_part_in, middle_in, tokens_in, cot_in, gain_rows_in, weights_in, low_in, normed_in, packed_in, attended_in,
    lse, start, table_in, mlp_terms,
    layer_out, input_grad, swapped_m, swapped_a, gain_out, landed_z, landed_x,
    d_part, mix_part, middle, own_tokens, own_cot, gain_rows, weights, low, normed, qkv_packed, attended, table,
    queries, keys, values,
    d_branch, d_mid, pair, half_sum, near, heads, head_in, key_t, d_key, d_value, packed, arrived,
    turned_rows, terms, m_early_z, m_early_x, m_carry_z, m_carry_x, m_mine_z, m_mine_x,
    m2_early_z, m2_early_x, m2_late_z, m2_late_x, m2_carry_z, m2_carry_x, m2_mine,
    a_early, a_late, a_carry, a_mine, a2_early, a2_late, a2_carry, a2_mine,
    gain_part, gain_y, gain_c, gain_x, gain_z,
    csem, ysem, asem, fsem, hsem, psem, rsem, local, gsem, outsem, in_sem,
):
    z, x, c, y = place()
    quarter = middle.shape[0]
    mine_at = some(y, quarter)
    taken = {}
    for k, (name, src, dst) in enumerate(
        (
            ("d_part", d_part_in.at[c], d_part),
            ("middle", middle_in, middle),
            ("gain_rows", gain_rows_in, gain_rows),
            ("own_cot", cot_in.at[mine_at, :], own_cot),
            ("mix_part", mix_part_in.at[c], mix_part),
            ("packed", packed_in, qkv_packed),
            ("weights", weights_in, weights),
            ("low", low_in, low),
            ("attended", attended_in, attended),
            ("normed", normed_in, normed),
            ("table", table_in, table),
            ("own_tokens", tokens_in.at[mine_at, :], own_tokens),
        )
    ):
        taken[name] = pltpu.make_async_copy(src, dst, in_sem.at[k])
        taken[name].start()

    def take(*names):
        for name in names:
            taken[name].wait()

    meet(("core", "x", "tensor", "shard"))
    chip, width = normed.shape
    side = chip // 2
    wide = 4 * HEAD_DIM
    shard = width // 32
    a_split = a_mine.shape[3]
    m_split = m_mine_z.shape[2]
    landed, m_early, m_carry, m_mine = (landed_z, landed_x), (m_early_z, m_early_x), (m_carry_z, m_carry_x), (m_mine_z, m_mine_x)
    m2_early, m2_late, m2_carry = (m2_early_z, m2_early_x), (m2_late_z, m2_late_x), (m2_carry_z, m2_carry_x)
    m_lanes = (pl.ds(0, m_split), pl.ds(m_split, m_mine_x.shape[2]))
    a_lanes = (pl.ds(0, a_split), pl.ds(a_split, a_split))
    waits = []

    def begin(copy):
        copy.start()
        waits.append(copy)
        return copy

    def sent_all(copies):
        for copy in copies:
            copy.wait_send()
        waits[:] = [w for w in waits if not any(w is copy for copy in copies)]

    def cross(r, part):
        return {
            d: begin(remote(part.at[turned(y, d)], pair.at[r % 2, turned(y, d)], csem.at[r, 0, d], csem.at[r, 1, d], "core", 1 - c))
            for d in (2, 1, 3, 0)
        }

    def along(r, part, crossed):
        sent = {}
        for d in (2, 1, 3):
            k = turned(y, d)
            crossed[d].wait_recv()
            half_sum[r % 2, d - 1] = part[k] + pair[r % 2, k]
            sent[d] = begin(remote(half_sum.at[r % 2, d - 1], near.at[r % 2, d - 1], ysem.at[r, 0, d - 1], ysem.at[r, 1, d - 1], "tensor", k))
        return sent

    def total_of(r, part, crossed, sent):
        crossed[0].wait_recv()
        total = part[y].astype(f32) + pair[r % 2, y].astype(f32)
        for d in (1, 3, 2):
            sent[d].wait_recv()
            total = total + near[r % 2, d - 1].astype(f32)
        return total

    def share(r, slot):
        cut = quarter // 2
        ring = Gather("tensor", y, slot, lambda k, h: slot(k).at[pl.ds(h * cut, cut)], asem.at[r], waits)
        ring.start()
        return ring

    def two(h):
        return pl.ds(2 * h, 2)

    def rows(h):
        return pl.ds(h * shard, shard)

    def apart(ref):
        return (ref.at[0], ref.at[1])

    def first_step(s, source, split, early, late, carry, r):
        axis, me = (("shard", z), ("x", x))[s]
        columns = split[s]

        def half(k, h):
            return source.at[k, two(h), :, columns] if s == 0 else source.at[two(h), k, :, columns]

        return Reduce(
            axis, me, half, lambda h: early[s].at[two(h)], lambda e, h: late[s].at[e, two(h)],
            lambda h: carry[s].at[two(h)], rsem.at[r + s], waits,
        ), half

    def second_step(s, mine, early, late, carry, r):
        axis, me = (("x", x), ("shard", z))[s]
        return Reduce(
            axis, me, lambda k, h: mine[s].at[k, rows(h)], lambda h: early[s].at[rows(h)],
            lambda e, h: late[s].at[e, rows(h)], lambda h: carry[s].at[rows(h)], rsem.at[r + s], waits,
        )

    m_rings, m_halves = zip(*[first_step(s, mlp_terms, m_lanes, m_early, landed, m_carry, 0) for s in range(2)])
    loads = {}

    def load(src, dst, s, k):
        loads[s, k] = pltpu.make_async_copy(src, dst, local.at[s, k])
        loads[s, k].start()

    d_crossed = cross(0, d_part_in.at[1 - c])
    for s, me in ((0, z), (1, x)):
        m_rings[s].start()
        load(m_halves[s](turned(me, 1), 0), m_carry[s].at[two(0)], s, 0)
        load(m_halves[s](turned(me, 3), 1), m_carry[s].at[two(1)], s, 1)
        load(m_halves[s](me, 0), m_mine[s].at[two(0)], s, 2)
        load(m_halves[s](me, 1), m_mine[s].at[two(1)], s, 3)
    m_crossed = cross(1, mix_part_in.at[1 - c])
    take("d_part", "mix_part")
    d_sent = along(0, d_part, d_crossed)
    take("middle", "gain_rows", "own_cot", "packed")
    mid = middle[...]
    scale = lax.rsqrt(jnp.mean(mid * mid, axis=-1, keepdims=True) + epsilon)
    unit = mid * scale
    for k in range(4):
        at = slice(k * chip, (k + 1) * chip)
        queries[at, :] = qkv_packed[k, 0:chip, 0:64] * HEAD_DIM ** (-0.5)
        block = qkv_packed[k, 0:chip, 64:128]
        keys[at, :] = block
        key_t[:, at] = jnp.transpose(block)
        values[at, :] = jnp.concatenate([qkv_packed[k, chip:, 0:64], qkv_packed[k, chip:, 64:128]], axis=0)
    d_key[...] = jnp.zeros_like(d_key)
    d_value[...] = jnp.zeros_like(d_value)
    def add_far(ring, s):
        def add(h):
            loads[s, h].wait()
            for q in (2 * h, 2 * h + 1):
                m_carry[s][q] = m_carry[s][q] + m_early[s][q]

        ring.join(add)

    add_far(m_rings[1], 1)
    d_two = total_of(0, d_part, d_crossed, d_sent)
    gain_two_part = jnp.sum(d_two * unit, axis=0, keepdims=True)
    scaled = d_two * gain_rows[1:2, :]
    d_middle = own_cot[...].astype(f32) + scale * (
        scaled - unit * jnp.mean(scaled * unit, axis=-1, keepdims=True)
    )
    d_mid[...] = d_middle
    d_branch[c, y] = d_middle.astype(bf16)
    shared = share(0, lambda k: d_branch.at[c, k])
    forward = []

    def forward_on(k):
        slot, d = d_branch.at[c, k], len(forward)
        forward.append(begin(remote(slot, slot, fsem.at[0, d], fsem.at[1, d], "core", 1 - c)))

    forward_on(y)
    add_far(m_rings[0], 0)
    m_rings[0].pass_on()
    shared.forward()
    forward_on(turned(y, 3))
    forward_on(turned(y, 1))
    m_sent = along(1, mix_part, m_crossed)
    shared.finish()
    forward_on(turned(y, 2))
    for copy in forward:
        copy.wait_recv()
    branch = d_branch[...].reshape(chip, width)
    take("weights", "low", "attended", "normed", "table", "own_tokens")

    def weights_of(k, n):
        return weights[:, :, :, k * wide : (k + n) * wide].reshape(width, n * wide)

    d_heads = dot_nn(branch, weights_of(3, 1)).astype(bf16)
    for h in range(4):
        heads[h] = d_heads[:, h * HEAD_DIM : (h + 1) * HEAD_DIM]
    head_sent = {}
    for d in (2, 1, 3):
        k = turned(x, d)
        head_sent[d] = begin(remote(heads.at[k], head_in.at[x], hsem.at[0, d - 1], hsem.at[1, d - 1], "x", k))
    head_in[x] = heads[x]
    m_rings[1].pass_on()
    turned_rows[...] = jnp.transpose(branch)
    terms[:, :, :, 3 * wide : 4 * wide] = (
        dot_nn(turned_rows[...], low[...]).astype(bf16).reshape(4, 4, width // 16, wide)
    )
    for d in (1, 3, 2):
        head_sent[d].wait_recv()


    for i in (3, 2, 1, 0):
        at = slice(i * BLOCK, (i + 1) * BLOCK)
        mine, d_out = queries[at, :], head_in[i]
        center = jnp.sum(jnp.transpose(d_out.astype(f32)) * attended[:, at], axis=0, keepdims=True)
        peak, first = lse[:, at], start[:, at]

        def step(j, d_query, diagonal=False):
            key_at = some(j, BLOCK)
            scores = masked(dot_nt(keys[key_at, :], mine), first, j, i, diagonal)
            weight = jnp.exp(scores - peak)
            d_prob = dot_nt(values[key_at, :], d_out)
            d_raw = (weight * (d_prob - center)).astype(bf16)
            d_key[key_at, :] += dot_nn(d_raw, mine)
            d_value[key_at, :] += dot_nn(weight.astype(bf16), d_out)
            return d_query + dot_nn(key_t[:, key_at], d_raw)

        d_query = step(i, jnp.zeros((HEAD_DIM, BLOCK), f32), True)
        d_query = lax.fori_loop(0, i, step, d_query) if i else d_query
        packed[i, 0:chip, :] = jnp.concatenate(
            [jnp.transpose(d_query * HEAD_DIM ** (-0.5)).astype(bf16), d_key[at, :].astype(bf16)], axis=1
        )
        d_rows = d_value[at, :].astype(bf16)
        packed[i, chip:, :] = jnp.concatenate([d_rows[0:side], d_rows[side:]], axis=1)

        @pl.when(x != i)
        def send(i=i):
            remote(packed.at[i], arrived.at[x], psem.at[0, i], psem.at[1, x], "x", i).start()

    arrived[x] = packed[x]

    def close_first(ring, s):
        ring.finish()
        sent_all(ring.both)
        load(landed[s].at[0], m_carry[s], s, 4)
        load(landed[s].at[1], m_early[s], s, 5)

    def sum_first(s):
        for k in (2, 3, 4, 5):
            loads[s, k].wait()
        for q in range(4):
            m_mine[s][q] = (
                m_mine[s][q].astype(f32) + m_carry[s][q].astype(f32) + m_early[s][q].astype(f32)
            ).astype(bf16)

    def add_to(carry, early, mine, s, me):
        def add(h):
            at = slice(h * shard, (h + 1) * shard)
            k = turned(me, (1, 3)[h])
            carry[s][at, :] = mine[s][k, at, :] + early[s][at, :]

        return add

    m2_rings = [second_step(s, m_mine, m2_early, m2_late, m2_carry, 2) for s in range(2)]
    close_first(m_rings[1], 1)
    layer_out[y] = (mid + total_of(1, mix_part, m_crossed, m_sent)).astype(bf16)
    out_shared = share(1, lambda k: layer_out.at[k])
    turned_rows[...] = jnp.transpose(normed[...])
    sum_first(1)
    m2_rings[1].start()
    close_first(m_rings[0], 0)
    sum_first(0)
    m2_rings[0].start()
    out_shared.forward()
    for d in (1, 2, 3):
        k = turned(x, d)
        copy = remote(packed.at[k], arrived.at[k], psem.at[0, k], psem.at[1, k], "x", k)
        copy.wait_recv()
        waits.append(copy)
    rotation = table[...].reshape(chip, 128)
    cosine = jnp.concatenate([rotation[:, 0:64]] * 4, axis=1)
    sine = jnp.concatenate([rotation[:, 64:128]] * 4, axis=1)

    def side_by_side(lanes):
        return jnp.concatenate([arrived[h, 0:chip, lanes].astype(f32) for h in range(4)], axis=1)

    d_lin = jnp.concatenate(
        [
            rope(side_by_side(slice(0, 64)), cosine, -sine).astype(bf16),
            rope(side_by_side(slice(64, 128)), cosine, -sine).astype(bf16),
            jnp.concatenate(
                [
                    jnp.concatenate([arrived[h, chip:, lanes] for h in range(4)], axis=1)
                    for lanes in (slice(0, 64), slice(64, 128))
                ],
                axis=0,
            ),
        ],
        axis=1,
    )
    sent_all([*d_crossed.values(), *d_sent.values(), shared.right, shared.left, shared.right_on, shared.left_on, *forward])
    partial = d_branch
    lin = [d_lin[0:side], d_lin[side:]]
    for k in range(2):
        partial[k] = dot_nt(lin[k], weights_of(0, 3)).astype(bf16).reshape(4, quarter, width)
    crossed = cross(2, partial.at[1 - c])
    terms[:, :, :, 0 : 3 * wide] = (
        dot_nn(turned_rows[...], d_lin).astype(bf16).reshape(4, 4, width // 16, 3 * wide)
    )
    a_rings = [first_step(s, terms, a_lanes, apart(a_early), apart(a_late), apart(a_carry), 4)[0] for s in range(2)]
    for ring in a_rings:
        ring.start()
    sent = along(2, partial.at[c], crossed)
    for s, me in ((1, z), (0, x)):
        m2_rings[s].middle(add_to(m2_carry, m2_early, m_mine, s, me))
    own = own_tokens[...].astype(f32)
    own_scale = lax.rsqrt(jnp.mean(own * own, axis=-1, keepdims=True) + epsilon)
    own_unit = own * own_scale

    def add_term(s, me):
        def add(h):
            k = turned(me, (1, 3)[h])
            for q in (2 * h, 2 * h + 1):
                mine = terms[k, q, :, 0:a_split] if s == 0 else terms[q, k, :, a_split:]
                a_carry[s, q] = mine + a_early[s, q]

        return add

    for s, me in ((0, z), (1, x)):
        a_rings[s].middle(add_term(s, me))
    d_one = total_of(2, partial.at[c], crossed, sent)
    scaled = d_one * gain_rows[0:1, :]
    input_grad[y] = (
        d_mid[...] + own_scale * (scaled - own_unit * jnp.mean(scaled * own_unit, axis=-1, keepdims=True))
    ).astype(bf16)
    in_shared = share(2, lambda k: input_grad.at[k])
    both = jnp.concatenate(
        [jnp.sum(d_one * own_unit, axis=0, keepdims=True), gain_two_part, jnp.zeros((6, width), f32)], axis=0
    )
    for k in range(16):
        gain_part[k] = both[:, k * 128 : (k + 1) * 128]

    def pass_on(r, src_of, into, axis, me):
        return {
            d: begin(remote(src_of(turned(me, d)), into.at[d - 1], gsem.at[r, 0, d - 1], gsem.at[r, 1, d - 1], axis, turned(me, d)))
            for d in (2, 1, 3)
        }

    moved = pass_on(0, lambda k: gain_part.at[some(k, 4)], gain_z, "shard", z)
    a2_rings = [second_step(s, apart(a_mine), apart(a2_early), apart(a2_late), apart(a2_carry), 6) for s in range(2)]
    for s, me in ((0, z), (1, x)):
        a_rings[s].finish()
        for q in range(4):
            mine = terms[me, q, :, 0:a_split] if s == 0 else terms[q, me, :, a_split:]
            a_mine[s, q] = (
                mine.astype(f32) + a_late[s, 0, q].astype(f32) + a_late[s, 1, q].astype(f32)
            ).astype(bf16)
        a2_rings[s].start()
    for d in (1, 3, 2):
        moved[d].wait_recv()
    gain_part[some(z, 4)] += gain_z[0] + gain_z[1] + gain_z[2]
    moved = pass_on(1, lambda k: gain_part.at[4 * z + k], gain_x, "x", x)

    def second_sum(ring, mine, late, s, me, into, columns):
        ring.finish()
        into[:, columns] = (mine[s][me].astype(f32) + late[s][0].astype(f32) + late[s][1].astype(f32)).astype(bf16)

    for s, me in ((0, x), (1, z)):
        second_sum(m2_rings[s], m_mine, m2_late, s, me, m2_mine, m_lanes[s])
    mine_rows, theirs_rows = some(c, shard), some(1 - c, shard)
    m_last = begin(remote(m2_mine.at[theirs_rows], swapped_m.at[c], outsem.at[0, 0], outsem.at[0, 1], "core", 1 - c))
    swapped_m[c] = m2_mine[mine_rows, :]
    for s, me in ((0, x), (1, z)):
        a2_rings[s].middle(add_to(apart(a2_carry), apart(a2_early), apart(a_mine), s, me))
    for d in (1, 3, 2):
        moved[d].wait_recv()
    gain_y[3] = gain_part[4 * z + x] + gain_x[0] + gain_x[1] + gain_x[2]
    moved = pass_on(2, lambda k: gain_y.at[3], gain_y, "tensor", y)
    in_shared.forward()
    for d in (1, 3, 2):
        moved[d].wait_recv()
    gain_c[0] = (gain_y[0] + gain_y[1]) + (gain_y[2] + gain_y[3])
    between = begin(remote(gain_c.at[0], gain_c.at[1], gsem.at[3, 0, 0], gsem.at[3, 1, 0], "core", 1 - c))
    for s, me in ((0, x), (1, z)):
        second_sum(a2_rings[s], apart(a_mine), apart(a2_late), s, me, a2_mine, a_lanes[s])
    a_last = begin(remote(a2_mine.at[theirs_rows], swapped_a.at[c], outsem.at[1, 0], outsem.at[1, 1], "core", 1 - c))
    swapped_a[c] = a2_mine[mine_rows, :]
    between.wait_recv()
    gain_out[...] = gain_c[0] + gain_c[1]
    a_last.wait_recv()
    m_last.wait_recv()
    out_shared.finish()
    in_shared.finish()
    for copy in waits:
        copy.wait_send()


def backward_pass(
    d_part, mix_part, middle, tokens, cot, gain_rows, weights, low, normed, packed, attended, lse, start, table, mlp_terms
):
    chip, width = normed.shape
    seq = start.shape[1]
    quarter, shard = chip // 8, width // 32
    columns, hidden = weights.shape[3], mlp_terms.shape[3] // 3
    m_split = 3 * hidden // 12 * 7 // 128 * 128
    a_half = columns // 2
    m_parts = (m_split, 3 * hidden - m_split)
    sds = jax.ShapeDtypeStruct
    dma = pltpu.SemaphoreType.DMA
    vmem = pltpu.VMEM

    return pl.pallas_call(
        backward_kernel,
        out_shape=(
            sds((4, quarter, width), bf16),
            sds((4, quarter, width), bf16),
            sds((2, shard, 3 * hidden), bf16),
            sds((2, shard, columns), bf16),
            sds((8, 128), f32),
            *(sds((2, 4, width // 16, n), bf16) for n in m_parts),
        ),
        in_specs=[HBM] * 11 + [VMEM] * 2 + [HBM] * 2,
        out_specs=(VMEM,) * 5 + (HBM,) * 2,
        scratch_shapes=[
            *(vmem(a.shape[1:], a.dtype) for a in (d_part, mix_part)),
            vmem(middle.shape, middle.dtype),
            vmem((quarter, width), bf16),
            vmem((quarter, width), bf16),
            *(vmem(a.shape, a.dtype) for a in (gain_rows, weights, low, normed, packed, attended, table)),
            *[vmem((seq, HEAD_DIM), bf16)] * 3,
            vmem((2, 4, quarter, width), bf16),
            vmem((quarter, width), f32),
            vmem((2, 4, quarter, width), bf16),
            vmem((2, 3, quarter, width), bf16),
            vmem((2, 3, quarter, width), bf16),
            vmem((4, chip, HEAD_DIM), bf16),
            vmem((4, chip, HEAD_DIM), bf16),
            vmem((HEAD_DIM, seq), bf16),
            vmem((seq, HEAD_DIM), f32),
            vmem((seq, HEAD_DIM), f32),
            vmem((4, chip * 3 // 2, 128), bf16),
            vmem((4, chip * 3 // 2, 128), bf16),
            vmem((width, chip), bf16),
            vmem((4, 4, width // 16, columns), bf16),
            *(vmem((4, width // 16, n), bf16) for _ in range(3) for n in m_parts),
            *(vmem((width // 16, n), bf16) for n in m_parts),
            *(vmem((2, width // 16, n), bf16) for n in m_parts),
            *(vmem((width // 16, n), bf16) for n in m_parts),
            vmem((width // 16, 3 * hidden), bf16),
            vmem((2, 4, width // 16, a_half), bf16),
            vmem((2, 2, 4, width // 16, a_half), bf16),
            vmem((2, 4, width // 16, a_half), bf16),
            vmem((2, 4, width // 16, a_half), bf16),
            vmem((2, width // 16, a_half), bf16),
            vmem((2, 2, width // 16, a_half), bf16),
            vmem((2, width // 16, a_half), bf16),
            vmem((width // 16, columns), bf16),
            vmem((16, 8, 128), f32),
            vmem((4, 8, 128), f32),
            vmem((2, 8, 128), f32),
            vmem((3, 8, 128), f32),
            vmem((3, 4, 8, 128), f32),
            dma((3, 2, 4)), dma((3, 2, 3)), dma((3, 2, 4)), dma((2, 4)), dma((2, 3)), dma((2, 4)),
            dma((8, 2, 6)), dma((2, 6)), dma((4, 2, 3)), dma((2, 2)), dma((12,)),
        ],
        compiler_params=pltpu.CompilerParams(
            collective_id=1, has_side_effects=True, vmem_limit_bytes=62 << 20
        ),
    )(
        d_part, mix_part, middle, tokens, cot, gain_rows, weights, low, normed, packed, attended, lse, start, table, mlp_terms
    )


def finish_kernel(
    out_in, grad_in, mlp_in, attn_in, gain_in,
    layer_out, input_grad, gain_one, gain_two, grad_q, grad_k, grad_v, grad_o, grad_gate, grad_up, grad_down,
):
    c = lax.axis_index("core")
    shard, wide = grad_q.shape[0], grad_q.shape[1] // 2
    layer_out[...] = out_in[...].reshape(layer_out.shape)
    input_grad[...] = grad_in[...].reshape(input_grad.shape)
    for k, out in enumerate((gain_one, gain_two)):
        out[...] = jnp.where(c == 0, gain_in[k : k + 1, 0:shard], gain_in[k : k + 1, shard : 2 * shard])
    span = grad_gate.shape[1] // 4
    for e in range(2):
        for k, out in enumerate((grad_q, grad_k, grad_v, grad_o)):
            out[:, e * wide : (e + 1) * wide] = attn_in[e, :, k * wide : (k + 1) * wide].astype(f32)
        for g in range(2):
            lanes = slice((2 * e + g) * span, (2 * e + g + 1) * span)
            for k, out in enumerate((grad_gate, grad_up, grad_down)):
                out[:, lanes] = mlp_in[e, :, (3 * g + k) * span : (3 * g + k + 1) * span].astype(f32)


def finish(layer_out, input_grad, mlp_grads, attn_grads, gains):
    quarters, quarter, width = layer_out.shape
    rows = quarters * quarter
    _, shard, columns = attn_grads.shape
    hidden = mlp_grads.shape[2] // 3
    sds = jax.ShapeDtypeStruct
    narrow, broad = sds((shard, columns // 2), f32), sds((shard, 2 * hidden), f32)
    return pl.pallas_call(
        finish_kernel,
        out_shape=(
            *[sds((rows, width), bf16)] * 2,
            *[sds((1, shard), f32)] * 2,
            *[narrow] * 4,
            *[broad] * 3,
        ),
        compiler_params=pltpu.CompilerParams(vmem_limit_bytes=32 << 20),
    )(layer_out, input_grad, mlp_grads, attn_grads, gains)


def angle_table(positions):
    half = HEAD_DIM // 2
    frequency = rope_base ** (-(jnp.arange(half, dtype=f32) * 2.0) / HEAD_DIM)
    angle = positions.astype(f32)[:, None] * jnp.tile(frequency, 4)[None, :]
    lane = jnp.arange(4 * half)
    sign = jnp.where(lane < 3 * half, -1.0, 1.0)[None, :]
    return jnp.where((lane < 2 * half)[None, :], jnp.cos(angle), jnp.sin(angle) * sign)


def body(
    tokens_in,
    cotangent,
    segments,
    positions,
    norm1_gain,
    q_weight,
    k_weight,
    v_weight,
    o_weight,
    norm2_gain,
    gate_weight,
    up_weight,
    down_weight,
):
    rows, width = tokens_in.shape
    quarter = rows // 4
    (
        full, table, normed_one, packed, low, attended, middle, mixed, d_normed, terms, gain_rows, start, lse,
    ) = forward_pass(
        q_weight, k_weight, v_weight, o_weight.T, gate_weight, up_weight, down_weight.T,
        norm1_gain[None], norm2_gain[None], tokens_in, cotangent, angle_table(positions), segments,
    )
    split = (2, 4, quarter, width)
    *results, _, _ = backward_pass(
        d_normed.reshape(split), mixed.reshape(split), middle, tokens_in, cotangent, gain_rows, full,
        low, normed_one, packed, attended, lse, start, table, terms,
    )
    (
        layer_out, input_grad, gain_one, gain_two, grad_q, grad_k, grad_v, grad_o, grad_gate, grad_up, grad_down,
    ) = finish(*results)
    return (
        layer_out, input_grad, gain_one[0], grad_q, grad_k, grad_v, grad_o.T, gain_two[0], grad_gate, grad_up, grad_down.T,
    )


def solution(mesh):
    apart = Mesh(mesh.devices.reshape(4, 4, 2, 4), ("shard", "x", "core", "tensor"))
    tokens = ("shard", "x", "core")
    placed = (
        P(tokens, None),
        P(tokens, None),
        P("shard", None),
        P(tokens),
        P(tokens),
        P(tokens, "tensor"),
        P(tokens, "tensor"),
        P(tokens, "tensor"),
        P("tensor", tokens),
        P(tokens),
        P(tokens, "tensor"),
        P(tokens, "tensor"),
        P("tensor", tokens),
    )
    return jax.shard_map(
        body,
        mesh=apart,
        in_specs=placed,
        out_specs=(
            P(tokens, None),
            P(tokens, None),
            P(tokens),
            P(tokens, "tensor"),
            P(tokens, "tensor"),
            P(tokens, "tensor"),
            P("tensor", tokens),
            P(tokens),
            P(tokens, "tensor"),
            P(tokens, "tensor"),
            P("tensor", tokens),
        ),
        check_vma=False,
    )
```

```python
import jax
import jax.numpy as jnp
from jax import lax
from jax.experimental import pallas as pl
from jax.experimental.pallas import tpu as pltpu
from jax.sharding import Mesh
from jax.sharding import PartitionSpec as P

HEAD_DIM = 64
BLOCK = 512

epsilon = 1e-05
rope_base = 130000.0
masked_low = -1000000000.0

f32 = jnp.float32
bf16 = jnp.bfloat16
MESH = pl.DeviceIdType.MESH
VMEM = pl.BlockSpec(memory_space=pltpu.VMEM)
HBM = pl.BlockSpec(memory_space=pl.ANY)


def dot_nn(a, b):
    return lax.dot_general(a, b, (((1,), (0,)), ((), ())), preferred_element_type=f32)


def dot_nt(a, b):
    return lax.dot_general(a, b, (((1,), (1,)), ((), ())), preferred_element_type=f32)


def place():
    return tuple(lax.axis_index(a) for a in ("shard", "x", "core", "tensor"))


def turned(index, step):
    return lax.rem(index + step, 4)


def some(index, size):
    return pl.ds(pl.multiple_of(index * size, size), size)


def meet(axes):
    barrier = pltpu.get_barrier_semaphore()
    count = 0
    for axis in axes:
        me = lax.axis_index(axis)
        peers = [1 - me] if axis == "core" else [turned(me, d) for d in (1, 2, 3)]
        for peer in peers:
            pl.semaphore_signal(barrier, inc=1, device_id={axis: peer}, device_id_type=MESH)
            count += 1
    pl.semaphore_wait(barrier, count)


def remote(src, dst, send, recv, axis, index):
    return pltpu.make_async_remote_copy(
        src_ref=src, dst_ref=dst, send_sem=send, recv_sem=recv, device_id={axis: index}, device_id_type=MESH
    )


class Gather:
    def __init__(self, axis, me, block, half, sems, waits):
        self.axis, self.me, self.block, self.half, self.sems, self.waits = axis, me, block, half, sems, waits

    def send(self, ref, slot, step):
        copy = remote(ref, ref, self.sems.at[0, slot], self.sems.at[1, slot], self.axis, turned(self.me, step))
        copy.start()
        self.waits.append(copy)
        return copy

    def start(self):
        mine = self.block(self.me)
        self.right, self.left = self.send(mine, 0, 1), self.send(mine, 1, 3)

    def forward(self):
        self.right.wait_recv()
        self.right_on = self.send(self.half(turned(self.me, 3), 0), 2, 1)
        self.left.wait_recv()
        self.left_on = self.send(self.half(turned(self.me, 1), 1), 3, 3)

    def finish(self):
        self.right_on.wait_recv()
        self.left_on.wait_recv()


class Reduce:
    def __init__(self, axis, me, half, early, late, carried, sems, waits):
        self.axis, self.me, self.half, self.sems, self.waits = axis, me, half, sems, waits
        self.early, self.late, self.carried = early, late, carried

    def send(self, src, dst, slot, step):
        copy = remote(src, dst, self.sems.at[0, slot], self.sems.at[1, slot], self.axis, turned(self.me, step))
        copy.start()
        self.waits.append(copy)
        return copy

    def start(self):
        far, right, left = turned(self.me, 2), turned(self.me, 1), turned(self.me, 3)
        self.far = [
            self.send(self.half(far, 0), self.early(0), 0, 1),
            self.send(self.half(far, 1), self.early(1), 1, 3),
        ]
        self.plain = [
            self.send(self.half(right, 1), self.late(0, 1), 2, 1),
            self.send(self.half(left, 0), self.late(1, 0), 3, 3),
        ]

    def join(self, add):
        for h in range(2):
            self.far[h].wait_recv()
            add(h)

    def pass_on(self):
        self.both = [self.send(self.carried(h), self.late(h, h), 4 + h, step) for h, step in ((0, 1), (1, 3))]

    def middle(self, add):
        self.join(add)
        self.pass_on()

    def finish(self):
        for copy in self.plain + self.both:
            copy.wait_recv()


def rope(vectors, table_cos, table_sin):
    n = vectors.shape[1]
    lane = lax.broadcasted_iota(jnp.int32, vectors.shape, 1)
    other = jnp.where(
        lax.rem(lane, HEAD_DIM) < HEAD_DIM // 2,
        pltpu.roll(vectors, n - HEAD_DIM // 2, 1),
        pltpu.roll(vectors, HEAD_DIM // 2, 1),
    )
    return vectors * table_cos + other * table_sin


def masked(raw, begin, j, i, diagonal):
    key = lax.broadcasted_iota(jnp.int32, raw.shape, 0)
    allowed = key >= begin - j * BLOCK
    if diagonal:
        allowed = allowed & (key <= lax.broadcasted_iota(jnp.int32, raw.shape, 1))
    return jnp.where(allowed, raw, masked_low)


def forward_kernel(
    wq, wk, wv, wo, wg, wu, wd, gain_one, gain_two, tokens, cot, rotary, seg_row,
    full_out, table_out, normed_out, packed_out, low_out, attended_out, middle_out, mixed_out, d_normed_out, terms_out,
    far_z, far_x, plain_z, plain_x, gain_rows, start, lse,
    full, normed, table, low, attended_t, middle, normed_two,
    gains, attn_give, mlp_give, gain_all, chip_tokens, packed, arrived, keys, value_t, scaled_q,
    head_out, low_in, own, other, pair, near,
    mlp_full, cot_held, cot_t, normed_t, both, made_hidden, made, d_held, mixed_held, d_hidden_held,
    local, core_sem, out_sem, made_sem, grad_sem, ring_sem, gain_sem, xsem, lsem, csem, ysem, asem, fsem,
):
    z, x, c, y = place()
    half = wq.shape[1] // 2
    shard = wq.shape[0]
    hidden = wg.shape[1] // 2
    groups = 2
    span = hidden // groups
    chip, width = normed.shape
    waits = []
    meet(("core", "x", "shard", "tensor"))

    at = some(c, shard)
    lane = lax.broadcasted_iota(jnp.int32, (8, 128), 1) // (2 * shard // 2)
    both_gains = jnp.concatenate(
        [gain_one[...].astype(f32), gain_two[...].astype(f32), jnp.zeros((6, shard), f32)], axis=0
    )
    both_gains = jnp.where(lane == c, jnp.concatenate([both_gains, both_gains], axis=1), 0.0)
    gains[...] = jnp.concatenate([both_gains, jnp.zeros((8, 128), f32)], axis=0).astype(bf16)
    for k, w in enumerate((wq, wk, wv, wo)):
        attn_give[:, k * half : (k + 1) * half] = w[:, some(1 - c, half)]
        full[z, x, at, k * half : (k + 1) * half] = w[:, some(c, half)]
    for k, w in enumerate((wg, wu, wd)):
        for g in range(groups):
            lanes = slice((3 * g + k) * span, (3 * g + k + 1) * span)
            mlp_give[:, lanes] = w[:, some((1 - c) * groups + g, span)]
            mlp_full[z, x, at, lanes] = w[:, some(c * groups + g, span)]
    pairs = [(gains, gains, gain_all.at[z, x, c]), (None, attn_give, full.at[z, x, at, :])]
    pairs += [(None, mlp_give, mlp_full.at[z, x, at, :])]
    pairs += [(a, a, b.at[c]) for a, b in ((tokens, chip_tokens), (rotary, table), (cot, cot_held))]
    inside, across = [], []
    for k, (mine, theirs, there) in enumerate(pairs):
        inside.append(pltpu.make_async_copy(mine, there, local.at[k]) if mine is not None else None)
        across.append(remote(theirs, there, core_sem.at[0, k], core_sem.at[1, k], "core", 1 - c))
        across[-1].start()
        if mine is not None:
            inside[-1].start()
    waits += across
    kept = []

    def keep(src, dst):
        kept.append(pltpu.make_async_copy(src, dst, out_sem.at[len(kept)]))
        kept[-1].start()

    def here(ks):
        for k in ks:
            if inside[k] is not None:
                inside[k].wait()
            across[k].wait_recv()

    def spread(src, r, axis, me):
        copies = []
        for d in (1, 2, 3):
            copies.append(remote(src, src, gain_sem.at[0, r, d - 1], gain_sem.at[1, r, d - 1], axis, turned(me, d)))
            copies[-1].start()
        waits.extend(copies)
        return copies

    all_rings = []

    def ring(axis, block, half_of):
        all_rings.append(Gather(axis, x if axis == "x" else z, block, half_of, ring_sem.at[len(all_rings)], waits))
        return all_rings[-1]

    def half_rows(h):
        return pl.ds(h * shard, shard)

    def both_of(p):
        return pl.ds(2 * p, 2)

    def first_along(axis, array, lanes):
        if axis == "x":
            return ring("x", lambda k: array.at[z, k, :, lanes], lambda k, h: array.at[z, k, half_rows(h), lanes])
        return ring("shard", lambda k: array.at[k, x, :, lanes], lambda k, h: array.at[k, x, half_rows(h), lanes])

    def then_along(axis, array, lanes):
        if axis == "x":
            return [
                ring("x", lambda k, p=p: array.at[both_of(p), k, :, lanes], lambda k, h, p=p: array.at[2 * p + h, k, :, lanes])
                for p in range(2)
            ]
        return [
            ring("shard", lambda k, p=p: array.at[k, both_of(p), :, lanes], lambda k, h, p=p: array.at[k, 2 * p + h, :, lanes])
            for p in range(2)
        ]

    qkv_a, qkv_b, out_a = pl.ds(0, 3 * half // 2), pl.ds(3 * half // 2, 3 * half // 2), pl.ds(3 * half, half)
    late_a = 3 * span * 7 // 12 // 128 * 128
    mlp_a1, mlp_b1 = pl.ds(0, 3 * span // 2), pl.ds(3 * span // 2, 3 * span // 2)
    mlp_a2, mlp_b2 = pl.ds(3 * span, late_a), pl.ds(3 * span + late_a, 3 * span - late_a)
    ax, az = first_along("x", full, qkv_a), then_along("shard", full, qkv_a)
    bz, bx = first_along("shard", full, qkv_b), then_along("x", full, qkv_b)
    ox, oz = first_along("x", full, out_a), then_along("shard", full, out_a)
    mx1, mz1 = first_along("x", mlp_full, mlp_a1), then_along("shard", mlp_full, mlp_a1)
    nz1, nx1 = first_along("shard", mlp_full, mlp_b1), then_along("x", mlp_full, mlp_b1)
    mx2, mz2 = first_along("x", mlp_full, mlp_a2), then_along("shard", mlp_full, mlp_a2)
    nz2, nx2 = first_along("shard", mlp_full, mlp_b2), then_along("x", mlp_full, mlp_b2)

    def start_all(rings):
        for one in rings:
            one.start()

    def forward_all(rings):
        for one in rings:
            one.forward()

    def finish_all(rings):
        for one in rings:
            one.finish()

    here((0,))
    gain_x = spread(gain_all.at[z, x], 0, "x", x)
    here((1,))
    start_all((ax, bz))
    here((2,))
    start_all((mx1, nz1))
    for copy in gain_x:
        copy.wait_recv()
    gain_z = spread(gain_all.at[z], 1, "shard", z)
    forward_all((ax, bz))
    ox.start()
    forward_all((mx1, nz1))
    ax.finish()
    start_all(az)
    bz.finish()
    start_all(bx)
    ox.forward()

    for copy in gain_z:
        copy.wait_recv()
    for i in range(16):
        two = (gain_all[i // 4, i % 4, 0] + gain_all[i // 4, i % 4, 1]).astype(f32)
        gain_rows[:, pl.ds(i * 128, 128)] = two[0:8, :]
    here((3, 4))

    def norm(i, unused):
        values = chip_tokens[i // 4, some(lax.rem(i, 4), 64), :].astype(f32)
        scale = lax.rsqrt(jnp.mean(values * values, axis=-1, keepdims=True) + epsilon)
        normed[some(i, 64), :] = ((values * scale) * gain_rows[0:1, :]).astype(bf16)
        return unused

    lax.fori_loop(0, chip // 64, norm, 0)
    keep(normed, normed_out)
    keep(table, table_out)
    row = seg_row[...].astype(f32)
    begins = [jnp.zeros((1, BLOCK), f32)] * 4
    for i in range(4):
        column = jnp.transpose(jnp.broadcast_to(row[:, i * BLOCK : (i + 1) * BLOCK], (128, BLOCK)))[:, 0:1]
        for j in range(i, 4):
            earlier = column < row[:, j * BLOCK : (j + 1) * BLOCK]
            begins[j] = begins[j] + jnp.sum(jnp.where(earlier, 1.0, 0.0), axis=0, keepdims=True)
    for i in range(4):
        start[:, i * BLOCK : (i + 1) * BLOCK] = begins[i].astype(jnp.int32)
    forward_all((az[0], bx[0], az[1], bx[1]))
    start_all((mx2, nz2))
    ox.finish()
    start_all(oz)
    mx1.finish()
    start_all(mz1)
    finish_all(az + bx)

    wide = 4 * HEAD_DIM

    def weights(k):
        return full[:, :, :, k * wide : (k + 1) * wide].reshape(width, wide)

    rotation = table[...].reshape(chip, 128)
    cosine = jnp.concatenate([rotation[:, 0:64]] * 4, axis=1)
    sine = jnp.concatenate([rotation[:, 64:128]] * 4, axis=1)
    queries = rope(dot_nn(normed[...], weights(0)), cosine, sine).astype(bf16)
    turned_keys = rope(dot_nn(normed[...], weights(1)), cosine, sine).astype(bf16)
    values = dot_nn(normed[...], weights(2)).astype(bf16)
    for h in range(4):
        lanes = slice(h * HEAD_DIM, (h + 1) * HEAD_DIM)
        packed[h, 0:chip, :] = jnp.concatenate([queries[:, lanes], turned_keys[:, lanes]], axis=1)
        packed[h, chip:, :] = jnp.concatenate(
            [values[0 : chip // 2, lanes], values[chip // 2 :, lanes]], axis=1
        )
    sent = []
    for d in (2, 1, 3):
        k = turned(x, d)
        sent.append(remote(packed.at[k], arrived.at[x], xsem.at[0, d - 1], xsem.at[1, d - 1], "x", k))
        sent[-1].start()
    waits += sent
    forward_all((mx2, nz2))
    forward_all(oz)
    nz1.finish()
    start_all(nx1)
    arrived[x] = packed[x]
    for copy in sent:
        copy.wait_recv()
    for k in range(4):
        rows = slice(k * chip, (k + 1) * chip)
        scaled_q[rows, :] = arrived[k, 0:chip, 0:64] * HEAD_DIM ** (-0.5)
        keys[rows, :] = arrived[k, 0:chip, 64:128]
        block = jnp.concatenate([arrived[k, chip:, 0:64], arrived[k, chip:, 64:128]], axis=0)
        value_t[:, rows] = jnp.transpose(block)
    keep(arrived, packed_out)

    for i in range(4):
        if i == 2:
            mz1[0].forward()
        if i == 3:
            mx2.finish()
            start_all(mz2)
        at = slice(i * BLOCK, (i + 1) * BLOCK)
        begin = start[:, at]
        mine = scaled_q[at, :]

        def step(j, state, diagonal=False):
            peak, total, summed = state
            scores = masked(dot_nt(keys[some(j, BLOCK), :], mine), begin, j, i, diagonal)
            new = jnp.maximum(peak, jnp.max(scores, axis=0, keepdims=True))
            weight = jnp.exp(scores - new)
            factor = jnp.exp(peak - new)
            total = total * factor + jnp.sum(weight, axis=0, keepdims=True)
            summed = summed * factor + dot_nn(value_t[:, some(j, BLOCK)], weight.astype(bf16))
            return (new, total, summed)

        state = (
            jnp.full((1, BLOCK), masked_low, f32),
            jnp.zeros((1, BLOCK), f32),
            jnp.zeros((HEAD_DIM, BLOCK), f32),
        )
        state = step(i, state, True)
        peak, total, summed = lax.fori_loop(0, i, step, state) if i else state
        attended = summed / total
        attended_t[:, at] = attended
        lse[:, at] = peak + jnp.log(total)
        head_out[i] = jnp.transpose(attended).astype(bf16)

        @pl.when(x != i)
        def send(i=i):
            remote(head_out.at[i], low_in.at[x], lsem.at[0, i], lsem.at[1, x], "x", i).start()

    nz2.finish()
    start_all(nx2)
    mz1[1].forward()
    nx1[0].forward()
    low_in[x] = head_out[x]
    for d in (1, 2, 3):
        k = turned(x, d)
        copy = remote(head_out.at[k], low_in.at[k], lsem.at[0, k], lsem.at[1, k], "x", k)
        copy.wait_recv()
        waits.append(copy)
    low[...] = jnp.concatenate([low_in[h] for h in range(4)], axis=1)
    finish_all(oz)
    keep(full, full_out)
    keep(low, low_out)
    keep(attended_t, attended_out)

    side, quarter = chip // 2, chip // 8
    out_weights = weights(3)
    other[...] = dot_nt(low[some(1 - c, side), :], out_weights).astype(bf16).reshape(other.shape)
    crossed = {}
    for d in (2, 1, 3, 0):
        k = turned(y, d)
        crossed[d] = remote(other.at[k], pair.at[k], csem.at[0, d], csem.at[1, d], "core", 1 - c)
        crossed[d].start()
    own[...] = dot_nt(low[some(c, side), :], out_weights).reshape(own.shape)
    along = {}
    for d in (2, 1, 3):
        k = turned(y, d)
        crossed[d].wait_recv()
        crossed[d].wait_send()
        other[k] = (own[k] + pair[k].astype(f32)).astype(bf16)
        along[d] = remote(other.at[k], near.at[d - 1], ysem.at[0, d - 1], ysem.at[1, d - 1], "tensor", k)
        along[d].start()
    crossed[0].wait_recv()
    crossed[0].wait_send()
    here((5,))
    nx1[1].forward()
    cot_t[...] = jnp.transpose(cot_held[...].reshape(chip, width))
    mz2[0].forward()
    total = own[y] + pair[y].astype(f32)
    for d in (1, 3, 2):
        along[d].wait_recv()
        total = total + near[d - 1].astype(f32)
    waits += [*along.values()]
    mid = chip_tokens[c, some(y, quarter), :].astype(f32) + total
    middle[...] = mid
    keep(middle, middle_out)
    scale = lax.rsqrt(jnp.mean(mid * mid, axis=-1, keepdims=True) + epsilon)
    normed_two[c, y] = ((mid * scale) * gain_rows[1:2, :]).astype(bf16)
    share = Gather(
        "tensor", y, lambda k: normed_two.at[c, k], lambda k, h: normed_two.at[c, k, pl.ds(h * quarter // 2, quarter // 2)],
        asem, waits,
    )
    forward = []

    def forward_on(k):
        slot = normed_two.at[c, k]
        d = len(forward)
        forward.append(remote(slot, slot, fsem.at[0, d], fsem.at[1, d], "core", 1 - c))
        forward[-1].start()

    share.start()
    forward_on(y)
    finish_all(nx1 + mz1)

    def group(g, k):
        return mlp_full[:, :, :, (3 * g + k) * span : (3 * g + k + 1) * span].reshape(width, span)

    chip_cot = cot_held[...].reshape(chip, width)
    share.forward()
    forward_on(turned(y, 3))
    forward_on(turned(y, 1))
    mz2[1].forward()
    nx2[0].forward()
    d_hidden_held[...] = dot_nn(chip_cot, group(0, 2))
    share.finish()
    forward_on(turned(y, 2))
    nx2[1].forward()
    for copy in forward:
        copy.wait_recv()
    waits += forward

    cut = far_z.shape[2]
    early_rings = [
        Reduce(
            "shard", z, lambda k, h: terms_out.at[k, both_of(h), :, pl.ds(0, cut)], lambda h: far_z.at[both_of(h)],
            lambda e, h: plain_z.at[e], None, grad_sem.at[0], waits,
        ),
        Reduce(
            "x", x, lambda k, h: terms_out.at[both_of(h), k, :, pl.ds(cut, cut)], lambda h: far_x.at[both_of(h)],
            lambda e, h: plain_x.at[e], None, grad_sem.at[1], waits,
        ),
    ]
    rows_two = normed_two[...].reshape(chip, width)
    normed_t[...] = jnp.transpose(rows_two)
    stores = {}
    for g in range(groups):
        if g == 1:
            finish_all(mz2 + nx2)
        gate = dot_nn(rows_two, group(g, 0))
        upper = dot_nn(rows_two, group(g, 1))
        d_hidden = dot_nn(chip_cot, group(g, 2)) if g else d_hidden_held[...]
        sigmoid = 1.0 / (1.0 + jnp.exp(-gate))
        silu = gate * sigmoid
        made_hidden[g] = (silu * upper).astype(bf16)
        both[g, :, 0:span] = (d_hidden * upper * (sigmoid * (1.0 + gate * (1.0 - sigmoid)))).astype(bf16)
        both[g, :, span : 2 * span] = (d_hidden * silu).astype(bf16)
        for k, (left, right) in enumerate(
            ((normed_t, both.at[g, :, 0:span]), (normed_t, both.at[g, :, span : 2 * span]), (cot_t, made_hidden.at[g]))
        ):
            for q in range(4):
                term = dot_nn(left[q * (width // 4) : (q + 1) * (width // 4), :], right[...])
                made[k, q] = term.astype(bf16).reshape(made.shape[2:])
            stores[g, k] = pltpu.make_async_copy(
                made.at[k], terms_out.at[:, :, :, pl.ds((3 * g + k) * span, span)], made_sem.at[g, k]
            )
            stores[g, k].start()
        if g == 0:
            for k in range(3):
                stores[g, k].wait()
            for ring in early_rings:
                ring.start()
    for held, out, left, first, n in ((d_held, d_normed_out, both, 0, 2), (mixed_held, mixed_out, made_hidden, 2, 1)):
        for t in range(4):
            lanes = slice(t * (width // 4), (t + 1) * (width // 4))
            term = [
                dot_nt(
                    left[g],
                    mlp_full[t, :, :, (3 * g + first) * span : (3 * g + first + n) * span].reshape(width // 4, n * span),
                )
                for g in range(groups)
            ]
            held[:, lanes] = (term[0] + term[1]).astype(bf16)
        keep(held, out)
    for k in range(3):
        stores[groups - 1, k].wait()
    for ring in early_rings:
        for copy in ring.far + ring.plain:
            copy.wait_recv()
    for copy in kept:
        copy.wait()
    for copy in waits:
        copy.wait_send()


def forward_pass(wq, wk, wv, wo, wg, wu, wd, gain_one, gain_two, tokens, cot, rotary, seg_row):
    rows, width = tokens.shape
    chip, quarter, seq = 2 * rows, rows // 4, seg_row.shape[1]
    columns, hidden = 2 * wq.shape[1], wg.shape[1] // 2
    sds = jax.ShapeDtypeStruct
    dma = pltpu.SemaphoreType.DMA
    vmem = pltpu.VMEM
    kept = (
        ((4, 4, width // 16, columns), bf16),
        ((chip, width), bf16),
        ((2, rows, 128), f32),
        ((chip, 4 * HEAD_DIM), bf16),
        ((HEAD_DIM, seq), f32),
        ((quarter, width), f32),
        ((2, 4, quarter, width), bf16),
    )
    full, normed, table, low, attended, middle, _ = (sds(*a) for a in kept)
    span = hidden // 2
    packed = (4, chip * 3 // 2, 128)
    return pl.pallas_call(
        forward_kernel,
        out_shape=(
            full,
            table,
            normed,
            sds(packed, bf16),
            low,
            attended,
            middle,
            sds((chip, width), bf16),
            sds((chip, width), bf16),
            sds((4, 4, width // 16, 3 * hidden), bf16),
            *[sds((4, width // 16, 3 * span // 2), bf16)] * 2,
            *[sds((2, 2, width // 16, 3 * span // 2), bf16)] * 2,
            sds((8, width), f32),
            sds((1, seq), jnp.int32),
            sds((1, seq), f32),
        ),
        in_specs=[VMEM] * 9 + [HBM] * 3 + [VMEM],
        out_specs=(HBM,) * 14 + (VMEM,) * 3,
        scratch_shapes=[
            *(vmem(*a) for a in kept),
            vmem((16, 128), bf16),
            vmem((width // 32, columns), bf16),
            vmem((width // 32, 3 * hidden), bf16),
            vmem((4, 4, 2, 16, 128), bf16),
            vmem((2, rows, width), bf16),
            vmem(packed, bf16),
            vmem(packed, bf16),
            vmem((seq, HEAD_DIM), bf16),
            vmem((HEAD_DIM, seq), bf16),
            vmem((seq, HEAD_DIM), bf16),
            vmem((4, chip, HEAD_DIM), bf16),
            vmem((4, chip, HEAD_DIM), bf16),
            vmem((4, quarter, width), f32),
            vmem((4, quarter, width), bf16),
            vmem((4, quarter, width), bf16),
            vmem((3, quarter, width), bf16),
            vmem((4, 4, width // 16, 3 * hidden), bf16),
            vmem((2, rows, width), bf16),
            vmem((width, chip), bf16),
            vmem((width, chip), bf16),
            vmem((2, chip, 2 * span), bf16),
            vmem((2, chip, span), bf16),
            vmem((3, 4, 4, width // 16, span), bf16),
            vmem((chip, width), bf16),
            vmem((chip, width), bf16),
            vmem((chip, span), f32),
            dma((6,)), dma((2, 6)), dma((9,)), dma((2, 3)), dma((2, 2, 6)), dma((21, 2, 4)), dma((2, 2, 3)), dma((2, 3)), dma((2, 4)),
            dma((2, 4)), dma((2, 3)), dma((2, 4)), dma((2, 4)),
        ],
        compiler_params=pltpu.CompilerParams(
            collective_id=0, has_side_effects=True, vmem_limit_bytes=62 << 20
        ),
    )(wq, wk, wv, wo, wg, wu, wd, gain_one, gain_two, tokens, cot, rotary, seg_row)


def backward_kernel(
    d_part_in, mix_part_in, middle_in, tokens_in, cot_in, gain_rows_in, weights_in, low_in, normed_in, packed_in, attended_in,
    lse, start, table_in, mlp_terms, far_z, far_x, plain_z, plain_x,
    layer_out, input_grad, swapped_m, swapped_a, gain_out, landed_z, landed_x,
    d_part, mix_part, middle, own_tokens, own_cot, gain_rows, weights, low, normed, qkv_packed, attended, table,
    queries, keys, values,
    d_branch, d_mid, pair, half_sum, near, heads, head_in, key_t, d_key, d_value, packed, arrived,
    turned_rows, terms, m_early_z, m_early_x, m_carry_z, m_carry_x, m_mine_z, m_mine_x,
    m2_early_z, m2_early_x, m2_late_z, m2_late_x, m2_carry_z, m2_carry_x, m2_mine,
    a_early, a_late, a_carry, a_mine, a2_in, o_early, o_late, o_carry, o_mine, o2_in, a2_mine,
    gain_part, gain_y, gain_c, gain_x, gain_z,
    csem, ysem, asem, fsem, hsem, psem, rsem, local, gsem, outsem, in_sem, dsem,
):
    z, x, c, y = place()
    quarter = middle.shape[0]
    mine_at = some(y, quarter)
    taken = {}
    for k, (name, src, dst) in enumerate(
        (
            ("d_part", d_part_in.at[c], d_part),
            ("middle", middle_in, middle),
            ("gain_rows", gain_rows_in, gain_rows),
            ("own_cot", cot_in.at[mine_at, :], own_cot),
            ("mix_part", mix_part_in.at[c], mix_part),
            ("packed", packed_in, qkv_packed),
            ("weights", weights_in, weights),
            ("low", low_in, low),
            ("attended", attended_in, attended),
            ("normed", normed_in, normed),
            ("table", table_in, table),
            ("own_tokens", tokens_in.at[mine_at, :], own_tokens),
        )
    ):
        taken[name] = pltpu.make_async_copy(src, dst, in_sem.at[k])
        taken[name].start()

    def take(*names):
        for name in names:
            taken[name].wait()

    meet(("core", "x", "tensor", "shard"))
    chip, width = normed.shape
    side = chip // 2
    wide = 4 * HEAD_DIM
    shard = width // 32
    a_split = a_mine.shape[3]
    cut = far_z.shape[2]
    m_span = mlp_terms.shape[3] // 2
    late_cut = m_mine_z.shape[2] - cut
    far, plain = (far_z, far_x), (plain_z, plain_x)
    landed, m_early, m_carry, m_mine = (landed_z, landed_x), (m_early_z, m_early_x), (m_carry_z, m_carry_x), (m_mine_z, m_mine_x)
    m2_early, m2_late, m2_carry = (m2_early_z, m2_early_x), (m2_late_z, m2_late_x), (m2_carry_z, m2_carry_x)
    e_lanes = (pl.ds(0, cut), pl.ds(cut, cut))
    l_lanes = (pl.ds(m_span, late_cut), pl.ds(m_span + late_cut, m_span - late_cut))
    held_e = pl.ds(0, cut)
    held_l = (pl.ds(cut, late_cut), pl.ds(cut, m_span - late_cut))
    o_split = o_mine.shape[3]
    a_lanes = (pl.ds(0, a_split), pl.ds(a_split, a_split))
    o_lanes = (pl.ds(2 * a_split, o_split), pl.ds(2 * a_split + o_split, o_split))
    waits = []

    def begin(copy):
        copy.start()
        waits.append(copy)
        return copy

    def sent_all(copies):
        for copy in copies:
            copy.wait_send()
        waits[:] = [w for w in waits if not any(w is copy for copy in copies)]

    def cross(r, part):
        return {
            d: begin(remote(part.at[turned(y, d)], pair.at[r % 2, turned(y, d)], csem.at[r, 0, d], csem.at[r, 1, d], "core", 1 - c))
            for d in (2, 1, 3, 0)
        }

    def along(r, part, crossed):
        sent = {}
        for d in (2, 1, 3):
            k = turned(y, d)
            crossed[d].wait_recv()
            half_sum[r % 2, d - 1] = part[k] + pair[r % 2, k]
            sent[d] = begin(remote(half_sum.at[r % 2, d - 1], near.at[r % 2, d - 1], ysem.at[r, 0, d - 1], ysem.at[r, 1, d - 1], "tensor", k))
        return sent

    def total_of(r, part, crossed, sent):
        crossed[0].wait_recv()
        total = part[y].astype(f32) + pair[r % 2, y].astype(f32)
        for d in (1, 3, 2):
            sent[d].wait_recv()
            total = total + near[r % 2, d - 1].astype(f32)
        return total

    def share(r, slot):
        cut = quarter // 2
        ring = Gather("tensor", y, slot, lambda k, h: slot(k).at[pl.ds(h * cut, cut)], asem.at[r], waits)
        ring.start()
        return ring

    def two(h):
        return pl.ds(2 * h, 2)

    def rows(h):
        return pl.ds(h * shard, shard)

    def apart(ref):
        return (ref.at[0], ref.at[1])

    def term_of(s, k, q, lanes):
        return terms[k, q, :, lanes[s]] if s == 0 else terms[q, k, :, lanes[s]]

    def join_terms(s, lanes, carry, early):
        def add(h):
            k = turned((z, x)[s], (1, 3)[h])
            for q in (2 * h, 2 * h + 1):
                carry[s, q] = term_of(s, k, q, lanes) + early[s, q]

        return add

    def sum_terms(ring, s, lanes, mine, late):
        ring.finish()
        for q in range(4):
            mine[s, q] = (
                term_of(s, (z, x)[s], q, lanes).astype(f32) + late[s, 0, q].astype(f32) + late[s, 1, q].astype(f32)
            ).astype(bf16)

    def direct(r, s, mine, into):
        axis, me = (("x", x), ("shard", z))[s]
        return [
            begin(remote(mine.at[s, turned(me, d)], into.at[s, d - 1], dsem.at[r, s, 0, d - 1], dsem.at[r, s, 1, d - 1], axis, turned(me, d)))
            for d in (2, 1, 3)
        ]

    def direct_sum(copies, s, mine, into, lanes):
        for copy in copies:
            copy.wait_recv()
        a2_mine[:, lanes[s]] = (
            (mine[s, (x, z)[s]].astype(f32) + into[s, 0].astype(f32))
            + (into[s, 1].astype(f32) + into[s, 2].astype(f32))
        ).astype(bf16)

    def first_step(s, source, split, early, late, carry, r):
        axis, me = (("shard", z), ("x", x))[s]
        columns = split[s]

        def half(k, h):
            return source.at[k, two(h), :, columns] if s == 0 else source.at[two(h), k, :, columns]

        return Reduce(
            axis, me, half, lambda h: early[s].at[two(h)], lambda e, h: late[s].at[e, two(h)],
            lambda h: carry[s].at[two(h)], rsem.at[r + s], waits,
        ), half

    def second_step(s, mine, early, late, carry, r):
        axis, me = (("x", x), ("shard", z))[s]
        return Reduce(
            axis, me, lambda k, h: mine[s].at[k, rows(h)], lambda h: early[s].at[rows(h)],
            lambda e, h: late[s].at[e, rows(h)], lambda h: carry[s].at[rows(h)], rsem.at[r + s], waits,
        )

    def group_ring(s, source_lanes, held, r):
        axis, me = (("shard", z), ("x", x))[s]

        def half(k, h):
            return mlp_terms.at[k, two(h), :, source_lanes] if s == 0 else mlp_terms.at[two(h), k, :, source_lanes]

        return Reduce(
            axis, me, half, lambda h: m_early[s].at[two(h), :, held], lambda e, h: landed[s].at[e, two(h), :, held],
            lambda h: m_carry[s].at[two(h), :, held], rsem.at[r + s], waits,
        )

    e_rings = [group_ring(s, e_lanes[s], held_e, 8) for s in range(2)]
    m_rings = [group_ring(s, l_lanes[s], held_l[s], 0) for s in range(2)]
    loads = {}

    def load(src, dst, s, k):
        loads[s, k] = pltpu.make_async_copy(src, dst, local.at[s, k])
        loads[s, k].start()

    d_crossed = cross(0, d_part_in.at[1 - c])
    for s, me in ((0, z), (1, x)):
        m_rings[s].start()
        for n, (rings, held) in enumerate(((e_rings, held_e), (m_rings, held_l[s]))):
            for h, k in ((0, turned(me, 1)), (1, turned(me, 3))):
                load(rings[s].half(k, h), m_carry[s].at[two(h), :, held], s, 4 * n + h)
                load(rings[s].half(me, h), m_mine[s].at[two(h), :, held], s, 4 * n + 2 + h)
        load(far[s], m_early[s].at[:, :, held_e], s, 8)
    m_crossed = cross(1, mix_part_in.at[1 - c])
    take("d_part", "mix_part")
    d_sent = along(0, d_part, d_crossed)
    take("middle", "gain_rows", "own_cot", "packed")
    mid = middle[...]
    scale = lax.rsqrt(jnp.mean(mid * mid, axis=-1, keepdims=True) + epsilon)
    unit = mid * scale
    for k in range(4):
        at = slice(k * chip, (k + 1) * chip)
        queries[at, :] = qkv_packed[k, 0:chip, 0:64] * HEAD_DIM ** (-0.5)
        block = qkv_packed[k, 0:chip, 64:128]
        keys[at, :] = block
        key_t[:, at] = jnp.transpose(block)
        values[at, :] = jnp.concatenate([qkv_packed[k, chip:, 0:64], qkv_packed[k, chip:, 64:128]], axis=0)
    d_key[...] = jnp.zeros_like(d_key)
    d_value[...] = jnp.zeros_like(d_value)
    def add_far(ring, s):
        def add(h):
            loads[s, 4 + h].wait()
            for q in (2 * h, 2 * h + 1):
                m_carry[s][q, :, held_l[s]] = m_carry[s][q, :, held_l[s]] + m_early[s][q, :, held_l[s]]

        ring.join(add)

    for s in range(2):
        for k in (0, 1, 8):
            loads[s, k].wait()
        for q in range(4):
            m_carry[s][q, :, held_e] = m_carry[s][q, :, held_e] + m_early[s][q, :, held_e]
        e_rings[s].pass_on()
    add_far(m_rings[1], 1)
    d_two = total_of(0, d_part, d_crossed, d_sent)
    gain_two_part = jnp.sum(d_two * unit, axis=0, keepdims=True)
    scaled = d_two * gain_rows[1:2, :]
    d_middle = own_cot[...].astype(f32) + scale * (
        scaled - unit * jnp.mean(scaled * unit, axis=-1, keepdims=True)
    )
    d_mid[...] = d_middle
    d_branch[c, y] = d_middle.astype(bf16)
    shared = share(0, lambda k: d_branch.at[c, k])
    forward = []

    def forward_on(k):
        slot, d = d_branch.at[c, k], len(forward)
        forward.append(begin(remote(slot, slot, fsem.at[0, d], fsem.at[1, d], "core", 1 - c)))

    forward_on(y)
    add_far(m_rings[0], 0)
    m_rings[0].pass_on()
    shared.forward()
    forward_on(turned(y, 3))
    forward_on(turned(y, 1))
    m_sent = along(1, mix_part, m_crossed)
    shared.finish()
    forward_on(turned(y, 2))
    for copy in forward:
        copy.wait_recv()
    branch = d_branch[...].reshape(chip, width)
    take("weights", "low", "attended", "normed", "table", "own_tokens")

    def weights_of(k, n):
        return weights[:, :, :, k * wide : (k + n) * wide].reshape(width, n * wide)

    d_heads = dot_nn(branch, weights_of(3, 1)).astype(bf16)
    for h in range(4):
        heads[h] = d_heads[:, h * HEAD_DIM : (h + 1) * HEAD_DIM]
    head_sent = {}
    for d in (2, 1, 3):
        k = turned(x, d)
        head_sent[d] = begin(remote(heads.at[k], head_in.at[x], hsem.at[0, d - 1], hsem.at[1, d - 1], "x", k))
    head_in[x] = heads[x]
    m_rings[1].pass_on()
    turned_rows[...] = jnp.transpose(branch)
    terms[:, :, :, 3 * wide : 4 * wide] = (
        dot_nn(turned_rows[...], low[...]).astype(bf16).reshape(4, 4, width // 16, wide)
    )
    o_rings = [first_step(s, terms, o_lanes, apart(o_early), apart(o_late), apart(o_carry), 6)[0] for s in range(2)]
    for ring in o_rings:
        ring.start()
    for d in (1, 3, 2):
        head_sent[d].wait_recv()


    for i in (3, 2, 1, 0):
        at = slice(i * BLOCK, (i + 1) * BLOCK)
        mine, d_out = queries[at, :], head_in[i]
        center = jnp.sum(jnp.transpose(d_out.astype(f32)) * attended[:, at], axis=0, keepdims=True)
        peak, first = lse[:, at], start[:, at]

        def step(j, d_query, diagonal=False):
            key_at = some(j, BLOCK)
            scores = masked(dot_nt(keys[key_at, :], mine), first, j, i, diagonal)
            weight = jnp.exp(scores - peak)
            d_prob = dot_nt(values[key_at, :], d_out)
            d_raw = (weight * (d_prob - center)).astype(bf16)
            d_key[key_at, :] += dot_nn(d_raw, mine)
            d_value[key_at, :] += dot_nn(weight.astype(bf16), d_out)
            return d_query + dot_nn(key_t[:, key_at], d_raw)

        d_query = step(i, jnp.zeros((HEAD_DIM, BLOCK), f32), True)
        d_query = lax.fori_loop(0, i, step, d_query) if i else d_query
        packed[i, 0:chip, :] = jnp.concatenate(
            [jnp.transpose(d_query * HEAD_DIM ** (-0.5)).astype(bf16), d_key[at, :].astype(bf16)], axis=1
        )
        d_rows = d_value[at, :].astype(bf16)
        packed[i, chip:, :] = jnp.concatenate([d_rows[0:side], d_rows[side:]], axis=1)

        @pl.when(x != i)
        def send(i=i):
            remote(packed.at[i], arrived.at[x], psem.at[0, i], psem.at[1, x], "x", i).start()

    arrived[x] = packed[x]

    def close_first(s):
        m_rings[s].finish()
        for copy in e_rings[s].both:
            copy.wait_recv()
        sent_all(m_rings[s].both + e_rings[s].both)
        for e, into in enumerate((m_carry, m_early)):
            load(landed[s].at[e, :, :, held_l[s]], into[s].at[:, :, held_l[s]], s, 9 + 3 * e)
            load(landed[s].at[e, two(e), :, held_e], into[s].at[two(e), :, held_e], s, 10 + 3 * e)
            load(plain[s].at[e], into[s].at[two(1 - e), :, held_e], s, 11 + 3 * e)

    def sum_first(s):
        for k in (2, 3, 6, 7, 9, 10, 11, 12, 13, 14):
            loads[s, k].wait()
        for q in range(4):
            m_mine[s][q] = (
                m_mine[s][q].astype(f32) + m_carry[s][q].astype(f32) + m_early[s][q].astype(f32)
            ).astype(bf16)

    def add_to(carry, early, mine, s, me):
        def add(h):
            at = slice(h * shard, (h + 1) * shard)
            k = turned(me, (1, 3)[h])
            carry[s][at, :] = mine[s][k, at, :] + early[s][at, :]

        return add

    m2_rings = [second_step(s, m_mine, m2_early, m2_late, m2_carry, 2) for s in range(2)]
    close_first(1)
    layer_out[y] = (mid + total_of(1, mix_part, m_crossed, m_sent)).astype(bf16)
    out_shared = share(1, lambda k: layer_out.at[k])
    turned_rows[...] = jnp.transpose(normed[...])
    for s in range(2):
        o_rings[s].middle(join_terms(s, o_lanes, o_carry, o_early))
    sum_first(1)
    m2_rings[1].start()
    close_first(0)
    sum_first(0)
    m2_rings[0].start()
    out_shared.forward()
    for d in (1, 2, 3):
        k = turned(x, d)
        copy = remote(packed.at[k], arrived.at[k], psem.at[0, k], psem.at[1, k], "x", k)
        copy.wait_recv()
        waits.append(copy)
    rotation = table[...].reshape(chip, 128)
    cosine = jnp.concatenate([rotation[:, 0:64]] * 4, axis=1)
    sine = jnp.concatenate([rotation[:, 64:128]] * 4, axis=1)

    def side_by_side(lanes):
        return jnp.concatenate([arrived[h, 0:chip, lanes].astype(f32) for h in range(4)], axis=1)

    d_lin = jnp.concatenate(
        [
            rope(side_by_side(slice(0, 64)), cosine, -sine).astype(bf16),
            rope(side_by_side(slice(64, 128)), cosine, -sine).astype(bf16),
            jnp.concatenate(
                [
                    jnp.concatenate([arrived[h, chip:, lanes] for h in range(4)], axis=1)
                    for lanes in (slice(0, 64), slice(64, 128))
                ],
                axis=0,
            ),
        ],
        axis=1,
    )
    terms[:, :, :, 0 : 3 * wide] = (
        dot_nn(turned_rows[...], d_lin).astype(bf16).reshape(4, 4, width // 16, 3 * wide)
    )
    a_rings = [first_step(s, terms, a_lanes, apart(a_early), apart(a_late), apart(a_carry), 4)[0] for s in range(2)]
    for ring in a_rings:
        ring.start()
    sent_all([*d_crossed.values(), *d_sent.values(), shared.right, shared.left, shared.right_on, shared.left_on, *forward])
    partial = d_branch
    lin = [d_lin[0:side], d_lin[side:]]
    gain_one_part = jnp.zeros((1, width), f32)
    for k in range(2):
        term = dot_nt(lin[k], weights_of(0, 3))
        partial[k] = term.astype(bf16).reshape(4, quarter, width)
        gain_one_part = gain_one_part + jnp.sum(
            term * normed[k * side : (k + 1) * side, :].astype(f32), axis=0, keepdims=True
        )
    crossed = cross(2, partial.at[1 - c])
    sent = along(2, partial.at[c], crossed)
    for s, me in ((1, z), (0, x)):
        m2_rings[s].middle(add_to(m2_carry, m2_early, m_mine, s, me))
    both = jnp.concatenate([gain_one_part / gain_rows[0:1, :], gain_two_part, jnp.zeros((6, width), f32)], axis=0)
    for k in range(16):
        gain_part[k] = both[:, k * 128 : (k + 1) * 128]

    def pass_on(r, src_of, into, axis, me):
        return {
            d: begin(remote(src_of(turned(me, d)), into.at[d - 1], gsem.at[r, 0, d - 1], gsem.at[r, 1, d - 1], axis, turned(me, d)))
            for d in (2, 1, 3)
        }

    moved = pass_on(0, lambda k: gain_part.at[some(k, 4)], gain_z, "shard", z)
    o_sent = []
    for s in range(2):
        sum_terms(o_rings[s], s, o_lanes, o_mine, o_late)
        o_sent.append(direct(1, s, o_mine, o2_in))
    own = own_tokens[...].astype(f32)
    own_scale = lax.rsqrt(jnp.mean(own * own, axis=-1, keepdims=True) + epsilon)
    own_unit = own * own_scale

    for s in range(2):
        a_rings[s].middle(join_terms(s, a_lanes, a_carry, a_early))
    for d in (1, 3, 2):
        moved[d].wait_recv()
    gain_part[some(z, 4)] += gain_z[0] + gain_z[1] + gain_z[2]
    moved = pass_on(1, lambda k: gain_part.at[4 * z + k], gain_x, "x", x)

    d_one = total_of(2, partial.at[c], crossed, sent)
    scaled = d_one * gain_rows[0:1, :]
    input_grad[y] = (
        d_mid[...] + own_scale * (scaled - own_unit * jnp.mean(scaled * own_unit, axis=-1, keepdims=True))
    ).astype(bf16)
    in_shared = share(2, lambda k: input_grad.at[k])
    a_sent = []
    for s in range(2):
        sum_terms(a_rings[s], s, a_lanes, a_mine, a_late)
        a_sent.append(direct(0, s, a_mine, a2_in))

    for s, me in ((0, x), (1, z)):
        m2_rings[s].finish()
        for held, lanes in ((held_e, e_lanes[s]), (held_l[s], l_lanes[s])):
            m2_mine[:, lanes] = (
                m_mine[s][me, :, held].astype(f32)
                + m2_late[s][0, :, held].astype(f32) + m2_late[s][1, :, held].astype(f32)
            ).astype(bf16)
    mine_rows, theirs_rows = some(c, shard), some(1 - c, shard)
    m_last = begin(remote(m2_mine.at[theirs_rows], swapped_m.at[c], outsem.at[0, 0], outsem.at[0, 1], "core", 1 - c))
    swapped_m[c] = m2_mine[mine_rows, :]
    for d in (1, 3, 2):
        moved[d].wait_recv()
    gain_y[3] = gain_part[4 * z + x] + gain_x[0] + gain_x[1] + gain_x[2]
    moved = pass_on(2, lambda k: gain_y.at[3], gain_y, "tensor", y)
    in_shared.forward()
    for d in (1, 3, 2):
        moved[d].wait_recv()
    gain_c[0] = (gain_y[0] + gain_y[1]) + (gain_y[2] + gain_y[3])
    between = begin(remote(gain_c.at[0], gain_c.at[1], gsem.at[3, 0, 0], gsem.at[3, 1, 0], "core", 1 - c))
    for s in range(2):
        direct_sum(o_sent[s], s, o_mine, o2_in, o_lanes)
    for s in range(2):
        direct_sum(a_sent[s], s, a_mine, a2_in, a_lanes)
    a_last = begin(remote(a2_mine.at[theirs_rows], swapped_a.at[c], outsem.at[1, 0], outsem.at[1, 1], "core", 1 - c))
    swapped_a[c] = a2_mine[mine_rows, :]
    between.wait_recv()
    gain_out[...] = gain_c[0] + gain_c[1]
    a_last.wait_recv()
    m_last.wait_recv()
    out_shared.finish()
    in_shared.finish()
    for copy in waits:
        copy.wait_send()


def backward_pass(
    d_part, mix_part, middle, tokens, cot, gain_rows, weights, low, normed, packed, attended, lse, start, table, mlp_terms, *early
):
    chip, width = normed.shape
    seq = start.shape[1]
    quarter, shard = chip // 8, width // 32
    columns, hidden = weights.shape[3], mlp_terms.shape[3] // 3
    first_cut = early[0].shape[2]
    m_split = first_cut + 3 * hidden // 24 * 7 // 128 * 128
    m_parts = (m_split, 3 * hidden - m_split)
    sds = jax.ShapeDtypeStruct
    dma = pltpu.SemaphoreType.DMA
    vmem = pltpu.VMEM

    def step_buffers(n):
        return (
            vmem((2, 4, width // 16, n), bf16),
            vmem((2, 2, 4, width // 16, n), bf16),
            vmem((2, 4, width // 16, n), bf16),
            vmem((2, 4, width // 16, n), bf16),
            vmem((2, 3, width // 16, n), bf16),
        )

    return pl.pallas_call(
        backward_kernel,
        out_shape=(
            sds((4, quarter, width), bf16),
            sds((4, quarter, width), bf16),
            sds((2, shard, 3 * hidden), bf16),
            sds((2, shard, columns), bf16),
            sds((8, 128), f32),
            *(sds((2, 4, width // 16, n), bf16) for n in m_parts),
        ),
        in_specs=[HBM] * 11 + [VMEM] * 2 + [HBM] * 6,
        out_specs=(VMEM,) * 5 + (HBM,) * 2,
        scratch_shapes=[
            *(vmem(a.shape[1:], a.dtype) for a in (d_part, mix_part)),
            vmem(middle.shape, middle.dtype),
            vmem((quarter, width), bf16),
            vmem((quarter, width), bf16),
            *(vmem(a.shape, a.dtype) for a in (gain_rows, weights, low, normed, packed, attended, table)),
            *[vmem((seq, HEAD_DIM), bf16)] * 3,
            vmem((2, 4, quarter, width), bf16),
            vmem((quarter, width), f32),
            vmem((2, 4, quarter, width), bf16),
            vmem((2, 3, quarter, width), bf16),
            vmem((2, 3, quarter, width), bf16),
            vmem((4, chip, HEAD_DIM), bf16),
            vmem((4, chip, HEAD_DIM), bf16),
            vmem((HEAD_DIM, seq), bf16),
            vmem((seq, HEAD_DIM), f32),
            vmem((seq, HEAD_DIM), f32),
            vmem((4, chip * 3 // 2, 128), bf16),
            vmem((4, chip * 3 // 2, 128), bf16),
            vmem((width, chip), bf16),
            vmem((4, 4, width // 16, columns), bf16),
            *(vmem((4, width // 16, n), bf16) for _ in range(3) for n in m_parts),
            *(vmem((width // 16, n), bf16) for n in m_parts),
            *(vmem((2, width // 16, n), bf16) for n in m_parts),
            *(vmem((width // 16, n), bf16) for n in m_parts),
            vmem((width // 16, 3 * hidden), bf16),
            *(a for n in (3 * columns // 8, columns // 8) for a in step_buffers(n)),
            vmem((width // 16, columns), bf16),
            vmem((16, 8, 128), f32),
            vmem((4, 8, 128), f32),
            vmem((2, 8, 128), f32),
            vmem((3, 8, 128), f32),
            vmem((3, 4, 8, 128), f32),
            dma((3, 2, 4)), dma((3, 2, 3)), dma((3, 2, 4)), dma((2, 4)), dma((2, 3)), dma((2, 4)),
            dma((10, 2, 6)), dma((2, 15)), dma((4, 2, 3)), dma((2, 2)), dma((12,)), dma((2, 2, 2, 3)),
        ],
        compiler_params=pltpu.CompilerParams(
            collective_id=1, has_side_effects=True, vmem_limit_bytes=62 << 20
        ),
    )(
        d_part, mix_part, middle, tokens, cot, gain_rows, weights, low, normed, packed, attended, lse, start, table, mlp_terms, *early
    )


def finish_kernel(
    out_hbm, grad_hbm, mlp_hbm, attn_hbm, gain_hbm,
    layer_out, input_grad, gain_one, gain_two, grad_q, grad_k, grad_v, grad_o, grad_gate, grad_up, grad_down,
    out_in, grad_in, mlp_in, attn_in, gain_in, sem,
):
    c = lax.axis_index("core")
    sources = (gain_hbm, attn_hbm, mlp_hbm, out_hbm, grad_hbm)
    copies = [
        pltpu.make_async_copy(src, dst, sem.at[k])
        for k, (src, dst) in enumerate(zip(sources, (gain_in, attn_in, mlp_in, out_in, grad_in)))
    ]
    for copy in copies:
        copy.start()
    for copy in copies:
        copy.wait()
    shard, wide = grad_q.shape[0], grad_q.shape[1] // 2
    layer_out[...] = out_in[...].reshape(layer_out.shape)
    input_grad[...] = grad_in[...].reshape(input_grad.shape)
    for k, out in enumerate((gain_one, gain_two)):
        out[...] = jnp.where(c == 0, gain_in[k : k + 1, 0:shard], gain_in[k : k + 1, shard : 2 * shard])
    span = grad_gate.shape[1] // 4
    for e in range(2):
        for k, out in enumerate((grad_q, grad_k, grad_v, grad_o)):
            out[:, e * wide : (e + 1) * wide] = attn_in[e, :, k * wide : (k + 1) * wide].astype(f32)
        for g in range(2):
            lanes = slice((2 * e + g) * span, (2 * e + g + 1) * span)
            for k, out in enumerate((grad_gate, grad_up, grad_down)):
                out[:, lanes] = mlp_in[e, :, (3 * g + k) * span : (3 * g + k + 1) * span].astype(f32)


def finish(layer_out, input_grad, mlp_grads, attn_grads, gains):
    quarters, quarter, width = layer_out.shape
    rows = quarters * quarter
    _, shard, columns = attn_grads.shape
    hidden = mlp_grads.shape[2] // 3
    sds = jax.ShapeDtypeStruct
    narrow, broad = sds((shard, columns // 2), f32), sds((shard, 2 * hidden), f32)
    return pl.pallas_call(
        finish_kernel,
        out_shape=(
            *[sds((rows, width), bf16)] * 2,
            *[sds((1, shard), f32)] * 2,
            *[narrow] * 4,
            *[broad] * 3,
        ),
        in_specs=[HBM] * 5,
        scratch_shapes=[
            *(pltpu.VMEM(a.shape, a.dtype) for a in (layer_out, input_grad, mlp_grads, attn_grads, gains)),
            pltpu.SemaphoreType.DMA((5,)),
        ],
        compiler_params=pltpu.CompilerParams(vmem_limit_bytes=60 << 20),
    )(layer_out, input_grad, mlp_grads, attn_grads, gains)


def angle_table(positions):
    half = HEAD_DIM // 2
    frequency = rope_base ** (-(jnp.arange(half, dtype=f32) * 2.0) / HEAD_DIM)
    angle = positions.astype(f32)[:, None] * jnp.tile(frequency, 4)[None, :]
    lane = jnp.arange(4 * half)
    sign = jnp.where(lane < 3 * half, -1.0, 1.0)[None, :]
    return jnp.where((lane < 2 * half)[None, :], jnp.cos(angle), jnp.sin(angle) * sign)


def body(
    tokens_in,
    cotangent,
    segments,
    positions,
    norm1_gain,
    q_weight,
    k_weight,
    v_weight,
    o_weight,
    norm2_gain,
    gate_weight,
    up_weight,
    down_weight,
):
    rows, width = tokens_in.shape
    quarter = rows // 4
    (
        full, table, normed_one, packed, low, attended, middle, mixed, d_normed, terms, *early, gain_rows, start, lse,
    ) = forward_pass(
        q_weight, k_weight, v_weight, o_weight.T, gate_weight, up_weight, down_weight.T,
        norm1_gain[None], norm2_gain[None], tokens_in, cotangent, angle_table(positions), segments,
    )
    split = (2, 4, quarter, width)
    *results, _, _ = backward_pass(
        d_normed.reshape(split), mixed.reshape(split), middle, tokens_in, cotangent, gain_rows, full,
        low, normed_one, packed, attended, lse, start, table, terms, *early,
    )
    (
        layer_out, input_grad, gain_one, gain_two, grad_q, grad_k, grad_v, grad_o, grad_gate, grad_up, grad_down,
    ) = finish(*results)
    return (
        layer_out, input_grad, gain_one[0], grad_q, grad_k, grad_v, grad_o.T, gain_two[0], grad_gate, grad_up, grad_down.T,
    )


def solution(mesh):
    apart = Mesh(mesh.devices.reshape(4, 4, 2, 4), ("shard", "x", "core", "tensor"))
    tokens = ("shard", "x", "core")
    placed = (
        P(tokens, None),
        P(tokens, None),
        P("shard", None),
        P(tokens),
        P(tokens),
        P(tokens, "tensor"),
        P(tokens, "tensor"),
        P(tokens, "tensor"),
        P("tensor", tokens),
        P(tokens),
        P(tokens, "tensor"),
        P(tokens, "tensor"),
        P("tensor", tokens),
    )
    return jax.shard_map(
        body,
        mesh=apart,
        in_specs=placed,
        out_specs=(
            P(tokens, None),
            P(tokens, None),
            P(tokens),
            P(tokens, "tensor"),
            P(tokens, "tensor"),
            P(tokens, "tensor"),
            P("tensor", tokens),
            P(tokens),
            P(tokens, "tensor"),
            P(tokens, "tensor"),
            P("tensor", tokens),
        ),
        check_vma=False,
    )
```

```python
import jax
import jax.numpy as jnp
from jax import lax
from jax.experimental import pallas as pl
from jax.experimental.pallas import tpu as pltpu
from jax.sharding import Mesh
from jax.sharding import PartitionSpec as P

HEAD_DIM = 64
BLOCK = 512

epsilon = 1e-05
rope_base = 130000.0
masked_low = -1000000000.0

f32 = jnp.float32
bf16 = jnp.bfloat16
MESH = pl.DeviceIdType.MESH
VMEM = pl.BlockSpec(memory_space=pltpu.VMEM)
HBM = pl.BlockSpec(memory_space=pl.ANY)


def dot_nn(a, b):
    return lax.dot_general(a, b, (((1,), (0,)), ((), ())), preferred_element_type=f32)


def dot_nt(a, b):
    return lax.dot_general(a, b, (((1,), (1,)), ((), ())), preferred_element_type=f32)


def place():
    return tuple(lax.axis_index(a) for a in ("shard", "x", "core", "tensor"))


def turned(index, step):
    return lax.rem(index + step, 4)


def some(index, size):
    return pl.ds(pl.multiple_of(index * size, size), size)


def meet(axes):
    barrier = pltpu.get_barrier_semaphore()
    count = 0
    for axis in axes:
        me = lax.axis_index(axis)
        peers = [1 - me] if axis == "core" else [turned(me, d) for d in (1, 2, 3)]
        for peer in peers:
            pl.semaphore_signal(barrier, inc=1, device_id={axis: peer}, device_id_type=MESH)
            count += 1
    pl.semaphore_wait(barrier, count)


def remote(src, dst, send, recv, axis, index):
    return pltpu.make_async_remote_copy(
        src_ref=src, dst_ref=dst, send_sem=send, recv_sem=recv, device_id={axis: index}, device_id_type=MESH
    )


class Gather:
    def __init__(self, axis, me, block, half, sems, waits):
        self.axis, self.me, self.block, self.half, self.sems, self.waits = axis, me, block, half, sems, waits

    def send(self, ref, slot, step):
        copy = remote(ref, ref, self.sems.at[0, slot], self.sems.at[1, slot], self.axis, turned(self.me, step))
        copy.start()
        self.waits.append(copy)
        return copy

    def start(self):
        mine = self.block(self.me)
        self.right, self.left = self.send(mine, 0, 1), self.send(mine, 1, 3)

    def forward(self):
        self.right.wait_recv()
        self.right_on = self.send(self.half(turned(self.me, 3), 0), 2, 1)
        self.left.wait_recv()
        self.left_on = self.send(self.half(turned(self.me, 1), 1), 3, 3)

    def finish(self):
        self.right_on.wait_recv()
        self.left_on.wait_recv()


class Reduce:
    def __init__(self, axis, me, half, early, late, carried, sems, waits):
        self.axis, self.me, self.half, self.sems, self.waits = axis, me, half, sems, waits
        self.early, self.late, self.carried = early, late, carried

    def send(self, src, dst, slot, step):
        copy = remote(src, dst, self.sems.at[0, slot], self.sems.at[1, slot], self.axis, turned(self.me, step))
        copy.start()
        self.waits.append(copy)
        return copy

    def start(self):
        far, right, left = turned(self.me, 2), turned(self.me, 1), turned(self.me, 3)
        self.far = [
            self.send(self.half(far, 0), self.early(0), 0, 1),
            self.send(self.half(far, 1), self.early(1), 1, 3),
        ]
        self.plain = [
            self.send(self.half(right, 1), self.late(0, 1), 2, 1),
            self.send(self.half(left, 0), self.late(1, 0), 3, 3),
        ]

    def join(self, add):
        for h in range(2):
            self.far[h].wait_recv()
            add(h)

    def pass_on(self):
        self.both = [self.send(self.carried(h), self.late(h, h), 4 + h, step) for h, step in ((0, 1), (1, 3))]

    def middle(self, add):
        self.join(add)
        self.pass_on()

    def finish(self):
        for copy in self.plain + self.both:
            copy.wait_recv()


def rope(vectors, table_cos, table_sin):
    n = vectors.shape[1]
    lane = lax.broadcasted_iota(jnp.int32, vectors.shape, 1)
    other = jnp.where(
        lax.rem(lane, HEAD_DIM) < HEAD_DIM // 2,
        pltpu.roll(vectors, n - HEAD_DIM // 2, 1),
        pltpu.roll(vectors, HEAD_DIM // 2, 1),
    )
    return vectors * table_cos + other * table_sin


def masked(raw, begin, j, i, diagonal):
    key = lax.broadcasted_iota(jnp.int32, raw.shape, 0)
    allowed = key >= begin - j * BLOCK
    if diagonal:
        allowed = allowed & (key <= lax.broadcasted_iota(jnp.int32, raw.shape, 1))
    return jnp.where(allowed, raw, masked_low)


def forward_kernel(
    wq, wk, wv, wo, wg, wu, wd, gain_one, gain_two, tokens, cot, rotary, seg_row,
    full_out, table_out, normed_out, packed_out, low_out, attended_out, middle_out, mixed_out, d_normed_out, terms_out,
    far_z, far_x, plain_z, plain_x, gain_rows, start, lse,
    full, normed, table, low, attended_t, middle, normed_two,
    gains, attn_give, mlp_give, gain_all, chip_tokens, packed, arrived, keys, value_t, scaled_q,
    head_out, low_in, own, other, pair, near,
    mlp_full, cot_held, cot_t, normed_t, both, made_hidden, made, d_held, mixed_held, d_hidden_held,
    local, core_sem, out_sem, made_sem, grad_sem, ring_sem, gain_sem, xsem, lsem, csem, ysem, asem, fsem,
):
    z, x, c, y = place()
    half = wq.shape[1] // 2
    shard = wq.shape[0]
    hidden = wg.shape[1] // 2
    groups = 2
    span = hidden // groups
    chip, width = normed.shape
    waits = []
    meet(("core", "x", "shard", "tensor"))

    at = some(c, shard)
    lane = lax.broadcasted_iota(jnp.int32, (8, 128), 1) // (2 * shard // 2)
    both_gains = jnp.concatenate(
        [gain_one[...].astype(f32), gain_two[...].astype(f32), jnp.zeros((6, shard), f32)], axis=0
    )
    both_gains = jnp.where(lane == c, jnp.concatenate([both_gains, both_gains], axis=1), 0.0)
    gains[...] = jnp.concatenate([both_gains, jnp.zeros((8, 128), f32)], axis=0).astype(bf16)
    for k, w in enumerate((wq, wk, wv, wo)):
        attn_give[:, k * half : (k + 1) * half] = w[:, some(1 - c, half)]
        full[z, x, at, k * half : (k + 1) * half] = w[:, some(c, half)]
    for k, w in enumerate((wg, wu, wd)):
        for g in range(groups):
            lanes = slice((3 * g + k) * span, (3 * g + k + 1) * span)
            mlp_give[:, lanes] = w[:, some((1 - c) * groups + g, span)]
            mlp_full[z, x, at, lanes] = w[:, some(c * groups + g, span)]
    pairs = [(gains, gains, gain_all.at[z, x, c]), (None, attn_give, full.at[z, x, at, :])]
    pairs += [(None, mlp_give, mlp_full.at[z, x, at, :])]
    pairs += [(a, a, b.at[c]) for a, b in ((tokens, chip_tokens), (rotary, table), (cot, cot_held))]
    inside, across = [], []
    for k, (mine, theirs, there) in enumerate(pairs):
        inside.append(pltpu.make_async_copy(mine, there, local.at[k]) if mine is not None else None)
        across.append(remote(theirs, there, core_sem.at[0, k], core_sem.at[1, k], "core", 1 - c))
        across[-1].start()
        if mine is not None:
            inside[-1].start()
    waits += across
    kept = []

    def keep(src, dst):
        kept.append(pltpu.make_async_copy(src, dst, out_sem.at[len(kept)]))
        kept[-1].start()

    def here(ks):
        for k in ks:
            if inside[k] is not None:
                inside[k].wait()
            across[k].wait_recv()

    def spread(src, r, axis, me):
        copies = []
        for d in (1, 2, 3):
            copies.append(remote(src, src, gain_sem.at[0, r, d - 1], gain_sem.at[1, r, d - 1], axis, turned(me, d)))
            copies[-1].start()
        waits.extend(copies)
        return copies

    all_rings = []

    def ring(axis, block, half_of):
        all_rings.append(Gather(axis, x if axis == "x" else z, block, half_of, ring_sem.at[len(all_rings)], waits))
        return all_rings[-1]

    def half_rows(h):
        return pl.ds(h * shard, shard)

    def both_of(p):
        return pl.ds(2 * p, 2)

    def first_along(axis, array, lanes):
        if axis == "x":
            return ring("x", lambda k: array.at[z, k, :, lanes], lambda k, h: array.at[z, k, half_rows(h), lanes])
        return ring("shard", lambda k: array.at[k, x, :, lanes], lambda k, h: array.at[k, x, half_rows(h), lanes])

    def then_along(axis, array, lanes):
        if axis == "x":
            return [
                ring("x", lambda k, p=p: array.at[both_of(p), k, :, lanes], lambda k, h, p=p: array.at[2 * p + h, k, :, lanes])
                for p in range(2)
            ]
        return [
            ring("shard", lambda k, p=p: array.at[k, both_of(p), :, lanes], lambda k, h, p=p: array.at[k, 2 * p + h, :, lanes])
            for p in range(2)
        ]

    qkv_a, qkv_b, out_a = pl.ds(0, 3 * half // 2), pl.ds(3 * half // 2, 3 * half // 2), pl.ds(3 * half, half)
    late_a = 3 * span * 7 // 12 // 128 * 128
    mlp_a1, mlp_b1 = pl.ds(0, 3 * span // 2), pl.ds(3 * span // 2, 3 * span // 2)
    mlp_a2, mlp_b2 = pl.ds(3 * span, late_a), pl.ds(3 * span + late_a, 3 * span - late_a)
    ax, az = first_along("x", full, qkv_a), then_along("shard", full, qkv_a)
    bz, bx = first_along("shard", full, qkv_b), then_along("x", full, qkv_b)
    ox, oz = first_along("x", full, out_a), then_along("shard", full, out_a)
    mx1, mz1 = first_along("x", mlp_full, mlp_a1), then_along("shard", mlp_full, mlp_a1)
    nz1, nx1 = first_along("shard", mlp_full, mlp_b1), then_along("x", mlp_full, mlp_b1)
    mx2, mz2 = first_along("x", mlp_full, mlp_a2), then_along("shard", mlp_full, mlp_a2)
    nz2, nx2 = first_along("shard", mlp_full, mlp_b2), then_along("x", mlp_full, mlp_b2)

    def start_all(rings):
        for one in rings:
            one.start()

    def forward_all(rings):
        for one in rings:
            one.forward()

    def finish_all(rings):
        for one in rings:
            one.finish()

    here((0,))
    gain_x = spread(gain_all.at[z, x], 0, "x", x)
    here((1,))
    start_all((ax, bz))
    here((2,))
    start_all((mx1, nz1))
    for copy in gain_x:
        copy.wait_recv()
    gain_z = spread(gain_all.at[z], 1, "shard", z)
    forward_all((ax, bz))
    ox.start()
    forward_all((mx1, nz1))
    ax.finish()
    start_all(az)
    bz.finish()
    start_all(bx)
    ox.forward()

    for copy in gain_z:
        copy.wait_recv()
    for i in range(16):
        two = (gain_all[i // 4, i % 4, 0] + gain_all[i // 4, i % 4, 1]).astype(f32)
        gain_rows[:, pl.ds(i * 128, 128)] = two[0:8, :]
    here((3, 4))

    def norm(i, unused):
        values = chip_tokens[i // 4, some(lax.rem(i, 4), 64), :].astype(f32)
        scale = lax.rsqrt(jnp.mean(values * values, axis=-1, keepdims=True) + epsilon)
        normed[some(i, 64), :] = ((values * scale) * gain_rows[0:1, :]).astype(bf16)
        return unused

    lax.fori_loop(0, chip // 64, norm, 0)
    keep(normed, normed_out)
    keep(table, table_out)
    row = seg_row[...].astype(f32)
    begins = [jnp.zeros((1, BLOCK), f32)] * 4
    for i in range(4):
        column = jnp.transpose(jnp.broadcast_to(row[:, i * BLOCK : (i + 1) * BLOCK], (128, BLOCK)))[:, 0:1]
        for j in range(i, 4):
            earlier = column < row[:, j * BLOCK : (j + 1) * BLOCK]
            begins[j] = begins[j] + jnp.sum(jnp.where(earlier, 1.0, 0.0), axis=0, keepdims=True)
    for i in range(4):
        start[:, i * BLOCK : (i + 1) * BLOCK] = begins[i].astype(jnp.int32)
    forward_all((az[0], bx[0], az[1], bx[1]))
    start_all((mx2, nz2))
    ox.finish()
    start_all(oz)
    mx1.finish()
    start_all(mz1)
    finish_all(az + bx)

    wide = 4 * HEAD_DIM

    def weights(k):
        return full[:, :, :, k * wide : (k + 1) * wide].reshape(width, wide)

    rotation = table[...].reshape(chip, 128)
    cosine = jnp.concatenate([rotation[:, 0:64]] * 4, axis=1)
    sine = jnp.concatenate([rotation[:, 64:128]] * 4, axis=1)
    queries = rope(dot_nn(normed[...], weights(0)), cosine, sine).astype(bf16)
    turned_keys = rope(dot_nn(normed[...], weights(1)), cosine, sine).astype(bf16)
    values = dot_nn(normed[...], weights(2)).astype(bf16)
    for h in range(4):
        lanes = slice(h * HEAD_DIM, (h + 1) * HEAD_DIM)
        packed[h, 0:chip, :] = jnp.concatenate([queries[:, lanes], turned_keys[:, lanes]], axis=1)
        packed[h, chip:, :] = jnp.concatenate(
            [values[0 : chip // 2, lanes], values[chip // 2 :, lanes]], axis=1
        )
    sent = []
    for d in (2, 1, 3):
        k = turned(x, d)
        sent.append(remote(packed.at[k], arrived.at[x], xsem.at[0, d - 1], xsem.at[1, d - 1], "x", k))
        sent[-1].start()
    waits += sent
    forward_all((mx2, nz2))
    forward_all(oz)
    nz1.finish()
    nx1[0].start()
    arrived[x] = packed[x]
    for copy in sent:
        copy.wait_recv()
    for k in range(4):
        rows = slice(k * chip, (k + 1) * chip)
        scaled_q[rows, :] = arrived[k, 0:chip, 0:64] * HEAD_DIM ** (-0.5)
        keys[rows, :] = arrived[k, 0:chip, 64:128]
        block = jnp.concatenate([arrived[k, chip:, 0:64], arrived[k, chip:, 64:128]], axis=0)
        value_t[:, rows] = jnp.transpose(block)
    keep(arrived, packed_out)

    for i in range(4):
        if i == 2:
            mz1[0].forward()
        if i == 3:
            mx2.finish()
            start_all(mz2)
        at = slice(i * BLOCK, (i + 1) * BLOCK)
        begin = start[:, at]
        mine = scaled_q[at, :]

        def step(j, state, diagonal=False):
            peak, total, summed = state
            scores = masked(dot_nt(keys[some(j, BLOCK), :], mine), begin, j, i, diagonal)
            new = jnp.maximum(peak, jnp.max(scores, axis=0, keepdims=True))
            weight = jnp.exp(scores - new)
            factor = jnp.exp(peak - new)
            total = total * factor + jnp.sum(weight, axis=0, keepdims=True)
            summed = summed * factor + dot_nn(value_t[:, some(j, BLOCK)], weight.astype(bf16))
            return (new, total, summed)

        state = (
            jnp.full((1, BLOCK), masked_low, f32),
            jnp.zeros((1, BLOCK), f32),
            jnp.zeros((HEAD_DIM, BLOCK), f32),
        )
        state = step(i, state, True)
        peak, total, summed = lax.fori_loop(0, i, step, state) if i else state
        attended = summed / total
        attended_t[:, at] = attended
        lse[:, at] = peak + jnp.log(total)
        head_out[i] = jnp.transpose(attended).astype(bf16)

        @pl.when(x != i)
        def send(i=i):
            remote(head_out.at[i], low_in.at[x], lsem.at[0, i], lsem.at[1, x], "x", i).start()

    nz2.finish()
    nx1[1].start()
    nx1[0].forward()
    start_all(nx2)
    mz1[1].forward()
    low_in[x] = head_out[x]
    for d in (1, 2, 3):
        k = turned(x, d)
        copy = remote(head_out.at[k], low_in.at[k], lsem.at[0, k], lsem.at[1, k], "x", k)
        copy.wait_recv()
        waits.append(copy)
    low[...] = jnp.concatenate([low_in[h] for h in range(4)], axis=1)
    finish_all(oz)
    keep(full, full_out)
    keep(low, low_out)
    keep(attended_t, attended_out)

    side, quarter = chip // 2, chip // 8
    out_weights = weights(3)
    other[...] = dot_nt(low[some(1 - c, side), :], out_weights).astype(bf16).reshape(other.shape)
    crossed = {}
    for d in (2, 1, 3, 0):
        k = turned(y, d)
        crossed[d] = remote(other.at[k], pair.at[k], csem.at[0, d], csem.at[1, d], "core", 1 - c)
        crossed[d].start()
    own[...] = dot_nt(low[some(c, side), :], out_weights).reshape(own.shape)
    along = {}
    for d in (2, 1, 3):
        k = turned(y, d)
        crossed[d].wait_recv()
        crossed[d].wait_send()
        other[k] = (own[k] + pair[k].astype(f32)).astype(bf16)
        along[d] = remote(other.at[k], near.at[d - 1], ysem.at[0, d - 1], ysem.at[1, d - 1], "tensor", k)
        along[d].start()
    crossed[0].wait_recv()
    crossed[0].wait_send()
    here((5,))
    nx1[1].forward()
    cot_t[...] = jnp.transpose(cot_held[...].reshape(chip, width))
    mz2[0].forward()
    total = own[y] + pair[y].astype(f32)
    for d in (1, 3, 2):
        along[d].wait_recv()
        total = total + near[d - 1].astype(f32)
    waits += [*along.values()]
    mid = chip_tokens[c, some(y, quarter), :].astype(f32) + total
    middle[...] = mid
    keep(middle, middle_out)
    scale = lax.rsqrt(jnp.mean(mid * mid, axis=-1, keepdims=True) + epsilon)
    normed_two[c, y] = ((mid * scale) * gain_rows[1:2, :]).astype(bf16)
    share = Gather(
        "tensor", y, lambda k: normed_two.at[c, k], lambda k, h: normed_two.at[c, k, pl.ds(h * quarter // 2, quarter // 2)],
        asem, waits,
    )
    forward = []

    def forward_on(k):
        slot = normed_two.at[c, k]
        d = len(forward)
        forward.append(remote(slot, slot, fsem.at[0, d], fsem.at[1, d], "core", 1 - c))
        forward[-1].start()

    share.start()
    forward_on(y)

    def group(g, k):
        return mlp_full[:, :, :, (3 * g + k) * span : (3 * g + k + 1) * span].reshape(width, span)

    chip_cot = cot_held[...].reshape(chip, width)
    share.forward()
    forward_on(turned(y, 3))
    forward_on(turned(y, 1))
    share.finish()
    forward_on(turned(y, 2))
    mz2[1].forward()
    forward_all(nx2)
    finish_all(nx1 + mz1)
    d_hidden_held[...] = dot_nn(chip_cot, group(0, 2))
    for copy in forward:
        copy.wait_recv()
    waits += forward

    cut = far_z.shape[2]
    early_rings = [
        Reduce(
            "shard", z, lambda k, h: terms_out.at[k, both_of(h), :, pl.ds(0, cut)], lambda h: far_z.at[both_of(h)],
            lambda e, h: plain_z.at[e], None, grad_sem.at[0], waits,
        ),
        Reduce(
            "x", x, lambda k, h: terms_out.at[both_of(h), k, :, pl.ds(cut, cut)], lambda h: far_x.at[both_of(h)],
            lambda e, h: plain_x.at[e], None, grad_sem.at[1], waits,
        ),
    ]
    rows_two = normed_two[...].reshape(chip, width)
    normed_t[...] = jnp.transpose(rows_two)
    stores = {}
    for g in range(groups):
        if g == 1:
            finish_all(mz2 + nx2)
        gate = dot_nn(rows_two, group(g, 0))
        upper = dot_nn(rows_two, group(g, 1))
        d_hidden = dot_nn(chip_cot, group(g, 2)) if g else d_hidden_held[...]
        sigmoid = 1.0 / (1.0 + jnp.exp(-gate))
        silu = gate * sigmoid
        made_hidden[g] = (silu * upper).astype(bf16)
        both[g, :, 0:span] = (d_hidden * upper * (sigmoid * (1.0 + gate * (1.0 - sigmoid)))).astype(bf16)
        both[g, :, span : 2 * span] = (d_hidden * silu).astype(bf16)
        for k, (left, right) in enumerate(
            ((normed_t, both.at[g, :, 0:span]), (normed_t, both.at[g, :, span : 2 * span]), (cot_t, made_hidden.at[g]))
        ):
            if g == 1 and k == 2:
                stores[0, 2].wait()
            for q in range(4):
                term = dot_nn(left[q * (width // 4) : (q + 1) * (width // 4), :], right[...])
                made[k, q] = term.astype(bf16).reshape(made.shape[2:])
            stores[g, k] = pltpu.make_async_copy(
                made.at[k], terms_out.at[:, :, :, pl.ds((3 * g + k) * span, span)], made_sem.at[g, k]
            )
            stores[g, k].start()
            if g == 0 and k > 0:
                stores[g, k - 1].wait()
                early_rings[k - 1].start()
    for held, out, left, first, n in ((d_held, d_normed_out, both, 0, 2), (mixed_held, mixed_out, made_hidden, 2, 1)):
        for t in range(4):
            lanes = slice(t * (width // 4), (t + 1) * (width // 4))
            term = [
                dot_nt(
                    left[g],
                    mlp_full[t, :, :, (3 * g + first) * span : (3 * g + first + n) * span].reshape(width // 4, n * span),
                )
                for g in range(groups)
            ]
            held[:, lanes] = (term[0] + term[1]).astype(bf16)
        keep(held, out)
    for k in range(3):
        stores[groups - 1, k].wait()
    for ring in early_rings:
        for copy in ring.far + ring.plain:
            copy.wait_recv()
    for copy in kept:
        copy.wait()
    for copy in waits:
        copy.wait_send()


def forward_pass(wq, wk, wv, wo, wg, wu, wd, gain_one, gain_two, tokens, cot, rotary, seg_row):
    rows, width = tokens.shape
    chip, quarter, seq = 2 * rows, rows // 4, seg_row.shape[1]
    columns, hidden = 2 * wq.shape[1], wg.shape[1] // 2
    sds = jax.ShapeDtypeStruct
    dma = pltpu.SemaphoreType.DMA
    vmem = pltpu.VMEM
    kept = (
        ((4, 4, width // 16, columns), bf16),
        ((chip, width), bf16),
        ((2, rows, 128), f32),
        ((chip, 4 * HEAD_DIM), bf16),
        ((HEAD_DIM, seq), f32),
        ((quarter, width), f32),
        ((2, 4, quarter, width), bf16),
    )
    full, normed, table, low, attended, middle, _ = (sds(*a) for a in kept)
    span = hidden // 2
    packed = (4, chip * 3 // 2, 128)
    return pl.pallas_call(
        forward_kernel,
        out_shape=(
            full,
            table,
            normed,
            sds(packed, bf16),
            low,
            attended,
            middle,
            sds((chip, width), bf16),
            sds((chip, width), bf16),
            sds((4, 4, width // 16, 3 * hidden), bf16),
            *[sds((4, width // 16, span), bf16)] * 2,
            *[sds((2, 2, width // 16, span), bf16)] * 2,
            sds((8, width), f32),
            sds((1, seq), jnp.int32),
            sds((1, seq), f32),
        ),
        in_specs=[VMEM] * 9 + [HBM] * 3 + [VMEM],
        out_specs=(HBM,) * 14 + (VMEM,) * 3,
        scratch_shapes=[
            *(vmem(*a) for a in kept),
            vmem((16, 128), bf16),
            vmem((width // 32, columns), bf16),
            vmem((width // 32, 3 * hidden), bf16),
            vmem((4, 4, 2, 16, 128), bf16),
            vmem((2, rows, width), bf16),
            vmem(packed, bf16),
            vmem(packed, bf16),
            vmem((seq, HEAD_DIM), bf16),
            vmem((HEAD_DIM, seq), bf16),
            vmem((seq, HEAD_DIM), bf16),
            vmem((4, chip, HEAD_DIM), bf16),
            vmem((4, chip, HEAD_DIM), bf16),
            vmem((4, quarter, width), f32),
            vmem((4, quarter, width), bf16),
            vmem((4, quarter, width), bf16),
            vmem((3, quarter, width), bf16),
            vmem((4, 4, width // 16, 3 * hidden), bf16),
            vmem((2, rows, width), bf16),
            vmem((width, chip), bf16),
            vmem((width, chip), bf16),
            vmem((2, chip, 2 * span), bf16),
            vmem((2, chip, span), bf16),
            vmem((3, 4, 4, width // 16, span), bf16),
            vmem((chip, width), bf16),
            vmem((chip, width), bf16),
            vmem((chip, span), f32),
            dma((6,)), dma((2, 6)), dma((9,)), dma((2, 3)), dma((2, 2, 6)), dma((21, 2, 4)), dma((2, 2, 3)), dma((2, 3)), dma((2, 4)),
            dma((2, 4)), dma((2, 3)), dma((2, 4)), dma((2, 4)),
        ],
        compiler_params=pltpu.CompilerParams(
            collective_id=0, has_side_effects=True, vmem_limit_bytes=62 << 20
        ),
    )(wq, wk, wv, wo, wg, wu, wd, gain_one, gain_two, tokens, cot, rotary, seg_row)


def backward_kernel(
    d_part_in, mix_part_in, middle_in, tokens_in, cot_in, gain_rows_in, weights_in, low_in, normed_in, packed_in, attended_in,
    lse, start, table_in, mlp_terms, far_z, far_x, plain_z, plain_x,
    layer_out, input_grad, swapped_m, swapped_a, gain_out, landed_z, landed_x,
    d_part, mix_part, middle, own_tokens, own_cot, gain_rows, weights, low, normed, qkv_packed, attended, table,
    queries, keys, values,
    d_branch, d_mid, pair, half_sum, near, heads, head_in, key_t, d_key, d_value, packed, arrived,
    turned_rows, terms, m_early_z, m_early_x, m_carry_z, m_carry_x, m_mine_z, m_mine_x,
    m2_early_z, m2_early_x, m2_late_z, m2_late_x, m2_carry_z, m2_carry_x, m2_mine,
    a_early, a_late, a_carry, a_mine, a2_in, o_early, o_late, o_carry, o_mine, o2_in, a2_mine,
    gain_part, gain_y, gain_c, gain_x, gain_z,
    csem, ysem, asem, fsem, hsem, psem, rsem, local, gsem, outsem, in_sem, dsem,
):
    z, x, c, y = place()
    quarter = middle.shape[0]
    mine_at = some(y, quarter)
    taken = {}
    for k, (name, src, dst) in enumerate(
        (
            ("d_part", d_part_in.at[c], d_part),
            ("middle", middle_in, middle),
            ("gain_rows", gain_rows_in, gain_rows),
            ("own_cot", cot_in.at[mine_at, :], own_cot),
            ("mix_part", mix_part_in.at[c], mix_part),
            ("packed", packed_in, qkv_packed),
            ("weights", weights_in, weights),
            ("low", low_in, low),
            ("attended", attended_in, attended),
            ("normed", normed_in, normed),
            ("table", table_in, table),
            ("own_tokens", tokens_in.at[mine_at, :], own_tokens),
        )
    ):
        taken[name] = pltpu.make_async_copy(src, dst, in_sem.at[k])
        taken[name].start()

    def take(*names):
        for name in names:
            taken[name].wait()

    meet(("core", "x", "tensor", "shard"))
    chip, width = normed.shape
    side = chip // 2
    wide = 4 * HEAD_DIM
    shard = width // 32
    a_split = a_mine.shape[3]
    cut = far_z.shape[2]
    others = mlp_terms.shape[3] - 2 * cut
    late_cut = m_mine_z.shape[2] - cut
    far, plain = (far_z, far_x), (plain_z, plain_x)
    landed, m_early, m_carry, m_mine = (landed_z, landed_x), (m_early_z, m_early_x), (m_carry_z, m_carry_x), (m_mine_z, m_mine_x)
    m2_early, m2_late, m2_carry = (m2_early_z, m2_early_x), (m2_late_z, m2_late_x), (m2_carry_z, m2_carry_x)
    e_lanes = (pl.ds(0, cut), pl.ds(cut, cut))
    l_lanes = (pl.ds(2 * cut, late_cut), pl.ds(2 * cut + late_cut, others - late_cut))
    held_e = pl.ds(0, cut)
    held_l = (pl.ds(cut, late_cut), pl.ds(cut, others - late_cut))
    o_split = o_mine.shape[3]
    a_lanes = (pl.ds(0, a_split), pl.ds(a_split, a_split))
    o_lanes = (pl.ds(2 * a_split, o_split), pl.ds(2 * a_split + o_split, o_split))
    waits = []

    def begin(copy):
        copy.start()
        waits.append(copy)
        return copy

    def sent_all(copies):
        for copy in copies:
            copy.wait_send()
        waits[:] = [w for w in waits if not any(w is copy for copy in copies)]

    def cross(r, part):
        return {
            d: begin(remote(part.at[turned(y, d)], pair.at[r % 2, turned(y, d)], csem.at[r, 0, d], csem.at[r, 1, d], "core", 1 - c))
            for d in (2, 1, 3, 0)
        }

    def along(r, part, crossed):
        sent = {}
        for d in (2, 1, 3):
            k = turned(y, d)
            crossed[d].wait_recv()
            half_sum[r % 2, d - 1] = part[k] + pair[r % 2, k]
            sent[d] = begin(remote(half_sum.at[r % 2, d - 1], near.at[r % 2, d - 1], ysem.at[r, 0, d - 1], ysem.at[r, 1, d - 1], "tensor", k))
        return sent

    def total_of(r, part, crossed, sent):
        crossed[0].wait_recv()
        total = part[y].astype(f32) + pair[r % 2, y].astype(f32)
        for d in (1, 3, 2):
            sent[d].wait_recv()
            total = total + near[r % 2, d - 1].astype(f32)
        return total

    def share(r, slot):
        cut = quarter // 2
        ring = Gather("tensor", y, slot, lambda k, h: slot(k).at[pl.ds(h * cut, cut)], asem.at[r], waits)
        ring.start()
        return ring

    def two(h):
        return pl.ds(2 * h, 2)

    def rows(h):
        return pl.ds(h * shard, shard)

    def apart(ref):
        return (ref.at[0], ref.at[1])

    def term_of(s, k, q, lanes):
        return terms[k, q, :, lanes[s]] if s == 0 else terms[q, k, :, lanes[s]]

    def join_terms(s, lanes, carry, early):
        def add(h):
            k = turned((z, x)[s], (1, 3)[h])
            for q in (2 * h, 2 * h + 1):
                carry[s, q] = term_of(s, k, q, lanes) + early[s, q]

        return add

    def sum_terms(ring, s, lanes, mine, late):
        ring.finish()
        for q in range(4):
            mine[s, q] = (
                term_of(s, (z, x)[s], q, lanes).astype(f32) + late[s, 0, q].astype(f32) + late[s, 1, q].astype(f32)
            ).astype(bf16)

    def direct(r, s, mine, into):
        axis, me = (("x", x), ("shard", z))[s]
        return [
            begin(remote(mine.at[s, turned(me, d)], into.at[s, d - 1], dsem.at[r, s, 0, d - 1], dsem.at[r, s, 1, d - 1], axis, turned(me, d)))
            for d in (2, 1, 3)
        ]

    def direct_sum(copies, s, mine, into, lanes):
        for copy in copies:
            copy.wait_recv()
        a2_mine[:, lanes[s]] = (
            (mine[s, (x, z)[s]].astype(f32) + into[s, 0].astype(f32))
            + (into[s, 1].astype(f32) + into[s, 2].astype(f32))
        ).astype(bf16)

    def first_step(s, source, split, early, late, carry, r):
        axis, me = (("shard", z), ("x", x))[s]
        columns = split[s]

        def half(k, h):
            return source.at[k, two(h), :, columns] if s == 0 else source.at[two(h), k, :, columns]

        return Reduce(
            axis, me, half, lambda h: early[s].at[two(h)], lambda e, h: late[s].at[e, two(h)],
            lambda h: carry[s].at[two(h)], rsem.at[r + s], waits,
        ), half

    def second_step(s, mine, early, late, carry, r):
        axis, me = (("x", x), ("shard", z))[s]
        return Reduce(
            axis, me, lambda k, h: mine[s].at[k, rows(h)], lambda h: early[s].at[rows(h)],
            lambda e, h: late[s].at[e, rows(h)], lambda h: carry[s].at[rows(h)], rsem.at[r + s], waits,
        )

    def group_ring(s, source_lanes, held, r):
        axis, me = (("shard", z), ("x", x))[s]

        def half(k, h):
            return mlp_terms.at[k, two(h), :, source_lanes] if s == 0 else mlp_terms.at[two(h), k, :, source_lanes]

        return Reduce(
            axis, me, half, lambda h: m_early[s].at[two(h), :, held], lambda e, h: landed[s].at[e, two(h), :, held],
            lambda h: m_carry[s].at[two(h), :, held], rsem.at[r + s], waits,
        )

    e_rings = [group_ring(s, e_lanes[s], held_e, 8) for s in range(2)]
    m_rings = [group_ring(s, l_lanes[s], held_l[s], 0) for s in range(2)]
    loads = {}

    def load(src, dst, s, k):
        loads[s, k] = pltpu.make_async_copy(src, dst, local.at[s, k])
        loads[s, k].start()

    d_crossed = cross(0, d_part_in.at[1 - c])
    for s, me in ((0, z), (1, x)):
        m_rings[s].start()
        for n, (rings, held) in enumerate(((e_rings, held_e), (m_rings, held_l[s]))):
            for h, k in ((0, turned(me, 1)), (1, turned(me, 3))):
                load(rings[s].half(k, h), m_carry[s].at[two(h), :, held], s, 4 * n + h)
                load(rings[s].half(me, h), m_mine[s].at[two(h), :, held], s, 4 * n + 2 + h)
        load(far[s], m_early[s].at[:, :, held_e], s, 8)
    m_crossed = cross(1, mix_part_in.at[1 - c])
    take("d_part", "mix_part")
    d_sent = along(0, d_part, d_crossed)
    take("middle", "gain_rows", "own_cot", "packed")
    mid = middle[...]
    scale = lax.rsqrt(jnp.mean(mid * mid, axis=-1, keepdims=True) + epsilon)
    unit = mid * scale
    for k in range(4):
        at = slice(k * chip, (k + 1) * chip)
        queries[at, :] = qkv_packed[k, 0:chip, 0:64] * HEAD_DIM ** (-0.5)
        block = qkv_packed[k, 0:chip, 64:128]
        keys[at, :] = block
        key_t[:, at] = jnp.transpose(block)
        values[at, :] = jnp.concatenate([qkv_packed[k, chip:, 0:64], qkv_packed[k, chip:, 64:128]], axis=0)
    d_key[...] = jnp.zeros_like(d_key)
    d_value[...] = jnp.zeros_like(d_value)
    def add_far(ring, s):
        def add(h):
            loads[s, 4 + h].wait()
            for q in (2 * h, 2 * h + 1):
                m_carry[s][q, :, held_l[s]] = m_carry[s][q, :, held_l[s]] + m_early[s][q, :, held_l[s]]

        ring.join(add)

    for s in range(2):
        for k in (0, 1, 8):
            loads[s, k].wait()
        for q in range(4):
            m_carry[s][q, :, held_e] = m_carry[s][q, :, held_e] + m_early[s][q, :, held_e]
        e_rings[s].pass_on()
    add_far(m_rings[1], 1)
    d_two = total_of(0, d_part, d_crossed, d_sent)
    gain_two_part = jnp.sum(d_two * unit, axis=0, keepdims=True)
    scaled = d_two * gain_rows[1:2, :]
    d_middle = own_cot[...].astype(f32) + scale * (
        scaled - unit * jnp.mean(scaled * unit, axis=-1, keepdims=True)
    )
    d_mid[...] = d_middle
    d_branch[c, y] = d_middle.astype(bf16)
    shared = share(0, lambda k: d_branch.at[c, k])
    forward = []

    def forward_on(k):
        slot, d = d_branch.at[c, k], len(forward)
        forward.append(begin(remote(slot, slot, fsem.at[0, d], fsem.at[1, d], "core", 1 - c)))

    forward_on(y)
    add_far(m_rings[0], 0)
    m_rings[0].pass_on()
    shared.forward()
    forward_on(turned(y, 3))
    forward_on(turned(y, 1))
    m_sent = along(1, mix_part, m_crossed)
    shared.finish()
    forward_on(turned(y, 2))
    for copy in forward:
        copy.wait_recv()
    branch = d_branch[...].reshape(chip, width)
    take("weights", "low", "attended", "normed", "table", "own_tokens")

    def weights_of(k, n):
        return weights[:, :, :, k * wide : (k + n) * wide].reshape(width, n * wide)

    d_heads = dot_nn(branch, weights_of(3, 1)).astype(bf16)
    for h in range(4):
        heads[h] = d_heads[:, h * HEAD_DIM : (h + 1) * HEAD_DIM]
    head_sent = {}
    for d in (2, 1, 3):
        k = turned(x, d)
        head_sent[d] = begin(remote(heads.at[k], head_in.at[x], hsem.at[0, d - 1], hsem.at[1, d - 1], "x", k))
    head_in[x] = heads[x]
    m_rings[1].pass_on()
    turned_rows[...] = jnp.transpose(branch)
    terms[:, :, :, 3 * wide : 4 * wide] = (
        dot_nn(turned_rows[...], low[...]).astype(bf16).reshape(4, 4, width // 16, wide)
    )
    o_rings = [first_step(s, terms, o_lanes, apart(o_early), apart(o_late), apart(o_carry), 6)[0] for s in range(2)]
    for ring in o_rings:
        ring.start()
    for d in (1, 3, 2):
        head_sent[d].wait_recv()


    for i in (3, 2, 1, 0):
        at = slice(i * BLOCK, (i + 1) * BLOCK)
        mine, d_out = queries[at, :], head_in[i]
        center = jnp.sum(jnp.transpose(d_out.astype(f32)) * attended[:, at], axis=0, keepdims=True)
        peak, first = lse[:, at], start[:, at]

        def step(j, d_query, diagonal=False):
            key_at = some(j, BLOCK)
            scores = masked(dot_nt(keys[key_at, :], mine), first, j, i, diagonal)
            weight = jnp.exp(scores - peak)
            d_prob = dot_nt(values[key_at, :], d_out)
            d_raw = (weight * (d_prob - center)).astype(bf16)
            d_key[key_at, :] += dot_nn(d_raw, mine)
            d_value[key_at, :] += dot_nn(weight.astype(bf16), d_out)
            return d_query + dot_nn(key_t[:, key_at], d_raw)

        d_query = step(i, jnp.zeros((HEAD_DIM, BLOCK), f32), True)
        d_query = lax.fori_loop(0, i, step, d_query) if i else d_query
        packed[i, 0:chip, :] = jnp.concatenate(
            [jnp.transpose(d_query * HEAD_DIM ** (-0.5)).astype(bf16), d_key[at, :].astype(bf16)], axis=1
        )
        d_rows = d_value[at, :].astype(bf16)
        packed[i, chip:, :] = jnp.concatenate([d_rows[0:side], d_rows[side:]], axis=1)

        @pl.when(x != i)
        def send(i=i):
            remote(packed.at[i], arrived.at[x], psem.at[0, i], psem.at[1, x], "x", i).start()

    arrived[x] = packed[x]

    def close_first(s):
        m_rings[s].finish()
        for copy in e_rings[s].both:
            copy.wait_recv()
        sent_all(m_rings[s].both + e_rings[s].both)
        for e, into in enumerate((m_carry, m_early)):
            load(landed[s].at[e, :, :, held_l[s]], into[s].at[:, :, held_l[s]], s, 9 + 3 * e)
            load(landed[s].at[e, two(e), :, held_e], into[s].at[two(e), :, held_e], s, 10 + 3 * e)
            load(plain[s].at[e], into[s].at[two(1 - e), :, held_e], s, 11 + 3 * e)

    def sum_first(s):
        for k in (2, 3, 6, 7, 9, 10, 11, 12, 13, 14):
            loads[s, k].wait()
        for q in range(4):
            m_mine[s][q] = (
                m_mine[s][q].astype(f32) + m_carry[s][q].astype(f32) + m_early[s][q].astype(f32)
            ).astype(bf16)

    def add_to(carry, early, mine, s, me):
        def add(h):
            at = slice(h * shard, (h + 1) * shard)
            k = turned(me, (1, 3)[h])
            carry[s][at, :] = mine[s][k, at, :] + early[s][at, :]

        return add

    m2_rings = [second_step(s, m_mine, m2_early, m2_late, m2_carry, 2) for s in range(2)]
    close_first(1)
    layer_out[y] = (mid + total_of(1, mix_part, m_crossed, m_sent)).astype(bf16)
    out_shared = share(1, lambda k: layer_out.at[k])
    turned_rows[...] = jnp.transpose(normed[...])
    for s in range(2):
        o_rings[s].middle(join_terms(s, o_lanes, o_carry, o_early))
    sum_first(1)
    m2_rings[1].start()
    close_first(0)
    sum_first(0)
    m2_rings[0].start()
    out_shared.forward()
    for d in (1, 2, 3):
        k = turned(x, d)
        copy = remote(packed.at[k], arrived.at[k], psem.at[0, k], psem.at[1, k], "x", k)
        copy.wait_recv()
        waits.append(copy)
    rotation = table[...].reshape(chip, 128)
    cosine = jnp.concatenate([rotation[:, 0:64]] * 4, axis=1)
    sine = jnp.concatenate([rotation[:, 64:128]] * 4, axis=1)

    def side_by_side(lanes):
        return jnp.concatenate([arrived[h, 0:chip, lanes].astype(f32) for h in range(4)], axis=1)

    d_lin = jnp.concatenate(
        [
            rope(side_by_side(slice(0, 64)), cosine, -sine).astype(bf16),
            rope(side_by_side(slice(64, 128)), cosine, -sine).astype(bf16),
            jnp.concatenate(
                [
                    jnp.concatenate([arrived[h, chip:, lanes] for h in range(4)], axis=1)
                    for lanes in (slice(0, 64), slice(64, 128))
                ],
                axis=0,
            ),
        ],
        axis=1,
    )
    terms[:, :, :, 0 : 3 * wide] = (
        dot_nn(turned_rows[...], d_lin).astype(bf16).reshape(4, 4, width // 16, 3 * wide)
    )
    a_rings = [first_step(s, terms, a_lanes, apart(a_early), apart(a_late), apart(a_carry), 4)[0] for s in range(2)]
    for ring in a_rings:
        ring.start()
    sent_all([*d_crossed.values(), *d_sent.values(), shared.right, shared.left, shared.right_on, shared.left_on, *forward])
    partial = d_branch
    lin = [d_lin[0:side], d_lin[side:]]
    gain_one_part = jnp.zeros((1, width), f32)
    for k in range(2):
        term = dot_nt(lin[k], weights_of(0, 3))
        partial[k] = term.astype(bf16).reshape(4, quarter, width)
        gain_one_part = gain_one_part + jnp.sum(
            term * normed[k * side : (k + 1) * side, :].astype(f32), axis=0, keepdims=True
        )
    crossed = cross(2, partial.at[1 - c])
    sent = along(2, partial.at[c], crossed)
    for s, me in ((1, z), (0, x)):
        m2_rings[s].middle(add_to(m2_carry, m2_early, m_mine, s, me))
    both = jnp.concatenate([gain_one_part / gain_rows[0:1, :], gain_two_part, jnp.zeros((6, width), f32)], axis=0)
    for k in range(16):
        gain_part[k] = both[:, k * 128 : (k + 1) * 128]

    def pass_on(r, src_of, into, axis, me):
        return {
            d: begin(remote(src_of(turned(me, d)), into.at[d - 1], gsem.at[r, 0, d - 1], gsem.at[r, 1, d - 1], axis, turned(me, d)))
            for d in (2, 1, 3)
        }

    moved = pass_on(0, lambda k: gain_part.at[some(k, 4)], gain_z, "shard", z)
    o_sent = []
    for s in range(2):
        sum_terms(o_rings[s], s, o_lanes, o_mine, o_late)
        o_sent.append(direct(1, s, o_mine, o2_in))
    own = own_tokens[...].astype(f32)
    own_scale = lax.rsqrt(jnp.mean(own * own, axis=-1, keepdims=True) + epsilon)
    own_unit = own * own_scale

    for s in range(2):
        a_rings[s].middle(join_terms(s, a_lanes, a_carry, a_early))
    for d in (1, 3, 2):
        moved[d].wait_recv()
    gain_part[some(z, 4)] += gain_z[0] + gain_z[1] + gain_z[2]
    moved = pass_on(1, lambda k: gain_part.at[4 * z + k], gain_x, "x", x)

    d_one = total_of(2, partial.at[c], crossed, sent)
    scaled = d_one * gain_rows[0:1, :]
    input_grad[y] = (
        d_mid[...] + own_scale * (scaled - own_unit * jnp.mean(scaled * own_unit, axis=-1, keepdims=True))
    ).astype(bf16)
    in_shared = share(2, lambda k: input_grad.at[k])
    a_sent = []
    for s in range(2):
        sum_terms(a_rings[s], s, a_lanes, a_mine, a_late)
        a_sent.append(direct(0, s, a_mine, a2_in))

    for s, me in ((0, x), (1, z)):
        m2_rings[s].finish()
        for held, lanes in ((held_e, e_lanes[s]), (held_l[s], l_lanes[s])):
            m2_mine[:, lanes] = (
                m_mine[s][me, :, held].astype(f32)
                + m2_late[s][0, :, held].astype(f32) + m2_late[s][1, :, held].astype(f32)
            ).astype(bf16)
    mine_rows, theirs_rows = some(c, shard), some(1 - c, shard)
    m_last = begin(remote(m2_mine.at[theirs_rows], swapped_m.at[c], outsem.at[0, 0], outsem.at[0, 1], "core", 1 - c))
    swapped_m[c] = m2_mine[mine_rows, :]
    for d in (1, 3, 2):
        moved[d].wait_recv()
    gain_y[3] = gain_part[4 * z + x] + gain_x[0] + gain_x[1] + gain_x[2]
    moved = pass_on(2, lambda k: gain_y.at[3], gain_y, "tensor", y)
    in_shared.forward()
    for d in (1, 3, 2):
        moved[d].wait_recv()
    gain_c[0] = (gain_y[0] + gain_y[1]) + (gain_y[2] + gain_y[3])
    between = begin(remote(gain_c.at[0], gain_c.at[1], gsem.at[3, 0, 0], gsem.at[3, 1, 0], "core", 1 - c))
    for s in range(2):
        direct_sum(o_sent[s], s, o_mine, o2_in, o_lanes)
    for s in range(2):
        direct_sum(a_sent[s], s, a_mine, a2_in, a_lanes)
    a_last = begin(remote(a2_mine.at[theirs_rows], swapped_a.at[c], outsem.at[1, 0], outsem.at[1, 1], "core", 1 - c))
    swapped_a[c] = a2_mine[mine_rows, :]
    between.wait_recv()
    gain_out[...] = gain_c[0] + gain_c[1]
    a_last.wait_recv()
    m_last.wait_recv()
    out_shared.finish()
    in_shared.finish()
    for copy in waits:
        copy.wait_send()


def backward_pass(
    d_part, mix_part, middle, tokens, cot, gain_rows, weights, low, normed, packed, attended, lse, start, table, mlp_terms, *early
):
    chip, width = normed.shape
    seq = start.shape[1]
    quarter, shard = chip // 8, width // 32
    columns, hidden = weights.shape[3], mlp_terms.shape[3] // 3
    first_cut = early[0].shape[2]
    m_split = first_cut + (3 * hidden - 2 * first_cut) // 16 * 9 // 128 * 128
    m_parts = (m_split, 3 * hidden - m_split)
    sds = jax.ShapeDtypeStruct
    dma = pltpu.SemaphoreType.DMA
    vmem = pltpu.VMEM

    def step_buffers(n):
        return (
            vmem((2, 4, width // 16, n), bf16),
            vmem((2, 2, 4, width // 16, n), bf16),
            vmem((2, 4, width // 16, n), bf16),
            vmem((2, 4, width // 16, n), bf16),
            vmem((2, 3, width // 16, n), bf16),
        )

    return pl.pallas_call(
        backward_kernel,
        out_shape=(
            sds((4, quarter, width), bf16),
            sds((4, quarter, width), bf16),
            sds((2, shard, 3 * hidden), bf16),
            sds((2, shard, columns), bf16),
            sds((8, 128), f32),
            *(sds((2, 4, width // 16, n), bf16) for n in m_parts),
        ),
        in_specs=[HBM] * 11 + [VMEM] * 2 + [HBM] * 6,
        out_specs=(VMEM,) * 5 + (HBM,) * 2,
        scratch_shapes=[
            *(vmem(a.shape[1:], a.dtype) for a in (d_part, mix_part)),
            vmem(middle.shape, middle.dtype),
            vmem((quarter, width), bf16),
            vmem((quarter, width), bf16),
            *(vmem(a.shape, a.dtype) for a in (gain_rows, weights, low, normed, packed, attended, table)),
            *[vmem((seq, HEAD_DIM), bf16)] * 3,
            vmem((2, 4, quarter, width), bf16),
            vmem((quarter, width), f32),
            vmem((2, 4, quarter, width), bf16),
            vmem((2, 3, quarter, width), bf16),
            vmem((2, 3, quarter, width), bf16),
            vmem((4, chip, HEAD_DIM), bf16),
            vmem((4, chip, HEAD_DIM), bf16),
            vmem((HEAD_DIM, seq), bf16),
            vmem((seq, HEAD_DIM), f32),
            vmem((seq, HEAD_DIM), f32),
            vmem((4, chip * 3 // 2, 128), bf16),
            vmem((4, chip * 3 // 2, 128), bf16),
            vmem((width, chip), bf16),
            vmem((4, 4, width // 16, columns), bf16),
            *(vmem((4, width // 16, n), bf16) for _ in range(3) for n in m_parts),
            *(vmem((width // 16, n), bf16) for n in m_parts),
            *(vmem((2, width // 16, n), bf16) for n in m_parts),
            *(vmem((width // 16, n), bf16) for n in m_parts),
            vmem((width // 16, 3 * hidden), bf16),
            *(a for n in (3 * columns // 8, columns // 8) for a in step_buffers(n)),
            vmem((width // 16, columns), bf16),
            vmem((16, 8, 128), f32),
            vmem((4, 8, 128), f32),
            vmem((2, 8, 128), f32),
            vmem((3, 8, 128), f32),
            vmem((3, 4, 8, 128), f32),
            dma((3, 2, 4)), dma((3, 2, 3)), dma((3, 2, 4)), dma((2, 4)), dma((2, 3)), dma((2, 4)),
            dma((10, 2, 6)), dma((2, 15)), dma((4, 2, 3)), dma((2, 2)), dma((12,)), dma((2, 2, 2, 3)),
        ],
        compiler_params=pltpu.CompilerParams(
            collective_id=1, has_side_effects=True, vmem_limit_bytes=62 << 20
        ),
    )(
        d_part, mix_part, middle, tokens, cot, gain_rows, weights, low, normed, packed, attended, lse, start, table, mlp_terms, *early
    )


def finish_kernel(
    out_hbm, grad_hbm, mlp_hbm, attn_hbm, gain_hbm,
    layer_out, input_grad, gain_one, gain_two, grad_q, grad_k, grad_v, grad_o, grad_gate, grad_up, grad_down,
    out_in, grad_in, mlp_in, attn_in, gain_in, sem,
):
    c = lax.axis_index("core")
    sources = (gain_hbm, attn_hbm, mlp_hbm, out_hbm, grad_hbm)
    copies = [
        pltpu.make_async_copy(src, dst, sem.at[k])
        for k, (src, dst) in enumerate(zip(sources, (gain_in, attn_in, mlp_in, out_in, grad_in)))
    ]
    for copy in copies:
        copy.start()
    for copy in copies:
        copy.wait()
    shard, wide = grad_q.shape[0], grad_q.shape[1] // 2
    layer_out[...] = out_in[...].reshape(layer_out.shape)
    input_grad[...] = grad_in[...].reshape(input_grad.shape)
    for k, out in enumerate((gain_one, gain_two)):
        out[...] = jnp.where(c == 0, gain_in[k : k + 1, 0:shard], gain_in[k : k + 1, shard : 2 * shard])
    span = grad_gate.shape[1] // 4
    for e in range(2):
        for k, out in enumerate((grad_q, grad_k, grad_v, grad_o)):
            out[:, e * wide : (e + 1) * wide] = attn_in[e, :, k * wide : (k + 1) * wide].astype(f32)
        for g in range(2):
            lanes = slice((2 * e + g) * span, (2 * e + g + 1) * span)
            for k, out in enumerate((grad_gate, grad_up, grad_down)):
                out[:, lanes] = mlp_in[e, :, (3 * g + k) * span : (3 * g + k + 1) * span].astype(f32)


def finish(layer_out, input_grad, mlp_grads, attn_grads, gains):
    quarters, quarter, width = layer_out.shape
    rows = quarters * quarter
    _, shard, columns = attn_grads.shape
    hidden = mlp_grads.shape[2] // 3
    sds = jax.ShapeDtypeStruct
    narrow, broad = sds((shard, columns // 2), f32), sds((shard, 2 * hidden), f32)
    return pl.pallas_call(
        finish_kernel,
        out_shape=(
            *[sds((rows, width), bf16)] * 2,
            *[sds((1, shard), f32)] * 2,
            *[narrow] * 4,
            *[broad] * 3,
        ),
        in_specs=[HBM] * 5,
        scratch_shapes=[
            *(pltpu.VMEM(a.shape, a.dtype) for a in (layer_out, input_grad, mlp_grads, attn_grads, gains)),
            pltpu.SemaphoreType.DMA((5,)),
        ],
        compiler_params=pltpu.CompilerParams(vmem_limit_bytes=60 << 20),
    )(layer_out, input_grad, mlp_grads, attn_grads, gains)


def angle_table(positions):
    half = HEAD_DIM // 2
    frequency = rope_base ** (-(jnp.arange(half, dtype=f32) * 2.0) / HEAD_DIM)
    angle = positions.astype(f32)[:, None] * jnp.tile(frequency, 4)[None, :]
    lane = jnp.arange(4 * half)
    sign = jnp.where(lane < 3 * half, -1.0, 1.0)[None, :]
    return jnp.where((lane < 2 * half)[None, :], jnp.cos(angle), jnp.sin(angle) * sign)


def body(
    tokens_in,
    cotangent,
    segments,
    positions,
    norm1_gain,
    q_weight,
    k_weight,
    v_weight,
    o_weight,
    norm2_gain,
    gate_weight,
    up_weight,
    down_weight,
):
    rows, width = tokens_in.shape
    quarter = rows // 4
    (
        full, table, normed_one, packed, low, attended, middle, mixed, d_normed, terms, *early, gain_rows, start, lse,
    ) = forward_pass(
        q_weight, k_weight, v_weight, o_weight.T, gate_weight, up_weight, down_weight.T,
        norm1_gain[None], norm2_gain[None], tokens_in, cotangent, angle_table(positions), segments,
    )
    split = (2, 4, quarter, width)
    *results, _, _ = backward_pass(
        d_normed.reshape(split), mixed.reshape(split), middle, tokens_in, cotangent, gain_rows, full,
        low, normed_one, packed, attended, lse, start, table, terms, *early,
    )
    (
        layer_out, input_grad, gain_one, gain_two, grad_q, grad_k, grad_v, grad_o, grad_gate, grad_up, grad_down,
    ) = finish(*results)
    return (
        layer_out, input_grad, gain_one[0], grad_q, grad_k, grad_v, grad_o.T, gain_two[0], grad_gate, grad_up, grad_down.T,
    )


def solution(mesh):
    apart = Mesh(mesh.devices.reshape(4, 4, 2, 4), ("shard", "x", "core", "tensor"))
    tokens = ("shard", "x", "core")
    placed = (
        P(tokens, None),
        P(tokens, None),
        P("shard", None),
        P(tokens),
        P(tokens),
        P(tokens, "tensor"),
        P(tokens, "tensor"),
        P(tokens, "tensor"),
        P("tensor", tokens),
        P(tokens),
        P(tokens, "tensor"),
        P(tokens, "tensor"),
        P("tensor", tokens),
    )
    return jax.shard_map(
        body,
        mesh=apart,
        in_specs=placed,
        out_specs=(
            P(tokens, None),
            P(tokens, None),
            P(tokens),
            P(tokens, "tensor"),
            P(tokens, "tensor"),
            P(tokens, "tensor"),
            P("tensor", tokens),
            P(tokens),
            P(tokens, "tensor"),
            P(tokens, "tensor"),
            P("tensor", tokens),
        ),
        check_vma=False,
    )
```

```python
import jax
import jax.numpy as jnp
import numpy as np
from jax import lax
from jax.experimental import pallas as pl
from jax.experimental.pallas import tpu as pltpu
from jax.sharding import Mesh
from jax.sharding import PartitionSpec as P

HEAD_DIM = 64
BLOCK = 512

epsilon = 1e-05
rope_base = 130000.0
masked_low = -1000000000.0

f32 = jnp.float32
bf16 = jnp.bfloat16
MESH = pl.DeviceIdType.MESH
VMEM = pl.BlockSpec(memory_space=pltpu.VMEM)
HBM = pl.BlockSpec(memory_space=pl.ANY)


def dot_nn(a, b):
    return lax.dot_general(a, b, (((1,), (0,)), ((), ())), preferred_element_type=f32)


def dot_nt(a, b):
    return lax.dot_general(a, b, (((1,), (1,)), ((), ())), preferred_element_type=f32)


def place():
    return tuple(lax.axis_index(a) for a in ("shard", "x", "core", "tensor"))


def turned(index, step):
    return lax.rem(index + step, 4)


def some(index, size):
    return pl.ds(pl.multiple_of(index * size, size), size)


def greet():
    barrier = pltpu.get_barrier_semaphore()
    count = 0
    for axis in ("core", "x", "shard", "tensor"):
        me = lax.axis_index(axis)
        peers = [1 - me] if axis == "core" else [turned(me, d) for d in (1, 2, 3)]
        for peer in peers:
            pl.semaphore_signal(barrier, inc=1, device_id={axis: peer}, device_id_type=MESH)
            count += 1
    return count


def meet(count):
    pl.semaphore_wait(pltpu.get_barrier_semaphore(), count)


def remote(src, dst, send, recv, axis, index):
    return pltpu.make_async_remote_copy(
        src_ref=src, dst_ref=dst, send_sem=send, recv_sem=recv, device_id={axis: index}, device_id_type=MESH
    )


class Gather:
    def __init__(self, axis, me, block, half, sems, waits):
        self.axis, self.me, self.block, self.half, self.sems, self.waits = axis, me, block, half, sems, waits

    def send(self, ref, slot, step):
        copy = remote(ref, ref, self.sems.at[0, slot], self.sems.at[1, slot], self.axis, turned(self.me, step))
        copy.start()
        self.waits.append(copy)
        return copy

    def start(self):
        mine = self.block(self.me)
        self.right, self.left = self.send(mine, 0, 1), self.send(mine, 1, 3)

    def forward(self):
        self.right.wait_recv()
        self.right_on = self.send(self.half(turned(self.me, 3), 0), 2, 1)
        self.left.wait_recv()
        self.left_on = self.send(self.half(turned(self.me, 1), 1), 3, 3)

    def finish(self):
        self.right_on.wait_recv()
        self.left_on.wait_recv()


class Reduce:
    def __init__(self, axis, me, half, early, late, carried, sems, waits):
        self.axis, self.me, self.half, self.sems, self.waits = axis, me, half, sems, waits
        self.early, self.late, self.carried = early, late, carried

    def send(self, src, dst, slot, step):
        copy = remote(src, dst, self.sems.at[0, slot], self.sems.at[1, slot], self.axis, turned(self.me, step))
        copy.start()
        self.waits.append(copy)
        return copy

    def start(self):
        far, right, left = turned(self.me, 2), turned(self.me, 1), turned(self.me, 3)
        self.far = [
            self.send(self.half(far, 0), self.early(0), 0, 1),
            self.send(self.half(far, 1), self.early(1), 1, 3),
        ]
        self.plain = [
            self.send(self.half(right, 1), self.late(0, 1), 2, 1),
            self.send(self.half(left, 0), self.late(1, 0), 3, 3),
        ]

    def join(self, add):
        for h in range(2):
            self.far[h].wait_recv()
            add(h)

    def pass_on(self):
        self.both = [self.send(self.carried(h), self.late(h, h), 4 + h, step) for h, step in ((0, 1), (1, 3))]

    def middle(self, add):
        self.join(add)
        self.pass_on()

    def finish(self):
        for copy in self.plain + self.both:
            copy.wait_recv()


def rope(vectors, table_cos, table_sin):
    n = vectors.shape[1]
    lane = lax.broadcasted_iota(jnp.int32, vectors.shape, 1)
    other = jnp.where(
        lax.rem(lane, HEAD_DIM) < HEAD_DIM // 2,
        pltpu.roll(vectors, n - HEAD_DIM // 2, 1),
        pltpu.roll(vectors, HEAD_DIM // 2, 1),
    )
    return vectors * table_cos + other * table_sin


def masked(raw, begin, j, i, diagonal):
    key = lax.broadcasted_iota(jnp.int32, raw.shape, 0)
    allowed = key >= begin - j * BLOCK
    if diagonal:
        allowed = allowed & (key <= lax.broadcasted_iota(jnp.int32, raw.shape, 1))
    return jnp.where(allowed, raw, masked_low)


def forward_kernel(
    wq, wk, wv, wo, wg, wu, wd, gain_one, gain_two, tokens, cot, positions, frequency, seg_row,
    full_out, table_out, normed_out, packed_out, low_out, attended_out, middle_out, mixed_out, d_normed_out, terms_out,
    far_z, far_x, plain_z, plain_x, gain_rows, start, lse,
    full, normed, table, low, attended_t, middle, normed_two,
    rotary, gains, attn_give, mlp_give, gain_all, chip_tokens, packed, arrived, keys, value_t, scaled_q,
    head_out, low_in, own, other, pair, near,
    mlp_full, cot_held, cot_t, normed_t, both, made_hidden, made, d_held, mixed_held, d_hidden_held,
    local, core_sem, out_sem, made_sem, grad_sem, ring_sem, gain_sem, xsem, lsem, csem, ysem, asem, fsem,
):
    z, x, c, y = place()
    half = wq.shape[1] // 2
    shard = wq.shape[0]
    hidden = wg.shape[1] // 2
    groups = 2
    span = hidden // groups
    chip, width = normed.shape
    waits = []
    count = greet()

    at = some(c, shard)
    lane = lax.broadcasted_iota(jnp.int32, (8, 128), 1) // (2 * shard // 2)
    both_gains = jnp.concatenate(
        [gain_one[...].astype(f32), gain_two[...].astype(f32), jnp.zeros((6, shard), f32)], axis=0
    )
    both_gains = jnp.where(lane == c, jnp.concatenate([both_gains, both_gains], axis=1), 0.0)
    gains[...] = jnp.concatenate([both_gains, jnp.zeros((8, 128), f32)], axis=0).astype(bf16)
    for k, w in enumerate((wq, wk, wv, wo)):
        attn_give[:, k * half : (k + 1) * half] = w[:, some(1 - c, half)]
        full[z, x, at, k * half : (k + 1) * half] = w[:, some(c, half)]
    for k, w in enumerate((wg, wu, wd)):
        for g in range(groups):
            lanes = slice((3 * g + k) * span, (3 * g + k + 1) * span)
            mlp_give[:, lanes] = w[:, some((1 - c) * groups + g, span)]
            mlp_full[z, x, at, lanes] = w[:, some(c * groups + g, span)]
    place_of = jnp.broadcast_to(positions[...].astype(f32), (128, positions.shape[1]))
    angle = jnp.transpose(place_of) * frequency[...]
    lane = lax.broadcasted_iota(jnp.int32, angle.shape, 1)
    sine_part = jnp.where(lane < 96, -jnp.sin(angle), jnp.sin(angle))
    rotary[...] = jnp.where(lane < 64, jnp.cos(angle), sine_part)
    meet(count)
    pairs = [(gains, gains, gain_all.at[z, x, c]), (None, attn_give, full.at[z, x, at, :])]
    pairs += [(None, mlp_give, mlp_full.at[z, x, at, :])]
    pairs += [(a, a, b.at[c]) for a, b in ((tokens, chip_tokens), (rotary, table), (cot, cot_held))]
    inside, across = [], []
    for k, (mine, theirs, there) in enumerate(pairs):
        inside.append(pltpu.make_async_copy(mine, there, local.at[k]) if mine is not None else None)
        across.append(remote(theirs, there, core_sem.at[0, k], core_sem.at[1, k], "core", 1 - c))
        across[-1].start()
        if mine is not None:
            inside[-1].start()
    waits += across
    kept = []

    def keep(src, dst):
        kept.append(pltpu.make_async_copy(src, dst, out_sem.at[len(kept)]))
        kept[-1].start()

    def here(ks):
        for k in ks:
            if inside[k] is not None:
                inside[k].wait()
            across[k].wait_recv()

    def spread(src, r, axis, me):
        copies = []
        for d in (1, 2, 3):
            copies.append(remote(src, src, gain_sem.at[0, r, d - 1], gain_sem.at[1, r, d - 1], axis, turned(me, d)))
            copies[-1].start()
        waits.extend(copies)
        return copies

    all_rings = []

    def ring(axis, block, half_of):
        all_rings.append(Gather(axis, x if axis == "x" else z, block, half_of, ring_sem.at[len(all_rings)], waits))
        return all_rings[-1]

    def half_rows(h):
        return pl.ds(h * shard, shard)

    def both_of(p):
        return pl.ds(2 * p, 2)

    def first_along(axis, array, lanes):
        if axis == "x":
            return ring("x", lambda k: array.at[z, k, :, lanes], lambda k, h: array.at[z, k, half_rows(h), lanes])
        return ring("shard", lambda k: array.at[k, x, :, lanes], lambda k, h: array.at[k, x, half_rows(h), lanes])

    def then_along(axis, array, lanes):
        if axis == "x":
            return [
                ring("x", lambda k, p=p: array.at[both_of(p), k, :, lanes], lambda k, h, p=p: array.at[2 * p + h, k, :, lanes])
                for p in range(2)
            ]
        return [
            ring("shard", lambda k, p=p: array.at[k, both_of(p), :, lanes], lambda k, h, p=p: array.at[k, 2 * p + h, :, lanes])
            for p in range(2)
        ]

    qkv_a, qkv_b, out_a = pl.ds(0, 3 * half // 2), pl.ds(3 * half // 2, 3 * half // 2), pl.ds(3 * half, half)
    late_a = 3 * span * 7 // 12 // 128 * 128
    mlp_a1, mlp_b1 = pl.ds(0, 3 * span // 2), pl.ds(3 * span // 2, 3 * span // 2)
    mlp_a2, mlp_b2 = pl.ds(3 * span, late_a), pl.ds(3 * span + late_a, 3 * span - late_a)
    ax, az = first_along("x", full, qkv_a), then_along("shard", full, qkv_a)
    bz, bx = first_along("shard", full, qkv_b), then_along("x", full, qkv_b)
    ox, oz = first_along("x", full, out_a), then_along("shard", full, out_a)
    mx1, mz1 = first_along("x", mlp_full, mlp_a1), then_along("shard", mlp_full, mlp_a1)
    nz1, nx1 = first_along("shard", mlp_full, mlp_b1), then_along("x", mlp_full, mlp_b1)
    mx2, mz2 = first_along("x", mlp_full, mlp_a2), then_along("shard", mlp_full, mlp_a2)
    nz2, nx2 = first_along("shard", mlp_full, mlp_b2), then_along("x", mlp_full, mlp_b2)

    def start_all(rings):
        for one in rings:
            one.start()

    def forward_all(rings):
        for one in rings:
            one.forward()

    def finish_all(rings):
        for one in rings:
            one.finish()

    here((0,))
    gain_x = spread(gain_all.at[z, x], 0, "x", x)
    here((1,))
    start_all((ax, bz))
    here((2,))
    start_all((mx1, nz1))
    for copy in gain_x:
        copy.wait_recv()
    gain_z = spread(gain_all.at[z], 1, "shard", z)
    forward_all((ax, bz))
    ox.start()
    forward_all((mx1, nz1))
    ax.finish()
    start_all(az)
    bz.finish()
    start_all(bx)
    ox.forward()

    for copy in gain_z:
        copy.wait_recv()
    for i in range(16):
        two = (gain_all[i // 4, i % 4, 0] + gain_all[i // 4, i % 4, 1]).astype(f32)
        gain_rows[:, pl.ds(i * 128, 128)] = two[0:8, :]
    here((3, 4))

    def norm(i, unused):
        values = chip_tokens[i // 4, some(lax.rem(i, 4), 64), :].astype(f32)
        scale = lax.rsqrt(jnp.mean(values * values, axis=-1, keepdims=True) + epsilon)
        normed[some(i, 64), :] = ((values * scale) * gain_rows[0:1, :]).astype(bf16)
        return unused

    lax.fori_loop(0, chip // 64, norm, 0)
    keep(normed, normed_out)
    keep(table, table_out)
    row = seg_row[...].astype(f32)
    begins = [jnp.zeros((1, BLOCK), f32)] * 4
    for i in range(4):
        column = jnp.transpose(jnp.broadcast_to(row[:, i * BLOCK : (i + 1) * BLOCK], (128, BLOCK)))[:, 0:1]
        for j in range(i, 4):
            earlier = column < row[:, j * BLOCK : (j + 1) * BLOCK]
            begins[j] = begins[j] + jnp.sum(jnp.where(earlier, 1.0, 0.0), axis=0, keepdims=True)
    for i in range(4):
        start[:, i * BLOCK : (i + 1) * BLOCK] = begins[i].astype(jnp.int32)
    forward_all((az[0], bx[0], az[1], bx[1]))
    start_all((mx2, nz2))
    ox.finish()
    start_all(oz)
    mx1.finish()
    start_all(mz1)
    finish_all(az + bx)

    wide = 4 * HEAD_DIM

    def weights(k):
        return full[:, :, :, k * wide : (k + 1) * wide].reshape(width, wide)

    rotation = table[...].reshape(chip, 128)
    cosine = jnp.concatenate([rotation[:, 0:64]] * 8, axis=1)
    sine = jnp.concatenate([rotation[:, 64:128]] * 8, axis=1)
    pair_weights = full[:, :, :, 0 : 2 * wide].reshape(width, 2 * wide)
    turned_both = rope(dot_nn(normed[...], pair_weights), cosine, sine).astype(bf16)
    sent = []

    def scatter(part, first):
        for d in (2, 1, 3):
            k, sem = turned(x, d), first + d - 1
            sent.append(remote(packed.at[k, part], arrived.at[x, part], xsem.at[0, sem], xsem.at[1, sem], "x", k))
            sent[-1].start()

    for h in range(4):
        lanes = slice(h * HEAD_DIM, (h + 1) * HEAD_DIM)
        packed[h, 0:chip, :] = jnp.concatenate(
            [turned_both[:, lanes], turned_both[:, wide + lanes.start : wide + lanes.stop]], axis=1
        )
    scatter(pl.ds(0, chip), 0)
    token_values = dot_nn(normed[...], weights(2)).astype(bf16)
    for h in range(4):
        lanes = slice(h * HEAD_DIM, (h + 1) * HEAD_DIM)
        packed[h, chip:, :] = jnp.concatenate(
            [token_values[0 : chip // 2, lanes], token_values[chip // 2 :, lanes]], axis=1
        )
    scatter(pl.ds(chip, chip // 2), 3)
    waits += sent
    forward_all((mx2, nz2))
    forward_all(oz)
    nz1.finish()
    nx1[0].start()
    arrived[x] = packed[x]
    for copy in sent:
        copy.wait_recv()
    for k in range(4):
        rows = slice(k * chip, (k + 1) * chip)
        scaled_q[rows, :] = arrived[k, 0:chip, 0:64] * HEAD_DIM ** (-0.5)
        keys[rows, :] = arrived[k, 0:chip, 64:128]
        block = jnp.concatenate([arrived[k, chip:, 0:64], arrived[k, chip:, 64:128]], axis=0)
        value_t[:, rows] = jnp.transpose(block)
    keep(arrived, packed_out)

    for i in range(4):
        if i == 2:
            mz1[0].forward()
        if i == 3:
            mx2.finish()
            start_all(mz2)
        at = slice(i * BLOCK, (i + 1) * BLOCK)
        begin = start[:, at]
        mine = scaled_q[at, :]

        def step(j, state, diagonal=False):
            peak, total, summed = state
            scores = masked(dot_nt(keys[some(j, BLOCK), :], mine), begin, j, i, diagonal)
            new = jnp.maximum(peak, jnp.max(scores, axis=0, keepdims=True))
            weight = jnp.exp(scores - new)
            factor = jnp.exp(peak - new)
            total = total * factor + jnp.sum(weight, axis=0, keepdims=True)
            summed = summed * factor + dot_nn(value_t[:, some(j, BLOCK)], weight.astype(bf16))
            return (new, total, summed)

        state = (
            jnp.full((1, BLOCK), masked_low, f32),
            jnp.zeros((1, BLOCK), f32),
            jnp.zeros((HEAD_DIM, BLOCK), f32),
        )
        state = step(i, state, True)
        peak, total, summed = lax.fori_loop(0, i, step, state) if i else state
        attended = summed / total
        attended_t[:, at] = attended
        lse[:, at] = peak + jnp.log(total)
        head_out[i] = jnp.transpose(attended).astype(bf16)

        @pl.when(x != i)
        def send(i=i):
            remote(head_out.at[i], low_in.at[x], lsem.at[0, i], lsem.at[1, x], "x", i).start()

    nz2.finish()
    nx1[1].start()
    nx1[0].forward()
    start_all(nx2)
    mz1[1].forward()
    low_in[x] = head_out[x]
    for d in (1, 2, 3):
        k = turned(x, d)
        copy = remote(head_out.at[k], low_in.at[k], lsem.at[0, k], lsem.at[1, k], "x", k)
        copy.wait_recv()
        waits.append(copy)
    low[...] = jnp.concatenate([low_in[h] for h in range(4)], axis=1)
    finish_all(oz)
    keep(full, full_out)
    keep(low, low_out)
    keep(attended_t, attended_out)

    side, quarter = chip // 2, chip // 8
    out_weights = weights(3)
    other[...] = dot_nt(low[some(1 - c, side), :], out_weights).astype(bf16).reshape(other.shape)
    crossed = {}
    for d in (2, 1, 3, 0):
        k = turned(y, d)
        crossed[d] = remote(other.at[k], pair.at[k], csem.at[0, d], csem.at[1, d], "core", 1 - c)
        crossed[d].start()
    own[...] = dot_nt(low[some(c, side), :], out_weights).reshape(own.shape)
    along = {}
    for d in (2, 1, 3):
        k = turned(y, d)
        crossed[d].wait_recv()
        crossed[d].wait_send()
        other[k] = (own[k] + pair[k].astype(f32)).astype(bf16)
        along[d] = remote(other.at[k], near.at[d - 1], ysem.at[0, d - 1], ysem.at[1, d - 1], "tensor", k)
        along[d].start()
    crossed[0].wait_recv()
    crossed[0].wait_send()
    here((5,))
    nx1[1].forward()
    cot_t[...] = jnp.transpose(cot_held[...].reshape(chip, width))
    mz2[0].forward()
    total = own[y] + pair[y].astype(f32)
    for d in (1, 3, 2):
        along[d].wait_recv()
        total = total + near[d - 1].astype(f32)
    waits += [*along.values()]
    mid = chip_tokens[c, some(y, quarter), :].astype(f32) + total
    middle[...] = mid
    keep(middle, middle_out)
    scale = lax.rsqrt(jnp.mean(mid * mid, axis=-1, keepdims=True) + epsilon)
    normed_two[c, y] = ((mid * scale) * gain_rows[1:2, :]).astype(bf16)
    share = Gather(
        "tensor", y, lambda k: normed_two.at[c, k], lambda k, h: normed_two.at[c, k, pl.ds(h * quarter // 2, quarter // 2)],
        asem, waits,
    )
    forward = []

    def forward_on(k):
        slot = normed_two.at[c, k]
        d = len(forward)
        forward.append(remote(slot, slot, fsem.at[0, d], fsem.at[1, d], "core", 1 - c))
        forward[-1].start()

    share.start()
    forward_on(y)

    def group(g, k):
        return mlp_full[:, :, :, (3 * g + k) * span : (3 * g + k + 1) * span].reshape(width, span)

    chip_cot = cot_held[...].reshape(chip, width)
    share.forward()
    forward_on(turned(y, 3))
    forward_on(turned(y, 1))
    share.finish()
    forward_on(turned(y, 2))
    mz2[1].forward()
    forward_all(nx2)
    finish_all(nx1 + mz1)
    d_hidden_held[...] = dot_nn(chip_cot, group(0, 2))
    for copy in forward:
        copy.wait_recv()
    waits += forward

    cut = far_z.shape[2]
    early_rings = [
        Reduce(
            "shard", z, lambda k, h: terms_out.at[k, both_of(h), :, pl.ds(0, cut)], lambda h: far_z.at[both_of(h)],
            lambda e, h: plain_z.at[e], None, grad_sem.at[0], waits,
        ),
        Reduce(
            "x", x, lambda k, h: terms_out.at[both_of(h), k, :, pl.ds(cut, cut)], lambda h: far_x.at[both_of(h)],
            lambda e, h: plain_x.at[e], None, grad_sem.at[1], waits,
        ),
    ]
    rows_two = normed_two[...].reshape(chip, width)
    normed_t[...] = jnp.transpose(rows_two)
    stores = {}
    for g in range(groups):
        if g == 1:
            finish_all(mz2 + nx2)
        gate = dot_nn(rows_two, group(g, 0))
        upper = dot_nn(rows_two, group(g, 1))
        d_hidden = dot_nn(chip_cot, group(g, 2)) if g else d_hidden_held[...]
        sigmoid = 1.0 / (1.0 + jnp.exp(-gate))
        silu = gate * sigmoid
        made_hidden[g] = (silu * upper).astype(bf16)
        both[g, :, 0:span] = (d_hidden * upper * (sigmoid * (1.0 + gate * (1.0 - sigmoid)))).astype(bf16)
        both[g, :, span : 2 * span] = (d_hidden * silu).astype(bf16)
        for k, (left, right) in enumerate(
            ((normed_t, both.at[g, :, 0:span]), (normed_t, both.at[g, :, span : 2 * span]), (cot_t, made_hidden.at[g]))
        ):
            if g == 1 and k == 2:
                stores[0, 2].wait()
            for q in range(4):
                term = dot_nn(left[q * (width // 4) : (q + 1) * (width // 4), :], right[...])
                made[k, q] = term.astype(bf16).reshape(made.shape[2:])
            stores[g, k] = pltpu.make_async_copy(
                made.at[k], terms_out.at[:, :, :, pl.ds((3 * g + k) * span, span)], made_sem.at[g, k]
            )
            stores[g, k].start()
            if g == 0 and k > 0:
                stores[g, k - 1].wait()
                early_rings[k - 1].start()
    for held, out, left, first, n in ((d_held, d_normed_out, both, 0, 2), (mixed_held, mixed_out, made_hidden, 2, 1)):
        for t in range(4):
            lanes = slice(t * (width // 4), (t + 1) * (width // 4))
            term = [
                dot_nt(
                    left[g],
                    mlp_full[t, :, :, (3 * g + first) * span : (3 * g + first + n) * span].reshape(width // 4, n * span),
                )
                for g in range(groups)
            ]
            held[:, lanes] = (term[0] + term[1]).astype(bf16)
        keep(held, out)
    for k in range(3):
        stores[groups - 1, k].wait()
    for ring in early_rings:
        for copy in ring.far + ring.plain:
            copy.wait_recv()
    for copy in kept:
        copy.wait()
    for copy in waits:
        copy.wait_send()


def forward_pass(wq, wk, wv, wo, wg, wu, wd, gain_one, gain_two, tokens, cot, positions, frequency, seg_row):
    rows, width = tokens.shape
    chip, quarter, seq = 2 * rows, rows // 4, seg_row.shape[1]
    columns, hidden = 2 * wq.shape[1], wg.shape[1] // 2
    sds = jax.ShapeDtypeStruct
    dma = pltpu.SemaphoreType.DMA
    vmem = pltpu.VMEM
    kept = (
        ((4, 4, width // 16, columns), bf16),
        ((chip, width), bf16),
        ((2, rows, 128), f32),
        ((chip, 4 * HEAD_DIM), bf16),
        ((HEAD_DIM, seq), f32),
        ((quarter, width), f32),
        ((2, 4, quarter, width), bf16),
    )
    full, normed, table, low, attended, middle, _ = (sds(*a) for a in kept)
    span = hidden // 2
    packed = (4, chip * 3 // 2, 128)
    return pl.pallas_call(
        forward_kernel,
        out_shape=(
            full,
            table,
            normed,
            sds(packed, bf16),
            low,
            attended,
            middle,
            sds((chip, width), bf16),
            sds((chip, width), bf16),
            sds((4, 4, width // 16, 3 * hidden), bf16),
            *[sds((4, width // 16, span), bf16)] * 2,
            *[sds((2, 2, width // 16, span), bf16)] * 2,
            sds((8, width), f32),
            sds((1, seq), jnp.int32),
            sds((1, seq), f32),
        ),
        in_specs=[VMEM] * 9 + [HBM] * 2 + [VMEM] * 3,
        out_specs=(HBM,) * 14 + (VMEM,) * 3,
        scratch_shapes=[
            *(vmem(*a) for a in kept),
            vmem((rows, 128), f32),
            vmem((16, 128), bf16),
            vmem((width // 32, columns), bf16),
            vmem((width // 32, 3 * hidden), bf16),
            vmem((4, 4, 2, 16, 128), bf16),
            vmem((2, rows, width), bf16),
            vmem(packed, bf16),
            vmem(packed, bf16),
            vmem((seq, HEAD_DIM), bf16),
            vmem((HEAD_DIM, seq), bf16),
            vmem((seq, HEAD_DIM), bf16),
            vmem((4, chip, HEAD_DIM), bf16),
            vmem((4, chip, HEAD_DIM), bf16),
            vmem((4, quarter, width), f32),
            vmem((4, quarter, width), bf16),
            vmem((4, quarter, width), bf16),
            vmem((3, quarter, width), bf16),
            vmem((4, 4, width // 16, 3 * hidden), bf16),
            vmem((2, rows, width), bf16),
            vmem((width, chip), bf16),
            vmem((width, chip), bf16),
            vmem((2, chip, 2 * span), bf16),
            vmem((2, chip, span), bf16),
            vmem((3, 4, 4, width // 16, span), bf16),
            vmem((chip, width), bf16),
            vmem((chip, width), bf16),
            vmem((chip, span), f32),
            dma((6,)), dma((2, 6)), dma((9,)), dma((2, 3)), dma((2, 2, 6)), dma((21, 2, 4)), dma((2, 2, 3)), dma((2, 6)), dma((2, 4)),
            dma((2, 4)), dma((2, 3)), dma((2, 4)), dma((2, 4)),
        ],
        compiler_params=pltpu.CompilerParams(
            collective_id=0, has_side_effects=True, vmem_limit_bytes=62 << 20
        ),
    )(wq, wk, wv, wo, wg, wu, wd, gain_one, gain_two, tokens, cot, positions, frequency, seg_row)


def backward_kernel(
    d_part_in, mix_part_in, middle_in, tokens_in, cot_in, gain_rows_in, weights_in, low_in, normed_in, packed_in, attended_in,
    lse, start, table_in, mlp_terms, far_z, far_x, plain_z, plain_x,
    layer_out, input_grad, swapped_m, swapped_a, gain_out, landed_z, landed_x,
    d_part, mix_part, middle, own_tokens, own_cot, gain_rows, weights, low, normed, qkv_packed, attended, table,
    queries, keys, values,
    d_branch, d_mid, pair, half_sum, near, heads, head_in, key_t, d_key, d_value, packed, arrived,
    turned_rows, terms, m_early_z, m_early_x, m_carry_z, m_carry_x, m_mine_z, m_mine_x,
    m2_early_z, m2_early_x, m2_late_z, m2_late_x, m2_carry_z, m2_carry_x, m2_mine,
    a_early, a_late, a_carry, a_mine, a2_in, o_early, o_late, o_carry, o_mine, o2_in, a2_mine,
    lin, gain_part, gain_y, gain_c, gain_x, gain_z,
    csem, ysem, asem, fsem, hsem, psem, rsem, local, gsem, outsem, in_sem, dsem,
):
    z, x, c, y = place()
    count = greet()
    quarter = middle.shape[0]
    mine_at = some(y, quarter)
    taken = {}
    for k, (name, src, dst) in enumerate(
        (
            ("d_part", d_part_in.at[c], d_part),
            ("middle", middle_in, middle),
            ("gain_rows", gain_rows_in, gain_rows),
            ("own_cot", cot_in.at[mine_at, :], own_cot),
            ("mix_part", mix_part_in.at[c], mix_part),
            ("packed", packed_in, qkv_packed),
            ("weights", weights_in, weights),
            ("low", low_in, low),
            ("attended", attended_in, attended),
            ("normed", normed_in, normed),
            ("table", table_in, table),
            ("own_tokens", tokens_in.at[mine_at, :], own_tokens),
        )
    ):
        taken[name] = pltpu.make_async_copy(src, dst, in_sem.at[k])
        taken[name].start()

    def take(*names):
        for name in names:
            taken[name].wait()

    meet(count)
    chip, width = normed.shape
    side = chip // 2
    wide = 4 * HEAD_DIM
    shard = width // 32
    a_split = a_mine.shape[3]
    cut = far_z.shape[2]
    others = mlp_terms.shape[3] - 2 * cut
    late_cut = m_mine_z.shape[2] - cut
    far, plain = (far_z, far_x), (plain_z, plain_x)
    landed, m_early, m_carry, m_mine = (landed_z, landed_x), (m_early_z, m_early_x), (m_carry_z, m_carry_x), (m_mine_z, m_mine_x)
    m2_early, m2_late, m2_carry = (m2_early_z, m2_early_x), (m2_late_z, m2_late_x), (m2_carry_z, m2_carry_x)
    e_lanes = (pl.ds(0, cut), pl.ds(cut, cut))
    l_lanes = (pl.ds(2 * cut, late_cut), pl.ds(2 * cut + late_cut, others - late_cut))
    held_e = pl.ds(0, cut)
    held_l = (pl.ds(cut, late_cut), pl.ds(cut, others - late_cut))
    o_split = o_mine.shape[3]
    a_lanes = (pl.ds(0, a_split), pl.ds(a_split, a_split))
    o_lanes = (pl.ds(2 * a_split, o_split), pl.ds(2 * a_split + o_split, o_split))
    waits = []

    def begin(copy):
        copy.start()
        waits.append(copy)
        return copy

    def sent_all(copies):
        for copy in copies:
            copy.wait_send()
        waits[:] = [w for w in waits if not any(w is copy for copy in copies)]

    def cross(r, part):
        return {
            d: begin(remote(part.at[turned(y, d)], pair.at[r % 2, turned(y, d)], csem.at[r, 0, d], csem.at[r, 1, d], "core", 1 - c))
            for d in (2, 1, 3, 0)
        }

    def along(r, part, crossed):
        sent = {}
        for d in (2, 1, 3):
            k = turned(y, d)
            crossed[d].wait_recv()
            half_sum[r % 2, d - 1] = part[k] + pair[r % 2, k]
            sent[d] = begin(remote(half_sum.at[r % 2, d - 1], near.at[r % 2, d - 1], ysem.at[r, 0, d - 1], ysem.at[r, 1, d - 1], "tensor", k))
        return sent

    def total_of(r, part, crossed, sent):
        crossed[0].wait_recv()
        total = part[y].astype(f32) + pair[r % 2, y].astype(f32)
        for d in (1, 3, 2):
            sent[d].wait_recv()
            total = total + near[r % 2, d - 1].astype(f32)
        return total

    def share(r, slot):
        cut = quarter // 2
        ring = Gather("tensor", y, slot, lambda k, h: slot(k).at[pl.ds(h * cut, cut)], asem.at[r], waits)
        ring.start()
        return ring

    def two(h):
        return pl.ds(2 * h, 2)

    def rows(h):
        return pl.ds(h * shard, shard)

    def apart(ref):
        return (ref.at[0], ref.at[1])

    def term_of(s, k, q, lanes):
        return terms[k, q, :, lanes[s]] if s == 0 else terms[q, k, :, lanes[s]]

    def join_terms(s, lanes, carry, early):
        def add(h):
            k = turned((z, x)[s], (1, 3)[h])
            for q in (2 * h, 2 * h + 1):
                carry[s, q] = term_of(s, k, q, lanes) + early[s, q]

        return add

    def sum_terms(ring, s, lanes, mine, late):
        ring.finish()
        for q in range(4):
            mine[s, q] = (
                term_of(s, (z, x)[s], q, lanes).astype(f32) + late[s, 0, q].astype(f32) + late[s, 1, q].astype(f32)
            ).astype(bf16)

    def direct(r, s, mine, into):
        axis, me = (("x", x), ("shard", z))[s]
        return [
            begin(remote(mine.at[s, turned(me, d)], into.at[s, d - 1], dsem.at[r, s, 0, d - 1], dsem.at[r, s, 1, d - 1], axis, turned(me, d)))
            for d in (2, 1, 3)
        ]

    def direct_sum(copies, s, mine, into, lanes):
        for copy in copies:
            copy.wait_recv()
        a2_mine[:, lanes[s]] = (
            (mine[s, (x, z)[s]].astype(f32) + into[s, 0].astype(f32))
            + (into[s, 1].astype(f32) + into[s, 2].astype(f32))
        ).astype(bf16)

    def first_step(s, source, split, early, late, carry, r):
        axis, me = (("shard", z), ("x", x))[s]
        columns = split[s]

        def half(k, h):
            return source.at[k, two(h), :, columns] if s == 0 else source.at[two(h), k, :, columns]

        return Reduce(
            axis, me, half, lambda h: early[s].at[two(h)], lambda e, h: late[s].at[e, two(h)],
            lambda h: carry[s].at[two(h)], rsem.at[r + s], waits,
        ), half

    def second_step(s, mine, early, late, carry, r):
        axis, me = (("x", x), ("shard", z))[s]
        return Reduce(
            axis, me, lambda k, h: mine[s].at[k, rows(h)], lambda h: early[s].at[rows(h)],
            lambda e, h: late[s].at[e, rows(h)], lambda h: carry[s].at[rows(h)], rsem.at[r + s], waits,
        )

    def group_ring(s, source_lanes, held, r):
        axis, me = (("shard", z), ("x", x))[s]

        def half(k, h):
            return mlp_terms.at[k, two(h), :, source_lanes] if s == 0 else mlp_terms.at[two(h), k, :, source_lanes]

        return Reduce(
            axis, me, half, lambda h: m_early[s].at[two(h), :, held], lambda e, h: landed[s].at[e, two(h), :, held],
            lambda h: m_carry[s].at[two(h), :, held], rsem.at[r + s], waits,
        )

    e_rings = [group_ring(s, e_lanes[s], held_e, 8) for s in range(2)]
    m_rings = [group_ring(s, l_lanes[s], held_l[s], 0) for s in range(2)]
    loads = {}

    def load(src, dst, s, k):
        loads[s, k] = pltpu.make_async_copy(src, dst, local.at[s, k])
        loads[s, k].start()

    d_crossed = cross(0, d_part_in.at[1 - c])
    for s, me in ((0, z), (1, x)):
        m_rings[s].start()
        for n, (rings, held) in enumerate(((e_rings, held_e), (m_rings, held_l[s]))):
            for h, k in ((0, turned(me, 1)), (1, turned(me, 3))):
                load(rings[s].half(k, h), m_carry[s].at[two(h), :, held], s, 4 * n + h)
                load(rings[s].half(me, h), m_mine[s].at[two(h), :, held], s, 4 * n + 2 + h)
        load(far[s], m_early[s].at[:, :, held_e], s, 8)
    m_crossed = cross(1, mix_part_in.at[1 - c])
    take("d_part", "mix_part")
    d_sent = along(0, d_part, d_crossed)
    take("middle", "gain_rows", "own_cot", "packed")
    mid = middle[...]
    scale = lax.rsqrt(jnp.mean(mid * mid, axis=-1, keepdims=True) + epsilon)
    unit = mid * scale
    for k in range(4):
        at = slice(k * chip, (k + 1) * chip)
        queries[at, :] = qkv_packed[k, 0:chip, 0:64] * HEAD_DIM ** (-0.5)
        block = qkv_packed[k, 0:chip, 64:128]
        keys[at, :] = block
        key_t[:, at] = jnp.transpose(block)
        values[at, :] = jnp.concatenate([qkv_packed[k, chip:, 0:64], qkv_packed[k, chip:, 64:128]], axis=0)
    d_key[...] = jnp.zeros_like(d_key)
    d_value[...] = jnp.zeros_like(d_value)
    def add_far(ring, s):
        def add(h):
            loads[s, 4 + h].wait()
            for q in (2 * h, 2 * h + 1):
                m_carry[s][q, :, held_l[s]] = m_carry[s][q, :, held_l[s]] + m_early[s][q, :, held_l[s]]

        ring.join(add)

    for s in range(2):
        for k in (0, 1, 8):
            loads[s, k].wait()
        for q in range(4):
            m_carry[s][q, :, held_e] = m_carry[s][q, :, held_e] + m_early[s][q, :, held_e]
        e_rings[s].pass_on()
    add_far(m_rings[1], 1)
    d_two = total_of(0, d_part, d_crossed, d_sent)
    gain_two_part = jnp.sum(d_two * unit, axis=0, keepdims=True)
    scaled = d_two * gain_rows[1:2, :]
    d_middle = own_cot[...].astype(f32) + scale * (
        scaled - unit * jnp.mean(scaled * unit, axis=-1, keepdims=True)
    )
    d_mid[...] = d_middle
    d_branch[c, y] = d_middle.astype(bf16)
    shared = share(0, lambda k: d_branch.at[c, k])
    forward = []

    def forward_on(k):
        slot, d = d_branch.at[c, k], len(forward)
        forward.append(begin(remote(slot, slot, fsem.at[0, d], fsem.at[1, d], "core", 1 - c)))

    forward_on(y)
    add_far(m_rings[0], 0)
    m_rings[0].pass_on()
    shared.forward()
    forward_on(turned(y, 3))
    forward_on(turned(y, 1))
    m_sent = along(1, mix_part, m_crossed)
    shared.finish()
    forward_on(turned(y, 2))
    for copy in forward:
        copy.wait_recv()
    branch = d_branch[...].reshape(chip, width)
    take("weights", "low", "attended", "normed", "table", "own_tokens")

    def weights_of(k, n):
        return weights[:, :, :, k * wide : (k + n) * wide].reshape(width, n * wide)

    d_heads = dot_nn(branch, weights_of(3, 1)).astype(bf16)
    for h in range(4):
        heads[h] = d_heads[:, h * HEAD_DIM : (h + 1) * HEAD_DIM]
    head_sent = {}
    for d in (2, 1, 3):
        k = turned(x, d)
        head_sent[d] = begin(remote(heads.at[k], head_in.at[x], hsem.at[0, d - 1], hsem.at[1, d - 1], "x", k))
    head_in[x] = heads[x]
    m_rings[1].pass_on()
    turned_rows[...] = jnp.transpose(branch)
    terms[:, :, :, 3 * wide : 4 * wide] = (
        dot_nn(turned_rows[...], low[...]).astype(bf16).reshape(4, 4, width // 16, wide)
    )
    o_rings = [first_step(s, terms, o_lanes, apart(o_early), apart(o_late), apart(o_carry), 6)[0] for s in range(2)]
    for ring in o_rings:
        ring.start()
    for d in (1, 3, 2):
        head_sent[d].wait_recv()


    for i in (3, 2, 1, 0):
        at = slice(i * BLOCK, (i + 1) * BLOCK)
        mine, d_out = queries[at, :], head_in[i]
        center = jnp.sum(jnp.transpose(d_out.astype(f32)) * attended[:, at], axis=0, keepdims=True)
        peak, first = lse[:, at], start[:, at]

        def step(j, d_query, diagonal=False):
            key_at = some(j, BLOCK)
            scores = masked(dot_nt(keys[key_at, :], mine), first, j, i, diagonal)
            weight = jnp.exp(scores - peak)
            d_prob = dot_nt(values[key_at, :], d_out)
            d_raw = (weight * (d_prob - center)).astype(bf16)
            d_key[key_at, :] += dot_nn(d_raw, mine)
            d_value[key_at, :] += dot_nn(weight.astype(bf16), d_out)
            return d_query + dot_nn(key_t[:, key_at], d_raw)

        d_query = step(i, jnp.zeros((HEAD_DIM, BLOCK), f32), True)
        d_query = lax.fori_loop(0, i, step, d_query) if i else d_query
        packed[i, 0:chip, :] = jnp.concatenate(
            [jnp.transpose(d_query * HEAD_DIM ** (-0.5)).astype(bf16), d_key[at, :].astype(bf16)], axis=1
        )
        d_rows = d_value[at, :].astype(bf16)
        packed[i, chip:, :] = jnp.concatenate([d_rows[0:side], d_rows[side:]], axis=1)

        @pl.when(x != i)
        def send(i=i):
            remote(packed.at[i], arrived.at[x], psem.at[0, i], psem.at[1, x], "x", i).start()

    arrived[x] = packed[x]

    def close_first(s):
        m_rings[s].finish()
        for copy in e_rings[s].both:
            copy.wait_recv()
        sent_all(m_rings[s].both + e_rings[s].both)
        for e, into in enumerate((m_carry, m_early)):
            load(landed[s].at[e, :, :, held_l[s]], into[s].at[:, :, held_l[s]], s, 9 + 3 * e)
            load(landed[s].at[e, two(e), :, held_e], into[s].at[two(e), :, held_e], s, 10 + 3 * e)
            load(plain[s].at[e], into[s].at[two(1 - e), :, held_e], s, 11 + 3 * e)

    def sum_first(s):
        for k in (2, 3, 6, 7, 9, 10, 11, 12, 13, 14):
            loads[s, k].wait()
        for q in range(4):
            m_mine[s][q] = (
                m_mine[s][q].astype(f32) + m_carry[s][q].astype(f32) + m_early[s][q].astype(f32)
            ).astype(bf16)

    def add_to(carry, early, mine, s, me):
        def add(h):
            at = slice(h * shard, (h + 1) * shard)
            k = turned(me, (1, 3)[h])
            carry[s][at, :] = mine[s][k, at, :] + early[s][at, :]

        return add

    m2_rings = [second_step(s, m_mine, m2_early, m2_late, m2_carry, 2) for s in range(2)]
    close_first(1)
    layer_out[y] = (mid + total_of(1, mix_part, m_crossed, m_sent)).astype(bf16)
    out_shared = share(1, lambda k: layer_out.at[k])
    turned_rows[...] = jnp.transpose(normed[...])
    for s in range(2):
        o_rings[s].middle(join_terms(s, o_lanes, o_carry, o_early))
    sum_first(1)
    m2_rings[1].start()
    close_first(0)
    sum_first(0)
    m2_rings[0].start()
    out_shared.forward()
    for d in (1, 2, 3):
        k = turned(x, d)
        copy = remote(packed.at[k], arrived.at[k], psem.at[0, k], psem.at[1, k], "x", k)
        copy.wait_recv()
        waits.append(copy)
    rotation = table[...].reshape(chip, 128)
    cosine = jnp.concatenate([rotation[:, 0:64]] * 4, axis=1)
    sine = jnp.concatenate([rotation[:, 64:128]] * 4, axis=1)

    def side_by_side(lanes):
        return jnp.concatenate([arrived[h, 0:chip, lanes].astype(f32) for h in range(4)], axis=1)

    d_lin = jnp.concatenate(
        [
            rope(side_by_side(slice(0, 64)), cosine, -sine).astype(bf16),
            rope(side_by_side(slice(64, 128)), cosine, -sine).astype(bf16),
            jnp.concatenate(
                [
                    jnp.concatenate([arrived[h, chip:, lanes] for h in range(4)], axis=1)
                    for lanes in (slice(0, 64), slice(64, 128))
                ],
                axis=0,
            ),
        ],
        axis=1,
    )
    terms[:, :, :, 0 : 3 * wide] = (
        dot_nn(turned_rows[...], d_lin).astype(bf16).reshape(4, 4, width // 16, 3 * wide)
    )
    a_rings = [first_step(s, terms, a_lanes, apart(a_early), apart(a_late), apart(a_carry), 4)[0] for s in range(2)]
    for ring in a_rings:
        ring.start()
    sent_all([*d_crossed.values(), *d_sent.values(), shared.right, shared.left, shared.right_on, shared.left_on, *forward])
    partial = d_branch
    lin[...] = d_lin.reshape(lin.shape)

    def token_part(k):
        term = dot_nt(lin[k], weights_of(0, 3))
        partial[k] = term.astype(bf16).reshape(4, quarter, width)
        return jnp.sum(term * normed[some(k, side), :].astype(f32), axis=0, keepdims=True)

    gain_one_part = token_part(1 - c)
    crossed = cross(2, partial.at[1 - c])
    gain_one_part = gain_one_part + token_part(c)
    sent = along(2, partial.at[c], crossed)
    for s, me in ((1, z), (0, x)):
        m2_rings[s].middle(add_to(m2_carry, m2_early, m_mine, s, me))
    both = jnp.concatenate([gain_one_part / gain_rows[0:1, :], gain_two_part, jnp.zeros((6, width), f32)], axis=0)
    for k in range(16):
        gain_part[k] = both[:, k * 128 : (k + 1) * 128]

    def pass_on(r, src_of, into, axis, me):
        return {
            d: begin(remote(src_of(turned(me, d)), into.at[d - 1], gsem.at[r, 0, d - 1], gsem.at[r, 1, d - 1], axis, turned(me, d)))
            for d in (2, 1, 3)
        }

    moved = pass_on(0, lambda k: gain_part.at[some(k, 4)], gain_z, "shard", z)
    o_sent = []
    for s in range(2):
        sum_terms(o_rings[s], s, o_lanes, o_mine, o_late)
        o_sent.append(direct(1, s, o_mine, o2_in))
    own = own_tokens[...].astype(f32)
    own_scale = lax.rsqrt(jnp.mean(own * own, axis=-1, keepdims=True) + epsilon)
    own_unit = own * own_scale

    for s in range(2):
        a_rings[s].middle(join_terms(s, a_lanes, a_carry, a_early))
    for d in (1, 3, 2):
        moved[d].wait_recv()
    gain_part[some(z, 4)] += gain_z[0] + gain_z[1] + gain_z[2]
    moved = pass_on(1, lambda k: gain_part.at[4 * z + k], gain_x, "x", x)

    d_one = total_of(2, partial.at[c], crossed, sent)
    scaled = d_one * gain_rows[0:1, :]
    input_grad[y] = (
        d_mid[...] + own_scale * (scaled - own_unit * jnp.mean(scaled * own_unit, axis=-1, keepdims=True))
    ).astype(bf16)
    in_shared = share(2, lambda k: input_grad.at[k])
    a_sent = []
    for s in range(2):
        sum_terms(a_rings[s], s, a_lanes, a_mine, a_late)
        a_sent.append(direct(0, s, a_mine, a2_in))

    for s, me in ((0, x), (1, z)):
        m2_rings[s].finish()
        for held, lanes in ((held_e, e_lanes[s]), (held_l[s], l_lanes[s])):
            m2_mine[:, lanes] = (
                m_mine[s][me, :, held].astype(f32)
                + m2_late[s][0, :, held].astype(f32) + m2_late[s][1, :, held].astype(f32)
            ).astype(bf16)
    mine_rows, theirs_rows = some(c, shard), some(1 - c, shard)
    m_last = begin(remote(m2_mine.at[theirs_rows], swapped_m.at[c], outsem.at[0, 0], outsem.at[0, 1], "core", 1 - c))
    swapped_m[c] = m2_mine[mine_rows, :]
    for d in (1, 3, 2):
        moved[d].wait_recv()
    gain_y[3] = gain_part[4 * z + x] + gain_x[0] + gain_x[1] + gain_x[2]
    moved = pass_on(2, lambda k: gain_y.at[3], gain_y, "tensor", y)
    in_shared.forward()
    for d in (1, 3, 2):
        moved[d].wait_recv()
    gain_c[0] = (gain_y[0] + gain_y[1]) + (gain_y[2] + gain_y[3])
    between = begin(remote(gain_c.at[0], gain_c.at[1], gsem.at[3, 0, 0], gsem.at[3, 1, 0], "core", 1 - c))
    for s in range(2):
        direct_sum(o_sent[s], s, o_mine, o2_in, o_lanes)
    for s in range(2):
        direct_sum(a_sent[s], s, a_mine, a2_in, a_lanes)
    a_last = begin(remote(a2_mine.at[theirs_rows], swapped_a.at[c], outsem.at[1, 0], outsem.at[1, 1], "core", 1 - c))
    swapped_a[c] = a2_mine[mine_rows, :]
    between.wait_recv()
    gain_out[...] = gain_c[0] + gain_c[1]
    a_last.wait_recv()
    m_last.wait_recv()
    out_shared.finish()
    in_shared.finish()
    for copy in waits:
        copy.wait_send()


def backward_pass(
    d_part, mix_part, middle, tokens, cot, gain_rows, weights, low, normed, packed, attended, lse, start, table, mlp_terms, *early
):
    chip, width = normed.shape
    seq = start.shape[1]
    quarter, shard = chip // 8, width // 32
    columns, hidden = weights.shape[3], mlp_terms.shape[3] // 3
    first_cut = early[0].shape[2]
    m_split = first_cut + (3 * hidden - 2 * first_cut) // 16 * 9 // 128 * 128
    m_parts = (m_split, 3 * hidden - m_split)
    sds = jax.ShapeDtypeStruct
    dma = pltpu.SemaphoreType.DMA
    vmem = pltpu.VMEM

    def step_buffers(n):
        return (
            vmem((2, 4, width // 16, n), bf16),
            vmem((2, 2, 4, width // 16, n), bf16),
            vmem((2, 4, width // 16, n), bf16),
            vmem((2, 4, width // 16, n), bf16),
            vmem((2, 3, width // 16, n), bf16),
        )

    return pl.pallas_call(
        backward_kernel,
        out_shape=(
            sds((4, quarter, width), bf16),
            sds((4, quarter, width), bf16),
            sds((2, shard, 3 * hidden), bf16),
            sds((2, shard, columns), bf16),
            sds((8, 128), f32),
            *(sds((2, 4, width // 16, n), bf16) for n in m_parts),
        ),
        in_specs=[HBM] * 11 + [VMEM] * 2 + [HBM] * 6,
        out_specs=(VMEM,) * 5 + (HBM,) * 2,
        scratch_shapes=[
            *(vmem(a.shape[1:], a.dtype) for a in (d_part, mix_part)),
            vmem(middle.shape, middle.dtype),
            vmem((quarter, width), bf16),
            vmem((quarter, width), bf16),
            *(vmem(a.shape, a.dtype) for a in (gain_rows, weights, low, normed, packed, attended, table)),
            *[vmem((seq, HEAD_DIM), bf16)] * 3,
            vmem((2, 4, quarter, width), bf16),
            vmem((quarter, width), f32),
            vmem((2, 4, quarter, width), bf16),
            vmem((2, 3, quarter, width), bf16),
            vmem((2, 3, quarter, width), bf16),
            vmem((4, chip, HEAD_DIM), bf16),
            vmem((4, chip, HEAD_DIM), bf16),
            vmem((HEAD_DIM, seq), bf16),
            vmem((seq, HEAD_DIM), f32),
            vmem((seq, HEAD_DIM), f32),
            vmem((4, chip * 3 // 2, 128), bf16),
            vmem((4, chip * 3 // 2, 128), bf16),
            vmem((width, chip), bf16),
            vmem((4, 4, width // 16, columns), bf16),
            *(vmem((4, width // 16, n), bf16) for _ in range(3) for n in m_parts),
            *(vmem((width // 16, n), bf16) for n in m_parts),
            *(vmem((2, width // 16, n), bf16) for n in m_parts),
            *(vmem((width // 16, n), bf16) for n in m_parts),
            vmem((width // 16, 3 * hidden), bf16),
            *(a for n in (3 * columns // 8, columns // 8) for a in step_buffers(n)),
            vmem((width // 16, columns), bf16),
            vmem((2, chip // 2, 3 * columns // 4), bf16),
            vmem((16, 8, 128), f32),
            vmem((4, 8, 128), f32),
            vmem((2, 8, 128), f32),
            vmem((3, 8, 128), f32),
            vmem((3, 4, 8, 128), f32),
            dma((3, 2, 4)), dma((3, 2, 3)), dma((3, 2, 4)), dma((2, 4)), dma((2, 3)), dma((2, 4)),
            dma((10, 2, 6)), dma((2, 15)), dma((4, 2, 3)), dma((2, 2)), dma((12,)), dma((2, 2, 2, 3)),
        ],
        compiler_params=pltpu.CompilerParams(
            collective_id=1, has_side_effects=True, vmem_limit_bytes=62 << 20
        ),
    )(
        d_part, mix_part, middle, tokens, cot, gain_rows, weights, low, normed, packed, attended, lse, start, table, mlp_terms, *early
    )


def finish_kernel(
    out_hbm, grad_hbm, mlp_hbm, attn_hbm, gain_hbm,
    layer_out, input_grad, gain_one, gain_two, grad_q, grad_k, grad_v, grad_o, grad_gate, grad_up, grad_down,
    out_in, grad_in, mlp_in, attn_in, gain_in, sem,
):
    c = lax.axis_index("core")
    sources = (gain_hbm, attn_hbm, mlp_hbm, out_hbm, grad_hbm)
    copies = [
        pltpu.make_async_copy(src, dst, sem.at[k])
        for k, (src, dst) in enumerate(zip(sources, (gain_in, attn_in, mlp_in, out_in, grad_in)))
    ]
    for copy in copies:
        copy.start()
    for copy in copies:
        copy.wait()
    shard, wide = grad_q.shape[0], grad_q.shape[1] // 2
    layer_out[...] = out_in[...].reshape(layer_out.shape)
    input_grad[...] = grad_in[...].reshape(input_grad.shape)
    for k, out in enumerate((gain_one, gain_two)):
        out[...] = jnp.where(c == 0, gain_in[k : k + 1, 0:shard], gain_in[k : k + 1, shard : 2 * shard])
    span = grad_gate.shape[1] // 4
    for e in range(2):
        for k, out in enumerate((grad_q, grad_k, grad_v, grad_o)):
            out[:, e * wide : (e + 1) * wide] = attn_in[e, :, k * wide : (k + 1) * wide].astype(f32)
        for g in range(2):
            lanes = slice((2 * e + g) * span, (2 * e + g + 1) * span)
            for k, out in enumerate((grad_gate, grad_up, grad_down)):
                out[:, lanes] = mlp_in[e, :, (3 * g + k) * span : (3 * g + k + 1) * span].astype(f32)


def finish(layer_out, input_grad, mlp_grads, attn_grads, gains):
    quarters, quarter, width = layer_out.shape
    rows = quarters * quarter
    _, shard, columns = attn_grads.shape
    hidden = mlp_grads.shape[2] // 3
    sds = jax.ShapeDtypeStruct
    narrow, broad = sds((shard, columns // 2), f32), sds((shard, 2 * hidden), f32)
    return pl.pallas_call(
        finish_kernel,
        out_shape=(
            *[sds((rows, width), bf16)] * 2,
            *[sds((1, shard), f32)] * 2,
            *[narrow] * 4,
            *[broad] * 3,
        ),
        in_specs=[HBM] * 5,
        scratch_shapes=[
            *(pltpu.VMEM(a.shape, a.dtype) for a in (layer_out, input_grad, mlp_grads, attn_grads, gains)),
            pltpu.SemaphoreType.DMA((5,)),
        ],
        compiler_params=pltpu.CompilerParams(vmem_limit_bytes=60 << 20),
    )(layer_out, input_grad, mlp_grads, attn_grads, gains)


def frequencies():
    half = HEAD_DIM // 2
    one = rope_base ** (-(np.arange(half) * 2.0) / HEAD_DIM)
    return np.tile(one, 4)[None].astype(np.float32)


def body(
    tokens_in,
    cotangent,
    segments,
    positions,
    norm1_gain,
    q_weight,
    k_weight,
    v_weight,
    o_weight,
    norm2_gain,
    gate_weight,
    up_weight,
    down_weight,
):
    rows, width = tokens_in.shape
    quarter = rows // 4
    (
        full, table, normed_one, packed, low, attended, middle, mixed, d_normed, terms, *early, gain_rows, start, lse,
    ) = forward_pass(
        q_weight, k_weight, v_weight, o_weight.T, gate_weight, up_weight, down_weight.T,
        norm1_gain[None], norm2_gain[None], tokens_in, cotangent, positions[None], frequencies(), segments,
    )
    split = (2, 4, quarter, width)
    *results, _, _ = backward_pass(
        d_normed.reshape(split), mixed.reshape(split), middle, tokens_in, cotangent, gain_rows, full,
        low, normed_one, packed, attended, lse, start, table, terms, *early,
    )
    (
        layer_out, input_grad, gain_one, gain_two, grad_q, grad_k, grad_v, grad_o, grad_gate, grad_up, grad_down,
    ) = finish(*results)
    return (
        layer_out, input_grad, gain_one[0], grad_q, grad_k, grad_v, grad_o.T, gain_two[0], grad_gate, grad_up, grad_down.T,
    )


def solution(mesh):
    apart = Mesh(mesh.devices.reshape(4, 4, 2, 4), ("shard", "x", "core", "tensor"))
    tokens = ("shard", "x", "core")
    placed = (
        P(tokens, None),
        P(tokens, None),
        P("shard", None),
        P(tokens),
        P(tokens),
        P(tokens, "tensor"),
        P(tokens, "tensor"),
        P(tokens, "tensor"),
        P("tensor", tokens),
        P(tokens),
        P(tokens, "tensor"),
        P(tokens, "tensor"),
        P("tensor", tokens),
    )
    return jax.shard_map(
        body,
        mesh=apart,
        in_specs=placed,
        out_specs=(
            P(tokens, None),
            P(tokens, None),
            P(tokens),
            P(tokens, "tensor"),
            P(tokens, "tensor"),
            P(tokens, "tensor"),
            P("tensor", tokens),
            P(tokens),
            P(tokens, "tensor"),
            P(tokens, "tensor"),
            P("tensor", tokens),
        ),
        check_vma=False,
    )
```
